32 devices in a mesh: section: 2 (over y), dp: 16 (over z, x, core).
Axes of the slice: x: 2, y: 2, z: 4, core: 2. Of those that a mesh axis runs over, the one named last changes fastest.
Arguments:
- tokens: bfloat16 [49152, 512], P('dp'), may hold values from -6 to 6
- cotangent: bfloat16 [49152, 512], P('dp'), may hold values from -6 to 6
- span_counts: int32 [32, 3], P('dp'), may hold values from 1 to 6, 12 in all within a row
- tail_lens: int32 [32, 3], P('dp'), may hold values from 1 to 128
- ln1_gain: float32 [2, 512], P('section'), may hold values from 0.1 to 1.9
- w_qkv: bfloat16 [2, 512, 1536], P('section'), may hold values from -0.25 to 0.25
- w_out: bfloat16 [2, 512, 512], P('section'), may hold values from -2 to 2
- ln2_gain: float32 [2, 512], P('section'), may hold values from 0.1 to 1.9
- w_up: bfloat16 [2, 512, 2048], P('section'), may hold values from -0.25 to 0.25
- w_down: bfloat16 [2, 2048, 512], P('section'), may hold values from -0.125 to 0.125
Outputs:
- activations: bfloat16 [2, 49152, 512], P('section', 'dp')
- input_grads: bfloat16 [2, 49152, 512], P('section', 'dp')
- grad_ln1: float32 [2, 512], P('section')
- grad_qkv: float32 [2, 512, 1536], P('section')
- grad_out: float32 [2, 512, 512], P('section')
- grad_ln2: float32 [2, 512], P('section')
- grad_up: float32 [2, 512, 2048], P('section')
- grad_down: float32 [2, 2048, 512], P('section')
The draws below stay inside these ranges and needn't reach their ends.
Inputs may be any that keep to these rules, and one draw needn't show every extreme that they name: `span_counts`: in every row the 3 counts sum to 12 and the largest is exactly 6.
All inputs are finite; a program needn't handle non-finite values.
Results may differ from the reference program's by a relative error of at most 0.02.
Values may be sent and summed in bfloat16 or wider, within the bound.
No kernel may reach another device: no remote copies, remote signals or barrier semaphores. Data moves between devices by JAX's collectives and lax.ppermute only.
A program may use at most 320 MiB of HBM per device.

```python
import math
import jax
import jax.numpy as jnp
import numpy as np
from jax import lax

D = 512
HEADS = 8
HEAD_DIM = 64
FF = 2048
SPAN = 128
MB_BLK = 12
SEQ_MB = 3
MB_TOK = 1536
TOKENS = 49152
GROUPS = 32
N_SECTION = 2


def set_ends(drawn, own_key, least, high):
    dims = drawn.shape
    place = [jax.random.randint(jax.random.fold_in(own_key, axis), (), 0, dims[axis]) for axis in range(len(dims))]
    drawn = drawn.at[tuple(place)].set(least)
    longest = dims.index(max(dims))
    place[longest] = (place[longest] + 1) % dims[longest]
    return drawn.at[tuple(place)].set(high)


def spiked(values, stream_key, source, target, shards_of, factor):
    owner, partner = [(jnp.arange(values.shape[dim]) // (values.shape[dim] // shards_of)).reshape([-1 if axis == dim else 1 for axis in range(values.ndim)]) for dim in (source, target)]
    chosen = jax.random.permutation(stream_key, shards_of)[partner]
    strong = (owner == chosen) | (owner == (partner + shards_of // 2) % shards_of)
    return jnp.where(strong, factor * values, values)


def block_scale(stream_key, dims, split, low, high):
    factor_of = 1.0
    for dim, shards_of in split:
        steps = jax.random.uniform(jax.random.fold_in(jax.random.fold_in(stream_key, 6), dim), (shards_of,), jnp.float32, low / len(split), high / len(split))
        factor_of = factor_of * jnp.repeat(jnp.exp(steps), dims[dim] // shards_of).reshape((-1,) + (1,) * (len(dims) - 1 - dim))
    return factor_of


def profile(number_of, total, bound, skew):
    weights = [(1 << 20) // math.isqrt(rank ** skew) + 1 for rank in range(2, number_of + 1)]
    spare, holding = total - bound - (number_of - 1), [1] * (number_of - 1)
    while spare > 0:
        free = [i for i in range(number_of - 1) if holding[i] < bound]
        pool, left = sum([weights[i] for i in free]), spare
        for i in free:
            more = min(bound - holding[i], max(1, left * weights[i] // pool), spare)
            holding[i] = holding[i] + more
            spare = spare - more
    return np.array([bound] + holding)


def uneven(own_key, count, total, bound, skew):
    if count == 2:
        one = jax.random.randint(own_key, (), max(1, total - bound), min(bound, total - 1) + 1)
        return jnp.stack([one, total - one])
    lengths = jnp.asarray(profile(count, total, bound, skew), jnp.int32)
    pairs = (count - 1) // 2
    source_of, taker = lengths[1:1 + 2 * pairs:2], lengths[2:2 + 2 * pairs:2]
    room = jnp.minimum(source_of - 1, bound - taker)
    moved = jax.random.randint(jax.random.fold_in(own_key, 1), (pairs,), 0, 1 << 20) % (room + 1)
    lengths = lengths.at[1:1 + 2 * pairs:2].set(source_of - moved).at[2:2 + 2 * pairs:2].set(taker + moved)
    return lengths[jax.random.permutation(jax.random.fold_in(own_key, 2), count)]


def gaussian(rng, dims, scale, bound, split=(), held_as=jnp.bfloat16):
    drawn = scale * jax.random.normal(rng, dims, jnp.float32)
    if split:
        drawn = drawn * block_scale(rng, dims, split, -0.22, 0.18)
    return jnp.clip(drawn, -bound, bound).astype(held_as)


def gaussian_with(key, extent, deviation, most, shards, heavy, kind=jnp.bfloat16):
    values = deviation * jax.random.normal(key, extent, jnp.float32)
    if shards:
        values = values * block_scale(key, extent, shards, -0.22, 0.18)
    return jnp.clip(spiked(values, jax.random.fold_in(key, 3), *heavy), -most, most).astype(kind)


def setup_inputs(seed: int = 0) -> dict:
    keys = jax.random.split(jax.random.key(seed), 11)
    tokens = gaussian(keys[0], (TOKENS, D), 1.0, 6.0, ((0, 16),))
    cotangent = gaussian_with(keys[1], (TOKENS, D), 1.0, 6.0, ((0, 16),), (0, 1, 16, 2.0))
    span_counts = jax.vmap(lambda own: uneven(own, SEQ_MB, MB_BLK, MB_BLK // 2, 2))(jax.random.split(keys[2], GROUPS)).reshape((GROUPS, SEQ_MB)).astype(jnp.int32)
    tail_lens = set_ends(jax.random.randint(keys[3], (GROUPS, SEQ_MB), 1, SPAN + 1), jax.random.fold_in(keys[3], 1), 1, SPAN).astype(jnp.int32)
    ln1_gain = jnp.clip(1.0 + 0.18 * jax.random.normal(keys[4], (N_SECTION, D), jnp.float32), 0.1, 1.9)
    w_qkv = gaussian(keys[5], (N_SECTION, D, 3 * D), D ** -0.5, 0.25, ((0, 2),))
    w_out = gaussian(keys[6], (N_SECTION, D, D), (max(D // 64, 1)) ** -0.5, 2.0, ((0, 2),))
    ln2_gain = jnp.clip(1.0 + 0.18 * jax.random.normal(keys[7], (N_SECTION, D), jnp.float32), 0.1, 1.9)
    w_up = gaussian(keys[8], (N_SECTION, D, FF), D ** -0.5, 0.25, ((0, 2),))
    w_down = gaussian(keys[9], (N_SECTION, FF, D), FF ** -0.5, 0.125, ((0, 2),))
    return {"tokens": tokens, "cotangent": cotangent, "span_counts": span_counts, "tail_lens": tail_lens, "ln1_gain": ln1_gain, "w_qkv": w_qkv, "w_out": w_out, "ln2_gain": ln2_gain, "w_up": w_up, "w_down": w_down}


HIGHEST = lax.Precision.HIGHEST
NEG_FILL = -1e+30
EPSILON = 1e-05

@jax.custom_vjp
def low(v):
    return lax.optimization_barrier(v.astype(jnp.bfloat16)).astype(jnp.float32)

@jax.custom_vjp
def low_back(v):
    return v

def low_keep(v):
    return (low(v), None)

def low_pass(kept, grad):
    return (grad,)

def back_keep(v):
    return (v, None)

def back_low(kept, grad):
    return (low(grad),)
low.defvjp(low_keep, low_pass)
low_back.defvjp(back_keep, back_low)

def norm_scale(values, gain):
    center = values - lax.optimization_barrier(jnp.mean(values, axis=-1, keepdims=True))
    spread = lax.optimization_barrier(jnp.mean(center * center, axis=-1, keepdims=True))
    return center * lax.rsqrt(spread + EPSILON) * gain

def block_tables(counts, tail_sizes, block_count, span_len):
    seq_ends = jnp.cumsum(counts).astype(jnp.int32)
    blocks = jnp.arange(block_count, dtype=jnp.int32)
    seq_of = lax.optimization_barrier(jnp.sum((blocks[:, None] >= seq_ends[None, :]).astype(jnp.int32), axis=1))
    members = seq_of[:, None] == jnp.arange(counts.shape[0], dtype=jnp.int32)[None, :]
    end_of = lax.optimization_barrier(jnp.sum(jnp.where(members, seq_ends[None, :], 0), axis=1))
    tail_of = lax.optimization_barrier(jnp.sum(jnp.where(members, tail_sizes[None, :], 0), axis=1))
    filled = jnp.where(blocks == end_of - 1, tail_of, span_len).astype(jnp.int32)
    offsets = jnp.arange(span_len, dtype=jnp.int32)
    live_mask = offsets[None, :] < filled[:, None]
    earlier = (blocks[None, :] < blocks[:, None]) & (seq_of[None, :] == seq_of[:, None])
    return (live_mask, filled, earlier)

def group_layer(inputs, counts, tail_sizes, params):
    gain_one, weight_qkv, weight_out, gain_two, weight_up, weight_down = params
    live_mask, filled, earlier = block_tables(counts, tail_sizes, MB_BLK, SPAN)
    float_type = inputs.dtype
    live_float = live_mask.astype(float_type)
    fill_float = filled.astype(float_type)
    normed = low(norm_scale(inputs, gain_one))
    qkv_all = low(low_back(jnp.dot(normed, weight_qkv, precision=HIGHEST)))
    parts = qkv_all.reshape(MB_BLK, SPAN, 3, HEADS, HEAD_DIM)
    queries, key_rows, value_rows = (parts[:, :, 0], parts[:, :, 1], parts[:, :, 2])
    key_sums = low(low_back(jnp.einsum('bshe,bs->bhe', key_rows, live_float, precision=HIGHEST) / fill_float[:, None, None]))
    value_sums = low(low_back(jnp.einsum('bshe,bs->bhe', value_rows, live_float, precision=HIGHEST) / fill_float[:, None, None]))
    scale_factor = HEAD_DIM ** (-0.5)
    offsets = jnp.arange(SPAN, dtype=jnp.int32)
    causal = offsets[:, None] >= offsets[None, :]
    local_ok = causal[None, None] & live_mask[:, None, None, :]
    summary_ok = earlier[:, None, None, :]
    local_raw = low_back(scale_factor * jnp.einsum('bihe,bjhe->bhij', queries, key_rows, precision=HIGHEST))
    summary_raw = low_back(scale_factor * jnp.einsum('bihe,che->bhic', queries, key_sums, precision=HIGHEST))
    local_scores = jnp.where(local_ok, local_raw, NEG_FILL)
    summary_scores = jnp.where(summary_ok, summary_raw, NEG_FILL)
    row_top = jnp.maximum(lax.optimization_barrier(jnp.max(local_scores, axis=-1)), lax.optimization_barrier(jnp.max(summary_scores, axis=-1)))[..., None]
    local_exp = jnp.exp(local_scores - row_top)
    summary_exp = jnp.exp(summary_scores - row_top)
    totals = lax.optimization_barrier(jnp.sum(local_exp, axis=-1, keepdims=True)) + lax.optimization_barrier(jnp.sum(summary_exp, axis=-1, keepdims=True))
    local_prob = low(local_exp / totals)
    summary_prob = low(summary_exp / totals)
    mixed = jnp.einsum('bhij,bjhe->bihe', local_prob, value_rows, precision=HIGHEST)
    mixed = mixed + jnp.einsum('bhic,che->bihe', summary_prob, value_sums, precision=HIGHEST)
    attended = low(low_back(mixed.reshape(MB_TOK, D)))
    hidden = inputs + low_back(jnp.dot(attended, weight_out, precision=HIGHEST))
    second = low(norm_scale(hidden, gain_two))
    upward = low_back(jnp.dot(second, weight_up, precision=HIGHEST))
    activated = low(jax.nn.gelu(upward, approximate=False))
    return hidden + low_back(jnp.dot(activated, weight_down, precision=HIGHEST))

def run_layer(inputs_all, counts_all, tails_all, params):
    checked = jax.checkpoint(group_layer)

    def one_group(packed):
        return checked(packed[0], packed[1], packed[2], params)
    return lax.map(one_group, (inputs_all, counts_all, tails_all))

def live_of(counts, tail_sizes):
    return block_tables(counts, tail_sizes, MB_BLK, SPAN)[0]

def reference(tokens, cotangent, span_counts, tail_lens, ln1_gain, w_qkv, w_out, ln2_gain, w_up, w_down):
    stacks = (ln1_gain, w_qkv, w_out, ln2_gain, w_up, w_down)
    first_params = tuple((weight_stack[0].astype(jnp.float32) for weight_stack in stacks))
    second_params = tuple((weight_stack[1].astype(jnp.float32) for weight_stack in stacks))
    inputs_all = tokens.astype(jnp.float32).reshape(GROUPS, MB_TOK, D)

    def layer_call(layer_input, *params):
        return run_layer(layer_input, span_counts, tail_lens, params)
    first_out, first_back = jax.vjp(layer_call, inputs_all, *first_params)
    second_in = lax.optimization_barrier(first_out.astype(jnp.bfloat16)).astype(jnp.float32)
    second_out, second_back = jax.vjp(layer_call, second_in, *second_params)
    live_all = jax.vmap(live_of)(span_counts, tail_lens).reshape(GROUPS, MB_TOK, 1).astype(jnp.float32)
    seed_grad = cotangent.astype(jnp.float32).reshape(GROUPS, MB_TOK, D) * live_all
    second_grads = second_back(seed_grad)
    passed = lax.optimization_barrier(second_grads[0].astype(jnp.bfloat16)).astype(jnp.float32)
    first_grads = first_back(passed)
    activations = jnp.stack([first_out, second_out]).reshape(2, TOKENS, D).astype(jnp.bfloat16)
    input_grads = jnp.stack([first_grads[0], second_grads[0]]).reshape(2, TOKENS, D).astype(jnp.bfloat16)
    return (activations, input_grads, jnp.stack([first_grads[1], second_grads[1]]), jnp.stack([first_grads[2], second_grads[2]]), jnp.stack([first_grads[3], second_grads[3]]), jnp.stack([first_grads[4], second_grads[4]]), jnp.stack([first_grads[5], second_grads[5]]), jnp.stack([first_grads[6], second_grads[6]]))
```

```python
import functools

import jax
import jax.numpy as jnp
from jax import lax
from jax.experimental import pallas as pl
from jax.experimental.pallas import tpu as pltpu
from jax.sharding import PartitionSpec as P

D = 512
HEADS = 8
HEAD_DIM = 64
FF = 2048
SPAN = 128
MB_BLK = 12
MB_TOK = MB_BLK * SPAN
PAD_BLK = 16
SUMS = HEADS * PAD_BLK
EPSILON = 1e-05
NEG_FILL = -1e30
BF = jnp.bfloat16
F32 = jnp.float32
VMEM_LIMIT = 58 * 2**20

TILE = 512
TILE_BLK = TILE // SPAN
N_TILE = MB_TOK // TILE
FF_STEP = 512


def dot(left, right, left_dim, right_dim):
    return lax.dot_general(
        left, right, (((left_dim,), (right_dim,)), ((), ())), preferred_element_type=F32
    )


def block_facts(meta_ref, block):
    end_one = meta_ref[0]
    end_two = end_one + meta_ref[1]
    in_one = block < end_one
    in_two = block < end_two
    first = jnp.where(in_one, 0, jnp.where(in_two, end_one, end_two))
    last = jnp.where(in_one, end_one, jnp.where(in_two, end_two, MB_BLK)) - 1
    tail = jnp.where(in_one, meta_ref[3], jnp.where(in_two, meta_ref[4], meta_ref[5]))
    filled = jnp.where(block == last, tail, SPAN)
    return filled, first


def filled_column(meta_ref, width):
    rows = lax.broadcasted_iota(jnp.int32, (PAD_BLK, width), 0)
    out = jnp.full((PAD_BLK, width), SPAN, jnp.int32)
    for block in range(MB_BLK):
        filled, _ = block_facts(meta_ref, block)
        out = jnp.where(rows == block, filled, out)
    return out.astype(F32)


def member_mask(meta_ref, tile_start):
    parts = []
    rows = lax.broadcasted_iota(jnp.int32, (PAD_BLK, SPAN), 0)
    cols = lax.broadcasted_iota(jnp.int32, (PAD_BLK, SPAN), 1)
    for j in range(TILE_BLK):
        block = tile_start + j
        filled, _ = block_facts(meta_ref, block)
        parts.append(jnp.where((rows == block) & (cols < filled), 1.0, 0.0).astype(BF))
    return jnp.concatenate(parts, axis=1)


def head_mask():
    rows = lax.broadcasted_iota(jnp.int32, (SUMS, D), 0) // PAD_BLK
    cols = lax.broadcasted_iota(jnp.int32, (SUMS, D), 1) // HEAD_DIM
    return rows == cols


def spread_heads(sums):
    return jnp.where(head_mask(), jnp.concatenate([sums] * HEADS, axis=0), jnp.zeros((), sums.dtype))


def pair_diag(rows_two):
    zero = jnp.zeros((HEAD_DIM, SPAN), rows_two.dtype)
    top = jnp.concatenate([rows_two[:HEAD_DIM], zero], axis=1)
    low = jnp.concatenate([zero, rows_two[HEAD_DIM:]], axis=1)
    return jnp.concatenate([top, low], axis=0)


def diag_rows(square):
    return jnp.concatenate([square[:HEAD_DIM, :SPAN], square[HEAD_DIM:, SPAN:]], axis=0)


def gain_column(gain_ref):
    return jnp.broadcast_to(gain_ref[...], (SPAN, D)).T


def times_gain(values, gain):
    return jnp.concatenate(
        [values[:, i * SPAN:(i + 1) * SPAN] * gain for i in range(values.shape[1] // SPAN)], axis=1
    )


def normalize(values):
    mean = jnp.sum(values, axis=0, keepdims=True) * (1.0 / D)
    center = values - mean
    spread = jnp.sum(center * center, axis=0, keepdims=True) * (1.0 / D)
    factor = lax.rsqrt(spread + EPSILON)
    return center * factor, factor


def local_mask(filled):
    keys = lax.broadcasted_iota(jnp.int32, (SPAN, 2 * SPAN), 0)
    rows = lax.broadcasted_iota(jnp.int32, (SPAN, 2 * SPAN), 1) % SPAN
    return (keys <= rows) & (keys < filled)


def summary_mask(block, first):
    cols = lax.broadcasted_iota(jnp.int32, (PAD_BLK, 2 * SPAN), 0)
    return (cols >= first) & (cols < block)


def pair_of(array, hp, cols):
    rows = slice(hp * 2 * PAD_BLK, hp * 2 * PAD_BLK + 2 * PAD_BLK)
    part = array[rows, cols]
    return jnp.concatenate([part[:PAD_BLK], part[PAD_BLK:]], axis=1)


def unpair(value):
    return jnp.concatenate([value[:, :SPAN], value[:, SPAN:]], axis=0)


def forward_kernel(
    meta_ref, x_ref, g1_ref, wqkv_ref, wout_ref, g2_ref, wup_ref, wdown_ref,
    out_ref, xh1_ref, r1_ref, qkv_ref, krow_ref, vrow_ref, lse_ref, att_ref, xh2_ref, r2_ref,
    act_ref, gp_ref, ks_ref, vs_ref,
    psum_ref, attf_ref,
):
    step = pl.program_id(0)
    tile_start = step * TILE_BLK
    x_t = x_ref[...].T.astype(F32)
    xhat, r1 = normalize(x_t)
    xh1_ref[...] = xhat.astype(BF)
    r1_ref[...] = r1
    normed = times_gain(xhat, gain_column(g1_ref)).astype(BF)
    q_t = (dot(wqkv_ref[:, :D], normed, 0, 0) * HEAD_DIM ** (-0.5)).astype(BF)
    k_t = dot(wqkv_ref[:, D:2 * D], normed, 0, 0).astype(BF)
    v_t = dot(wqkv_ref[:, 2 * D:], normed, 0, 0).astype(BF)
    qkv_ref[:D] = q_t
    qkv_ref[D:2 * D] = k_t
    qkv_ref[2 * D:] = v_t
    krow = k_t.T
    vrow = v_t.T
    krow_ref[...] = krow
    vrow_ref[...] = vrow
    members = member_mask(meta_ref, tile_start)
    fill = filled_column(meta_ref, D)
    block_rows = lax.broadcasted_iota(jnp.int32, (PAD_BLK, D), 0)
    fresh = (block_rows >= tile_start) & (block_rows < tile_start + TILE_BLK)

    @pl.when(step == 0)
    def _():
        ks_ref[...] = jnp.zeros_like(ks_ref)
        vs_ref[...] = jnp.zeros_like(vs_ref)

    key_sums = jnp.where(fresh, (dot(members, krow, 1, 0) / fill).astype(BF), ks_ref[...])
    value_sums = jnp.where(fresh, (dot(members, vrow, 1, 0) / fill).astype(BF), vs_ref[...])
    ks_ref[...] = key_sums
    vs_ref[...] = value_sums
    s_sum = dot(spread_heads(key_sums), q_t, 1, 0)
    for j in range(TILE_BLK):
        cols = slice(j * SPAN, (j + 1) * SPAN)
        block = tile_start + j
        filled, first = block_facts(meta_ref, block)
        ok = local_mask(filled)
        ok_sum = summary_mask(block, first)
        for hp in range(HEADS // 2):
            feats = slice(hp * SPAN, (hp + 1) * SPAN)
            scores = dot(krow[cols, feats], pair_diag(q_t[feats, cols]), 1, 0)
            scores = jnp.where(ok, scores, NEG_FILL)
            sums = jnp.where(ok_sum, pair_of(s_sum, hp, cols), NEG_FILL)
            top = jnp.maximum(
                jnp.max(scores, axis=0, keepdims=True), jnp.max(sums, axis=0, keepdims=True)
            )
            probs = jnp.exp(scores - top)
            probs_sum = jnp.exp(sums - top)
            total = jnp.sum(probs, axis=0, keepdims=True) + jnp.sum(probs_sum, axis=0, keepdims=True)
            inverse = 1.0 / total
            logs = top + jnp.log(total)
            lse_ref[2 * hp:2 * hp + 1, cols] = logs[:, :SPAN]
            lse_ref[2 * hp + 1:2 * hp + 2, cols] = logs[:, SPAN:]
            probs = (probs * inverse).astype(BF)
            psum_ref[hp * 2 * PAD_BLK:(hp + 1) * 2 * PAD_BLK, cols] = unpair(
                (probs_sum * inverse).astype(BF)
            )
            attf_ref[feats, cols] = diag_rows(dot(v_t[feats, cols], probs, 1, 0))
    att = (attf_ref[...] + dot(spread_heads(value_sums), psum_ref[...], 0, 0)).astype(BF)
    att_ref[...] = att
    hidden = x_t + dot(wout_ref[...], att, 0, 0)
    xhat2, r2 = normalize(hidden)
    xh2_ref[...] = xhat2.astype(BF)
    r2_ref[...] = r2
    second = times_gain(xhat2, gain_column(g2_ref)).astype(BF)
    total_out = hidden
    for f in range(FF // FF_STEP):
        part = slice(f * FF_STEP, (f + 1) * FF_STEP)
        up = dot(wup_ref[:, part], second, 0, 0)
        bell = jnp.exp(up * up * -0.5)
        phi = 0.5 + 0.5 * lax.erf(up * (0.5 ** 0.5))
        act = (up * phi).astype(BF)
        act_ref[part] = act
        gp_ref[part] = (phi + up * bell * 0.3989422804014327).astype(BF)
        total_out = total_out + dot(wdown_ref[part], act, 0, 0)
    out_ref[...] = total_out.astype(BF).T


def spec(shape, index):
    return pl.BlockSpec(shape, index)


def whole(shape):
    return pl.BlockSpec(shape, lambda t, *_: (0,) * len(shape), pipeline_mode=pl.Buffered(1))


def rows_spec(width):
    return pl.BlockSpec((TILE, width), lambda t, *_: (t, 0))


def cols_spec(height):
    return pl.BlockSpec((height, TILE), lambda t, *_: (0, t))


def layer_forward(meta, x, params, x_offset_tiles=False):
    g1, wqkv, wout, g2, wup, wdown = params
    sds = jax.ShapeDtypeStruct
    if x_offset_tiles:
        x_spec = pl.BlockSpec((TILE, D), lambda t, m: (m[6] * N_TILE + t, 0))
    else:
        x_spec = rows_spec(D)
    return pl.pallas_call(
        forward_kernel,
        out_shape=(
            sds((MB_TOK, D), BF), sds((D, MB_TOK), BF), sds((1, MB_TOK), F32),
            sds((3 * D, MB_TOK), BF), sds((MB_TOK, D), BF), sds((MB_TOK, D), BF),
            sds((HEADS, MB_TOK), F32), sds((D, MB_TOK), BF), sds((D, MB_TOK), BF),
            sds((1, MB_TOK), F32), sds((FF, MB_TOK), BF), sds((FF, MB_TOK), BF),
            sds((PAD_BLK, D), BF), sds((PAD_BLK, D), BF),
        ),
        grid_spec=pltpu.PrefetchScalarGridSpec(
            num_scalar_prefetch=1,
            grid=(N_TILE,),
            in_specs=[
                x_spec, whole((1, D)), whole((D, 3 * D)), whole((D, D)), whole((1, D)),
                whole((D, FF)), whole((FF, D)),
            ],
            out_specs=[
                rows_spec(D), cols_spec(D), cols_spec(1), cols_spec(3 * D), rows_spec(D),
                rows_spec(D), cols_spec(HEADS), cols_spec(D), cols_spec(D), cols_spec(1),
                cols_spec(FF), cols_spec(FF), whole((PAD_BLK, D)), whole((PAD_BLK, D)),
            ],
            scratch_shapes=[pltpu.VMEM((SUMS, TILE), BF), pltpu.VMEM((D, TILE), F32)],
        ),
        compiler_params=pltpu.CompilerParams(vmem_limit_bytes=VMEM_LIMIT),
    )(meta, x, g1, wqkv, wout, g2, wup, wdown)


def mlp_back_kernel(
    meta_ref, seed_ref, act_ref, gp_ref, xh2_ref, r2_ref, att_ref, g2_ref, wup_ref, wdown_ref,
    wout_ref,
    gcat_ref, gln_ref, gh_ref, gatt_ref,
    gdown_acc, gup_acc, gout_acc, gln_acc, *, masked,
):
    step = pl.program_id(0)
    tile = N_TILE - 1 - step

    @pl.when(step == 0)
    def _():
        gdown_acc[...] = jnp.zeros_like(gdown_acc)
        gup_acc[...] = jnp.zeros_like(gup_acc)
        gout_acc[...] = jnp.zeros_like(gout_acc)
        gln_acc[...] = jnp.zeros_like(gln_acc)

    low = seed_ref[...].T
    if masked:
        parts = []
        cols = lax.broadcasted_iota(jnp.int32, (D, SPAN), 1)
        for j in range(TILE_BLK):
            filled, _ = block_facts(meta_ref, tile * TILE_BLK + j)
            part = low[:, j * SPAN:(j + 1) * SPAN]
            parts.append(jnp.where(cols < filled, part, jnp.zeros((), BF)))
        low = jnp.concatenate(parts, axis=1)
    gain = gain_column(g2_ref)
    xhat = xh2_ref[...].astype(F32)
    second = times_gain(xhat, gain).astype(BF)
    e = None
    for f in range(FF // FF_STEP):
        part = slice(f * FF_STEP, (f + 1) * FF_STEP)
        gdown_acc[part] += dot(act_ref[part], low, 1, 1)
        ga = dot(wdown_ref[part], low, 1, 0)
        gui = (ga * gp_ref[part].astype(F32)).astype(BF)
        gup_acc[part] += dot(gui, second, 1, 1)
        term = dot(wup_ref[:, part], gui, 1, 0)
        e = term if e is None else e + term
    prod = e * xhat
    for j in range(TILE_BLK):
        gln_acc[...] += prod[:, j * SPAN:(j + 1) * SPAN]
    f_val = times_gain(e, gain)
    mean_f = jnp.sum(f_val, axis=0, keepdims=True) * (1.0 / D)
    mean_fx = jnp.sum(f_val * xhat, axis=0, keepdims=True) * (1.0 / D)
    gh = low.astype(F32) + r2_ref[...] * (f_val - mean_f - xhat * mean_fx)
    gh_ref[...] = gh
    ghb = gh.astype(BF)
    gout_acc[...] += dot(att_ref[...], ghb, 1, 1)
    gatt_ref[...] = dot(wout_ref[...], ghb, 1, 0).astype(BF)

    @pl.when(step == N_TILE - 1)
    def _():
        gcat_ref[:FF] = gdown_acc[...].astype(BF)
        gcat_ref[FF:2 * FF] = gup_acc[...].astype(BF)
        gcat_ref[2 * FF:] = gout_acc[...].astype(BF)
        gln_ref[...] = jnp.sum(gln_acc[...].T, axis=0, keepdims=True)


def rev_rows(width):
    return pl.BlockSpec((TILE, width), lambda t, *_: (N_TILE - 1 - t, 0))


def rev_cols(height):
    return pl.BlockSpec((height, TILE), lambda t, *_: (0, N_TILE - 1 - t))


def mlp_back(meta, seed, stash, params, masked):
    _, _, wout, g2, wup, wdown = params
    _, _, _, _, _, _, att, xh2, r2, act, gp, _, _ = stash
    sds = jax.ShapeDtypeStruct
    if masked:
        seed_spec = pl.BlockSpec((TILE, D), lambda t, m: (m[6] * N_TILE + N_TILE - 1 - t, 0))
    else:
        seed_spec = rev_rows(D)
    return pl.pallas_call(
        functools.partial(mlp_back_kernel, masked=masked),
        out_shape=(
            sds((2 * FF + D, D), BF), sds((1, D), F32), sds((D, MB_TOK), F32), sds((D, MB_TOK), BF),
        ),
        grid_spec=pltpu.PrefetchScalarGridSpec(
            num_scalar_prefetch=1,
            grid=(N_TILE,),
            in_specs=[
                seed_spec, rev_cols(FF), rev_cols(FF), rev_cols(D), rev_cols(1), rev_cols(D),
                whole((1, D)), whole((D, FF)), whole((FF, D)), whole((D, D)),
            ],
            out_specs=[whole((2 * FF + D, D)), whole((1, D)), rev_cols(D), rev_cols(D)],
            scratch_shapes=[
                pltpu.VMEM((FF, D), F32), pltpu.VMEM((FF, D), F32), pltpu.VMEM((D, D), F32),
                pltpu.VMEM((D, SPAN), F32),
            ],
        ),
        compiler_params=pltpu.CompilerParams(vmem_limit_bytes=VMEM_LIMIT),
    )(meta, seed, act, gp, xh2, r2, att, g2, wup, wdown, wout)


def attn_back_kernel(
    meta_ref, gh_ref, gatt_ref, xh1_ref, r1_ref, qkv_ref, krow_ref, vrow_ref, lse_ref, ks_ref,
    vs_ref, g1_ref, wqkv_ref,
    gin_ref, gqkv_ref, gln_ref,
    gqkv_acc, gln_acc, gks_acc, gvs_acc, rows_ref, psum_ref, dsum_ref,
):
    step = pl.program_id(0)
    tile_start = (N_TILE - 1 - step) * TILE_BLK

    @pl.when(step == 0)
    def _():
        gqkv_acc[...] = jnp.zeros_like(gqkv_acc)
        gln_acc[...] = jnp.zeros_like(gln_acc)
        gks_acc[...] = jnp.zeros_like(gks_acc)
        gvs_acc[...] = jnp.zeros_like(gvs_acc)

    q_t = qkv_ref[:D]
    gatt = gatt_ref[...]
    ks_heads = spread_heads(ks_ref[...])
    vs_heads = spread_heads(vs_ref[...])
    s_sum = dot(ks_heads, q_t, 1, 0)
    dp_sum = dot(vs_heads, gatt, 1, 0)
    for j in range(TILE_BLK):
        cols = slice(j * SPAN, (j + 1) * SPAN)
        block = tile_start + j
        filled, first = block_facts(meta_ref, block)
        ok = local_mask(filled)
        ok_sum = summary_mask(block, first)
        for hp in range(HEADS // 2):
            feats = slice(hp * SPAN, (hp + 1) * SPAN)
            keys = slice(D + hp * SPAN, D + (hp + 1) * SPAN)
            values = slice(2 * D + hp * SPAN, 2 * D + (hp + 1) * SPAN)
            logs = jnp.concatenate(
                [lse_ref[2 * hp:2 * hp + 1, cols], lse_ref[2 * hp + 1:2 * hp + 2, cols]], axis=1
            )
            q_diag = pair_diag(q_t[feats, cols])
            g_diag = pair_diag(gatt[feats, cols])
            scores = jnp.where(ok, dot(krow_ref[cols, feats], q_diag, 1, 0), NEG_FILL)
            probs = jnp.exp(scores - logs)
            dp = dot(vrow_ref[cols, feats], g_diag, 1, 0)
            sums = jnp.where(ok_sum, pair_of(s_sum, hp, cols), NEG_FILL)
            probs_sum = jnp.exp(sums - logs)
            dps = pair_of(dp_sum, hp, cols)
            weighted = probs * dp
            weighted_sum = probs_sum * dps
            delta = jnp.sum(weighted, axis=0, keepdims=True) + jnp.sum(
                weighted_sum, axis=0, keepdims=True
            )
            ds = (probs * (dp - delta)).astype(BF)
            dss = (probs_sum * (dps - delta)).astype(BF)
            sum_rows = slice(hp * 2 * PAD_BLK, (hp + 1) * 2 * PAD_BLK)
            psum_ref[sum_rows, cols] = unpair(probs_sum.astype(BF))
            dsum_ref[sum_rows, cols] = unpair(dss)
            rows_ref[feats, cols] = diag_rows(dot(qkv_ref[keys, cols], ds, 1, 0))
            rows_ref[keys, cols] = dot(q_diag, ds, 1, 1)
            rows_ref[values, cols] = dot(g_diag, probs.astype(BF), 1, 1)
    dsum = dsum_ref[...]
    gks_acc[...] += dot(dsum, q_t, 1, 1)
    gvs_acc[...] += dot(psum_ref[...], gatt, 1, 1)
    heads = head_mask()
    members = member_mask(meta_ref, tile_start)
    fill = filled_column(meta_ref, D)

    def spread_back(acc_ref):
        kept = jnp.where(heads, acc_ref[...], 0.0)
        merged = kept[:PAD_BLK]
        for h in range(1, HEADS):
            merged = merged + kept[h * PAD_BLK:(h + 1) * PAD_BLK]
        back = (merged.astype(BF).astype(F32) / fill).astype(BF)
        return dot(back, members, 0, 0)

    grad_q = (rows_ref[:D] + dot(ks_heads, dsum, 0, 0)) * HEAD_DIM ** (-0.5)
    grad_k = rows_ref[D:2 * D] + spread_back(gks_acc)
    grad_v = rows_ref[2 * D:] + spread_back(gvs_acc)
    gain = gain_column(g1_ref)
    xhat = xh1_ref[...].astype(F32)
    normed = times_gain(xhat, gain).astype(BF)
    e = None
    for i, rows in enumerate((grad_q, grad_k, grad_v)):
        rows = rows.astype(BF)
        part = slice(i * D, (i + 1) * D)
        gqkv_acc[part] += dot(rows, normed, 1, 1)
        term = dot(wqkv_ref[:, part], rows, 1, 0)
        e = term if e is None else e + term
    prod = e * xhat
    for j in range(TILE_BLK):
        gln_acc[...] += prod[:, j * SPAN:(j + 1) * SPAN]
    f_val = times_gain(e, gain)
    mean_f = jnp.sum(f_val, axis=0, keepdims=True) * (1.0 / D)
    mean_fx = jnp.sum(f_val * xhat, axis=0, keepdims=True) * (1.0 / D)
    gin = gh_ref[...] + r1_ref[...] * (f_val - mean_f - xhat * mean_fx)
    gin_ref[...] = gin.astype(BF).T

    @pl.when(step == N_TILE - 1)
    def _():
        gqkv_ref[...] = gqkv_acc[...].astype(BF)
        gln_ref[...] = jnp.sum(gln_acc[...].T, axis=0, keepdims=True)


def attn_back(meta, gh, gatt, stash, params):
    g1, wqkv = params[:2]
    xh1, r1, qkv, krow, vrow, lse, _, _, _, _, _, ks, vs = stash
    sds = jax.ShapeDtypeStruct
    return pl.pallas_call(
        attn_back_kernel,
        out_shape=(sds((MB_TOK, D), BF), sds((3 * D, D), BF), sds((1, D), F32)),
        grid_spec=pltpu.PrefetchScalarGridSpec(
            num_scalar_prefetch=1,
            grid=(N_TILE,),
            in_specs=[
                rev_cols(D), rev_cols(D), rev_cols(D), rev_cols(1), rev_cols(3 * D), rev_rows(D),
                rev_rows(D), rev_cols(HEADS), whole((PAD_BLK, D)), whole((PAD_BLK, D)),
                whole((1, D)), whole((D, 3 * D)),
            ],
            out_specs=[rev_rows(D), whole((3 * D, D)), whole((1, D))],
            scratch_shapes=[
                pltpu.VMEM((3 * D, D), F32), pltpu.VMEM((D, SPAN), F32),
                pltpu.VMEM((SUMS, D), F32), pltpu.VMEM((SUMS, D), F32),
                pltpu.VMEM((3 * D, TILE), F32), pltpu.VMEM((SUMS, TILE), BF),
                pltpu.VMEM((SUMS, TILE), BF),
            ],
        ),
        compiler_params=pltpu.CompilerParams(vmem_limit_bytes=VMEM_LIMIT),
    )(meta, gh, gatt, xh1, r1, qkv, krow, vrow, lse, ks, vs, g1, wqkv)


def axis_bits(axis):
    return lax.axis_size(axis).bit_length() - 1


def swap_bit(value, bit):
    size = lax.axis_size("dp")
    return lax.ppermute(value, "dp", [(i, i ^ (1 << bit)) for i in range(size)])


def reversed_index():
    index = lax.axis_index("dp")
    bits = axis_bits("dp")
    out = jnp.zeros((), jnp.int32)
    for bit in range(bits):
        out = out | (((index >> bit) & 1) << (bits - 1 - bit))
    return out


def scatter_sum(value):
    index = lax.axis_index("dp")
    for bit in range(axis_bits("dp")):
        half = value.shape[0] // 2
        mine = (index >> bit) & 1
        kept = lax.dynamic_slice_in_dim(value, mine * half, half, 0)
        sent = lax.dynamic_slice_in_dim(value, (1 - mine) * half, half, 0)
        value = (kept.astype(F32) + swap_bit(sent, bit).astype(F32)).astype(BF)
    return value


def gather_rows(value):
    index = lax.axis_index("dp")
    for bit in reversed(range(axis_bits("dp"))):
        mine = (index >> bit) & 1
        other = swap_bit(value, bit)
        value = jnp.where(
            mine == 0,
            jnp.concatenate([value, other], axis=0),
            jnp.concatenate([other, value], axis=0),
        )
    return value


def sum_all(value):
    for bit in range(axis_bits("dp")):
        value = value + swap_bit(value, bit)
    return value


def swap_section(value):
    return lax.ppermute(value, "section", [(0, 1), (1, 0)])


def to_section(value, target):
    return lax.ppermute(value, "section", [(1 - target, target)])


def per_device(
    tokens, cotangent, span_counts, tail_lens, ln1_gain, w_qkv, w_out, ln2_gain, w_up, w_down
):
    section = lax.axis_index("section")
    first = section == 0
    size = lax.axis_size("dp")
    meta = jnp.concatenate([
        lax.dynamic_index_in_dim(span_counts, section, 0, keepdims=False),
        lax.dynamic_index_in_dim(tail_lens, section, 0, keepdims=False),
        section.astype(jnp.int32)[None], jnp.zeros((1,), jnp.int32),
    ])
    own = (ln1_gain, w_qkv[0], w_out[0], ln2_gain, w_up[0], w_down[0])
    place = reversed_index()

    def shard_of(weight):
        rows = weight.shape[0] // size
        return lax.dynamic_slice_in_dim(weight, place * rows, rows, 0)

    attn_cat = jnp.concatenate([own[1], own[2]], axis=1)
    other_gains = swap_section(jnp.concatenate([ln1_gain, ln2_gain], axis=0))
    other_attn = gather_rows(swap_section(shard_of(attn_cat)))
    other_up = gather_rows(swap_section(shard_of(own[4])))
    other_down = gather_rows(swap_section(shard_of(own[5])))
    other = (
        other_gains[:1], other_attn[:, :3 * D], other_attn[:, 3 * D:], other_gains[1:],
        other_up, other_down,
    )
    layers = [
        tuple(jnp.where(first, a, b) for a, b in zip(own, other)),
        tuple(jnp.where(first, b, a) for a, b in zip(own, other)),
    ]
    out0 = layer_forward(meta, tokens, layers[0], True)
    act0, stash0 = out0[0], out0[1:]
    act0_in = to_section(act0, 0)
    out1 = layer_forward(meta, act0, layers[1], False)
    act1, stash1 = out1[0], out1[1:]
    act1_in = to_section(act1, 1)
    cat1, ln2_1, gh1, gatt1 = mlp_back(meta, cotangent, stash1, layers[1], True)
    cat1 = scatter_sum(cat1)
    ig1, qkv1, ln1_1 = attn_back(meta, gh1, gatt1, stash1, layers[1])
    ig1_in = to_section(ig1, 1)
    qkv1 = scatter_sum(qkv1)
    cat0, ln2_0, gh0, gatt0 = mlp_back(meta, ig1, stash0, layers[0], False)
    cat0 = scatter_sum(cat0)
    ig0, qkv0, ln1_0 = attn_back(meta, gh0, gatt0, stash0, layers[0])
    ig0_in = to_section(ig0, 0)
    qkv0 = scatter_sum(qkv0)
    lns = sum_all(jnp.concatenate([ln1_0, ln2_0, ln1_1, ln2_1], axis=0))
    lns_in = swap_section(jnp.where(first, lns[2:], lns[:2]))
    lns = jnp.where(first, lns[:2], lns[2:]) + lns_in

    def own_sum(grad0, grad1):
        other_in = swap_section(jnp.where(first, grad1, grad0))
        mine = jnp.where(first, grad0, grad1)
        return gather_rows((mine.astype(F32) + other_in.astype(F32)).astype(BF))

    cat = own_sum(cat0, cat1)
    qkv = own_sum(qkv0, qkv1)
    activations = jnp.concatenate(
        [jnp.where(first, act0, act1_in), jnp.where(first, act0_in, act1)], axis=0
    )
    input_grads = jnp.concatenate(
        [jnp.where(first, ig0, ig1_in), jnp.where(first, ig0_in, ig1)], axis=0
    )
    return (
        activations[None],
        input_grads[None],
        lns[:1],
        qkv.T.astype(F32)[None],
        cat[2 * FF:].astype(F32)[None],
        lns[1:],
        cat[FF:2 * FF].T.astype(F32)[None],
        cat[:FF].astype(F32)[None],
    )


def solution(mesh):
    return jax.shard_map(
        per_device,
        mesh=mesh,
        in_specs=(
            P("dp", None),
            P("dp", None),
            P("dp", None),
            P("dp", None),
            P("section", None),
            P("section", None, None),
            P("section", None, None),
            P("section", None),
            P("section", None, None),
            P("section", None, None),
        ),
        out_specs=(
            P("section", "dp", None),
            P("section", "dp", None),
            P("section", None),
            P("section", None, None),
            P("section", None, None),
            P("section", None),
            P("section", None, None),
            P("section", None, None),
        ),
        check_vma=False,
    )
```

```python
import functools

import jax
import jax.numpy as jnp
from jax import lax
from jax.experimental import pallas as pl
from jax.experimental.pallas import tpu as pltpu
from jax.sharding import PartitionSpec as P

D = 512
HEADS = 8
HEAD_DIM = 64
FF = 2048
SPAN = 128
MB_BLK = 12
MB_TOK = MB_BLK * SPAN
PAD_BLK = 16
EPSILON = 1e-05
NEG_FILL = -1e30
BF = jnp.bfloat16
F32 = jnp.float32
VMEM_LIMIT = 58 * 2**20

TILE = 512
TILE_BLK = TILE // SPAN
N_TILE = MB_TOK // TILE
FF_STEP = 512
FWD_STEP = 512
FWD_GROUP = 2
BACK_GROUP = 2


def dot(left, right, left_dim, right_dim):
    return lax.dot_general(
        left, right, (((left_dim,), (right_dim,)), ((), ())), preferred_element_type=F32
    )


def block_facts(meta_ref, block):
    end_one = meta_ref[0]
    end_two = end_one + meta_ref[1]
    in_one = block < end_one
    in_two = block < end_two
    first = jnp.where(in_one, 0, jnp.where(in_two, end_one, end_two))
    last = jnp.where(in_one, end_one, jnp.where(in_two, end_two, MB_BLK)) - 1
    tail = jnp.where(in_one, meta_ref[3], jnp.where(in_two, meta_ref[4], meta_ref[5]))
    filled = jnp.where(block == last, tail, SPAN)
    return filled, first


def filled_column(meta_ref, width):
    rows = lax.broadcasted_iota(jnp.int32, (PAD_BLK, width), 0)
    out = jnp.full((PAD_BLK, width), SPAN, jnp.int32)
    for block in range(MB_BLK):
        filled, _ = block_facts(meta_ref, block)
        out = jnp.where(rows == block, filled, out)
    return out.astype(F32)


def filled_row(meta_ref):
    cols = lax.broadcasted_iota(jnp.int32, (1, PAD_BLK), 1)
    out = jnp.full((1, PAD_BLK), SPAN, jnp.int32)
    for block in range(MB_BLK):
        filled, _ = block_facts(meta_ref, block)
        out = jnp.where(cols == block, filled, out)
    return out.astype(F32)


def member_mask(meta_ref, tile_start):
    parts = []
    rows = lax.broadcasted_iota(jnp.int32, (PAD_BLK, SPAN), 0)
    cols = lax.broadcasted_iota(jnp.int32, (PAD_BLK, SPAN), 1)
    for j in range(TILE_BLK):
        block = tile_start + j
        filled, _ = block_facts(meta_ref, block)
        parts.append(jnp.where((rows == block) & (cols < filled), 1.0, 0.0).astype(BF))
    return jnp.concatenate(parts, axis=1)


def pair_diag(rows_two):
    zero = jnp.zeros((HEAD_DIM, SPAN), rows_two.dtype)
    top = jnp.concatenate([rows_two[:HEAD_DIM], zero], axis=1)
    low = jnp.concatenate([zero, rows_two[HEAD_DIM:]], axis=1)
    return jnp.concatenate([top, low], axis=0)


def diag_rows(square):
    return jnp.concatenate([square[:HEAD_DIM, :SPAN], square[HEAD_DIM:, SPAN:]], axis=0)


def gain_column(gains_ref, index):
    return jnp.broadcast_to(gains_ref[index:index + 1], (SPAN, D)).T


def times_gain(values, gain):
    return jnp.concatenate(
        [values[:, i * SPAN:(i + 1) * SPAN] * gain for i in range(values.shape[1] // SPAN)], axis=1
    )


def normalize(values):
    mean = jnp.sum(values, axis=0, keepdims=True) * (1.0 / D)
    center = values - mean
    spread = jnp.sum(center * center, axis=0, keepdims=True) * (1.0 / D)
    factor = lax.rsqrt(spread + EPSILON)
    return center * factor, factor


def score_mask(block, filled, first):
    rows = lax.broadcasted_iota(jnp.int32, (SPAN + PAD_BLK, 2 * SPAN), 0)
    cols = lax.broadcasted_iota(jnp.int32, (SPAN + PAD_BLK, 2 * SPAN), 1) % SPAN
    local = (rows <= cols) & (rows < filled)
    earlier = (rows >= SPAN + first) & (rows < SPAN + block)
    return local | earlier


def attention_items(meta_ref, tile_start, blocks):
    items = []
    for j in blocks:
        filled, first = block_facts(meta_ref, tile_start + j)
        mask = score_mask(tile_start + j, filled, first)
        for hp in range(HEADS // 2):
            items.append((slice(j * SPAN, (j + 1) * SPAN), hp, slice(hp * SPAN, (hp + 1) * SPAN), mask))
    return items


def weight_rows(place, index, rows):
    return pl.ds(pl.multiple_of((place ^ index) * rows, rows), rows)


def start_weight(meta_ref, layer, refs, target, sem):
    own, pieces = refs[0], refs[1:]

    @pl.when(meta_ref[6] == layer)
    def _():
        pltpu.make_async_copy(own, target, sem).start()

    @pl.when(meta_ref[6] != layer)
    def _():
        rows = target.shape[0] // 4
        for index, piece in enumerate(pieces):
            pltpu.make_async_copy(
                piece, target.at[weight_rows(meta_ref[7], index, rows)], sem
            ).start()


def wait_weight(refs, target, sem):
    pltpu.make_async_copy(refs[0], target, sem).wait()


def forward_attn_part(meta_ref, x_ref, gains_ref, outs, scratch, wqkv_ref, wout_ref, wait):
    (xh1_ref, r1_ref, qkv_ref, krow_ref, vrow_ref, lse_ref, att_ref, xh2_ref, r2_ref, ks_ref,
     vs_ref) = outs
    (attf_ref,) = scratch
    step = pl.program_id(0)
    tile_start = step * TILE_BLK

    @pl.when(step == 0)
    def _():
        ks_ref[...] = jnp.zeros_like(ks_ref)
        vs_ref[...] = jnp.zeros_like(vs_ref)

    x_t = x_ref[...].T.astype(F32)
    xhat, r1 = normalize(x_t)
    xh1_ref[...] = xhat.astype(BF)
    r1_ref[...] = r1
    normed = times_gain(xhat, gain_column(gains_ref, 0)).astype(BF)
    wait(0)
    q_t = (dot(wqkv_ref[:, :D], normed, 0, 0) * HEAD_DIM ** (-0.5)).astype(BF)
    k_t = dot(wqkv_ref[:, D:2 * D], normed, 0, 0).astype(BF)
    v_t = dot(wqkv_ref[:, 2 * D:], normed, 0, 0).astype(BF)
    qkv_ref[:D] = q_t
    qkv_ref[D:2 * D] = k_t
    qkv_ref[2 * D:] = v_t
    krow = k_t.T
    vrow = v_t.T
    krow_ref[...] = krow
    vrow_ref[...] = vrow
    members = member_mask(meta_ref, tile_start)
    fill = filled_column(meta_ref, D)
    block_rows = lax.broadcasted_iota(jnp.int32, (PAD_BLK, D), 0)
    fresh = (block_rows >= tile_start) & (block_rows < tile_start + TILE_BLK)
    key_sums = jnp.where(fresh, (dot(members, krow, 1, 0) / fill).astype(BF), ks_ref[...])
    value_sums = jnp.where(fresh, (dot(members, vrow, 1, 0) / fill).astype(BF), vs_ref[...])
    ks_ref[...] = key_sums
    vs_ref[...] = value_sums
    vs_t = value_sums.T
    for j in range(0, TILE_BLK, FWD_GROUP):
        items = attention_items(meta_ref, tile_start, range(j, j + FWD_GROUP))
        scores = [
            dot(
                jnp.concatenate([krow[cols, feats], key_sums[:, feats]], axis=0),
                pair_diag(q_t[feats, cols]), 1, 0,
            )
            for cols, _, feats, _ in items
        ]
        probs = []
        for (cols, hp, feats, mask), score in zip(items, scores):
            score = jnp.where(mask, score, NEG_FILL)
            top = jnp.max(score, axis=0, keepdims=True)
            prob = jnp.exp(score - top)
            total = jnp.sum(prob, axis=0, keepdims=True)
            logs = top + jnp.log(total)
            lse_ref[2 * hp:2 * hp + 1, cols] = logs[:, :SPAN]
            lse_ref[2 * hp + 1:2 * hp + 2, cols] = logs[:, SPAN:]
            probs.append((prob * (1.0 / total)).astype(BF))
        for (cols, _, feats, _), prob in zip(items, probs):
            values = jnp.concatenate([v_t[feats, cols], vs_t[feats]], axis=1)
            attf_ref[feats, cols] = diag_rows(dot(values, prob, 1, 0)).astype(BF)
    att = attf_ref[...]
    att_ref[...] = att
    wait(1)
    hidden = x_t + dot(wout_ref[...], att, 0, 0)
    xhat2, r2 = normalize(hidden)
    xh2_ref[...] = xhat2.astype(BF)
    r2_ref[...] = r2
    return hidden, times_gain(xhat2, gain_column(gains_ref, 1)).astype(BF)


def forward_mlp_part(hidden, second, outs, wup_ref, wdown_ref):
    out_ref, act_ref, gp_ref = outs
    total_out = hidden
    up = dot(wup_ref[:, :FWD_STEP], second, 0, 0)
    for f in range(FF // FWD_STEP):
        part = slice(f * FWD_STEP, (f + 1) * FWD_STEP)
        later = slice((f + 1) * FWD_STEP, (f + 2) * FWD_STEP)
        ahead = dot(wup_ref[:, later], second, 0, 0) if later.stop <= FF else None
        bell = jnp.exp(up * up * -0.5)
        phi = 0.5 + 0.5 * lax.erf(up * (0.5 ** 0.5))
        act = (up * phi).astype(BF)
        act_ref[part] = act
        gp_ref[part] = (phi + up * bell * 0.3989422804014327).astype(BF)
        total_out = total_out + dot(wdown_ref[part], act, 0, 0)
        up = ahead
    out_ref[...] = total_out.astype(BF).T


def weight_waits(meta_ref, layer, weights, targets, sems):
    begin = pl.program_id(0) == 0

    @pl.when(begin)
    def _():
        for i, (sources, target) in enumerate(zip(weights, targets)):
            start_weight(meta_ref, layer, sources, target, sems.at[i])

    def wait(i):
        @pl.when(begin)
        def _():
            wait_weight(weights[i], targets[i], sems.at[i])

    return wait


def fives(refs, count):
    return [refs[5 * i:5 * i + 5] for i in range(count)], refs[5 * count:]


def forward_kernel(meta_ref, x_ref, gains_ref, *refs, layer):
    weights, refs = fives(refs, 4)
    attn_outs, mlp_outs, scratch, targets, sems = (
        refs[:11], refs[11:14], refs[14:15], refs[15:19], refs[19]
    )
    wait = weight_waits(meta_ref, layer, weights, targets, sems)
    hidden, second = forward_attn_part(
        meta_ref, x_ref, gains_ref, attn_outs, scratch, targets[0], targets[1], wait
    )
    wait(2)
    wait(3)
    forward_mlp_part(hidden, second, mlp_outs, targets[2], targets[3])


def forward_attn_kernel(meta_ref, x_ref, gains_ref, *refs, layer):
    weights, refs = fives(refs, 2)
    attn_outs, (hid_ref, sec_ref), scratch, targets, sems = (
        refs[:11], refs[11:13], refs[13:14], refs[14:16], refs[16]
    )
    wait = weight_waits(meta_ref, layer, weights, targets, sems)
    hidden, second = forward_attn_part(
        meta_ref, x_ref, gains_ref, attn_outs, scratch, targets[0], targets[1], wait
    )
    hid_ref[...] = hidden
    sec_ref[...] = second


def forward_mlp_kernel(meta_ref, hid_ref, sec_ref, *refs, layer):
    weights, refs = fives(refs, 2)
    outs, targets, sems = refs[:3], refs[3:5], refs[5]
    wait = weight_waits(meta_ref, layer, weights, targets, sems)
    wait(0)
    wait(1)
    forward_mlp_part(hid_ref[...], sec_ref[...], outs, *targets)


def write_halves(meta_ref, accs, shards, send_ref, keep_ref, last=None):
    core = meta_ref[7] & 1
    total = send_ref.shape[0] // 8
    for target, side in ((send_ref, 1 - core), (keep_ref, core)):
        for s in range(8):
            start = s * total
            for acc, shard in zip(accs, shards):
                rows = pl.ds(pl.multiple_of(side * (8 * shard), 8 * shard) + s * shard, shard)
                target[pl.ds(start, shard)] = acc[rows].astype(BF)
                start += shard
            if last is not None:
                target[pl.ds(start, last.shape[0])] = last


MLP_SHARDS = (FF // 16, FF // 16, D // 16)
QKV_SHARDS = (3 * D // 16,)
GAIN_ROWS = 16


def norm_back(grad, gain, xhat, factor, gln_acc):
    prod = grad * xhat
    for j in range(TILE_BLK):
        gln_acc[...] += prod[:, j * SPAN:(j + 1) * SPAN]
    scaled = times_gain(grad, gain)
    mean = jnp.sum(scaled, axis=0, keepdims=True) * (1.0 / D)
    mean_x = jnp.sum(scaled * xhat, axis=0, keepdims=True) * (1.0 / D)
    return factor * (scaled - mean - xhat * mean_x)


def mlp_back_kernel(
    meta_ref, seed_ref, act_ref, gp_ref, xh2_ref, r2_ref, att_ref, gains_ref, *refs, layer, masked,
):
    weights, refs = fives(refs, 3)
    (send_ref, keep_ref, gln_ref, gh_ref, gatt_ref, gdown_acc, gup_acc, gout_acc, gln_acc,
     wdown_ref, wup_ref, wout_ref, sems) = refs
    step = pl.program_id(0)
    tile = N_TILE - 1 - step
    wait = weight_waits(meta_ref, layer, weights, (wdown_ref, wup_ref, wout_ref), sems)

    @pl.when(step == 0)
    def _():
        gdown_acc[...] = jnp.zeros_like(gdown_acc)
        gup_acc[...] = jnp.zeros_like(gup_acc)
        gout_acc[...] = jnp.zeros_like(gout_acc)
        gln_acc[...] = jnp.zeros_like(gln_acc)

    low = seed_ref[...].T
    if masked:
        parts = []
        cols = lax.broadcasted_iota(jnp.int32, (D, SPAN), 1)
        for j in range(TILE_BLK):
            filled, _ = block_facts(meta_ref, tile * TILE_BLK + j)
            part = low[:, j * SPAN:(j + 1) * SPAN]
            parts.append(jnp.where(cols < filled, part, jnp.zeros((), BF)))
        low = jnp.concatenate(parts, axis=1)
    gain = gain_column(gains_ref, 1)
    xhat = xh2_ref[...].astype(F32)
    second = times_gain(xhat, gain).astype(BF)
    wait(0)
    wait(1)
    e = None
    for f in range(FF // FF_STEP):
        part = slice(f * FF_STEP, (f + 1) * FF_STEP)
        gdown_acc[part] += dot(act_ref[part], low, 1, 1)
        ga = dot(wdown_ref[part], low, 1, 0)
        gui = (ga * gp_ref[part].astype(F32)).astype(BF)
        gup_acc[part] += dot(gui, second, 1, 1)
        term = dot(wup_ref[:, part], gui, 1, 0)
        e = term if e is None else e + term
    gh = low.astype(F32) + norm_back(e, gain, xhat, r2_ref[...], gln_acc)
    gh_ref[...] = gh
    ghb = gh.astype(BF)
    gout_acc[...] += dot(att_ref[...], ghb, 1, 1)
    wait(2)
    gatt_ref[...] = dot(wout_ref[...], ghb, 1, 0).astype(BF)

    @pl.when(step == N_TILE - 1)
    def _():
        write_halves(meta_ref, (gdown_acc, gup_acc, gout_acc), MLP_SHARDS, send_ref, keep_ref)
        gln_ref[...] = jnp.sum(gln_acc[...].T, axis=0, keepdims=True)


def attn_back_kernel(
    meta_ref, gh_ref, gatt_ref, xh1_ref, r1_ref, qkv_ref, krow_ref, vrow_ref, lse_ref, ks_ref,
    vs_ref, gains_ref, gln2_ref, *refs, layer,
):
    weights, refs = fives(refs, 1)
    (gin_ref, send_ref, keep_ref, gqkv_acc, gln_acc, gks_acc, gvs_acc, rows_ref, wqkv_ref,
     sems) = refs
    step = pl.program_id(0)
    tile_start = (N_TILE - 1 - step) * TILE_BLK
    wait = weight_waits(meta_ref, layer, weights, (wqkv_ref,), sems)

    @pl.when(step == 0)
    def _():
        gqkv_acc[...] = jnp.zeros_like(gqkv_acc)
        gln_acc[...] = jnp.zeros_like(gln_acc)
        gks_acc[...] = jnp.zeros_like(gks_acc)
        gvs_acc[...] = jnp.zeros_like(gvs_acc)

    q_t = qkv_ref[:D]
    gatt = gatt_ref[...]
    key_sums, value_sums = ks_ref[...], vs_ref[...]
    ks_t = key_sums.T
    for j in range(0, TILE_BLK, BACK_GROUP):
        items = attention_items(meta_ref, tile_start, range(j, j + BACK_GROUP))
        q_diags = [pair_diag(q_t[feats, cols]) for cols, _, feats, _ in items]
        g_diags = [pair_diag(gatt[feats, cols]) for cols, _, feats, _ in items]
        scores = [
            dot(jnp.concatenate([krow_ref[cols, feats], key_sums[:, feats]], axis=0), q, 1, 0)
            for (cols, _, feats, _), q in zip(items, q_diags)
        ]
        dps = [
            dot(jnp.concatenate([vrow_ref[cols, feats], value_sums[:, feats]], axis=0), g, 1, 0)
            for (cols, _, feats, _), g in zip(items, g_diags)
        ]
        grads, probs = [], []
        for (cols, hp, feats, mask), score, dp in zip(items, scores, dps):
            logs = jnp.concatenate(
                [lse_ref[2 * hp:2 * hp + 1, cols], lse_ref[2 * hp + 1:2 * hp + 2, cols]], axis=1
            )
            prob = jnp.exp(jnp.where(mask, score, NEG_FILL) - logs)
            weighted = prob * dp
            delta = jnp.sum(weighted, axis=0, keepdims=True)
            grads.append((weighted - prob * delta).astype(BF))
            probs.append(prob.astype(BF))
        for (cols, hp, feats, _), grad, prob, q, g in zip(items, grads, probs, q_diags, g_diags):
            key_feats = slice(D + hp * SPAN, D + (hp + 1) * SPAN)
            value_feats = slice(2 * D + hp * SPAN, 2 * D + (hp + 1) * SPAN)
            keys = jnp.concatenate([qkv_ref[key_feats, cols], ks_t[feats]], axis=1)
            rows_ref[feats, cols] = diag_rows(dot(keys, grad, 1, 0))
            key_grad = dot(q, grad, 1, 1)
            value_grad = dot(g, prob, 1, 1)
            rows_ref[key_feats, cols] = key_grad[:, :SPAN]
            rows_ref[value_feats, cols] = value_grad[:, :SPAN]
            gks_acc[feats] += key_grad[:, SPAN:]
            gvs_acc[feats] += value_grad[:, SPAN:]
    members = member_mask(meta_ref, tile_start)
    fill = filled_row(meta_ref)

    def spread_back(acc_ref):
        back = (acc_ref[...].astype(BF).astype(F32) / fill).astype(BF)
        return dot(back, members, 1, 0)

    grad_q = rows_ref[:D] * HEAD_DIM ** (-0.5)
    grad_k = rows_ref[D:2 * D] + spread_back(gks_acc)
    grad_v = rows_ref[2 * D:] + spread_back(gvs_acc)
    gain = gain_column(gains_ref, 0)
    xhat = xh1_ref[...].astype(F32)
    normed = times_gain(xhat, gain).astype(BF)
    wait(0)
    e = None
    for i, rows in enumerate((grad_q, grad_k, grad_v)):
        rows = rows.astype(BF)
        part = slice(i * D, (i + 1) * D)
        gqkv_acc[part] += dot(rows, normed, 1, 1)
        term = dot(wqkv_ref[:, part], rows, 1, 0)
        e = term if e is None else e + term
    gin = gh_ref[...] + norm_back(e, gain, xhat, r1_ref[...], gln_acc)
    gin_ref[...] = gin.astype(BF).T

    @pl.when(step == N_TILE - 1)
    def _():
        gln = jnp.sum(gln_acc[...].T, axis=0, keepdims=True)
        rest = jnp.zeros((GAIN_ROWS - 2, D), F32)
        last = jnp.concatenate([gln, gln2_ref[...], rest], axis=0).astype(BF)
        write_halves(meta_ref, (gqkv_acc,), QKV_SHARDS, send_ref, keep_ref, last)


ANY = pl.BlockSpec(memory_space=pl.ANY)
sds = jax.ShapeDtypeStruct


def whole(shape):
    return pl.BlockSpec(shape, lambda t, *_: (0,) * len(shape), pipeline_mode=pl.Buffered(1))


def rows_spec(width):
    return pl.BlockSpec((TILE, width), lambda t, *_: (t, 0))


def cols_spec(height):
    return pl.BlockSpec((height, TILE), lambda t, *_: (0, t))


def rev_rows(width):
    return pl.BlockSpec((TILE, width), lambda t, *_: (N_TILE - 1 - t, 0))


def rev_cols(height):
    return pl.BlockSpec((height, TILE), lambda t, *_: (0, N_TILE - 1 - t))


def call(kernel, grid, outs, in_specs, out_specs, scratch, flops, args):
    moved = sum(a.size * a.dtype.itemsize for a in args) + sum(
        o.size * o.dtype.itemsize for o in outs
    )
    return pl.pallas_call(
        kernel,
        out_shape=tuple(outs),
        grid_spec=pltpu.PrefetchScalarGridSpec(
            num_scalar_prefetch=1, grid=grid, in_specs=in_specs, out_specs=out_specs,
            scratch_shapes=scratch,
        ),
        cost_estimate=pl.CostEstimate(
            flops=int(flops), bytes_accessed=int(moved), transcendentals=0
        ),
        compiler_params=pltpu.CompilerParams(vmem_limit_bytes=VMEM_LIMIT),
    )(*args)


LINEAR = 2.0 * MB_TOK * D


def col(height, kind=BF):
    return sds((height, MB_TOK), kind)


def attn_outputs():
    shapes = [
        col(D), col(1, F32), col(3 * D), sds((MB_TOK, D), BF), sds((MB_TOK, D), BF),
        col(HEADS, F32), col(D), col(D), col(1, F32), sds((PAD_BLK, D), BF), sds((PAD_BLK, D), BF),
    ]
    specs = [
        cols_spec(D), cols_spec(1), cols_spec(3 * D), rows_spec(D), rows_spec(D), cols_spec(HEADS),
        cols_spec(D), cols_spec(D), cols_spec(1), whole((PAD_BLK, D)), whole((PAD_BLK, D)),
    ]
    return shapes, specs


MLP_OUTS = ([sds((MB_TOK, D), BF), col(FF), col(FF)], [(D, 0), (FF, 1), (FF, 1)])


def input_spec(layer):
    if layer == 0:
        return pl.BlockSpec((TILE, D), lambda t, m: (m[6] * N_TILE + t, 0))
    return rows_spec(D)


def weight_scratch(*weights):
    return [pltpu.VMEM(w[0].shape, BF) for w in weights] + [
        pltpu.SemaphoreType.DMA((len(weights),))
    ]


def flat(weights):
    return [ref for weight in weights for ref in weight]


def attn_scratch():
    return [pltpu.VMEM((D, TILE), BF)]


def forward(meta, x, gains, wqkv, wout, wup, wdown, layer):
    shapes, specs = attn_outputs()
    weights = (wqkv, wout, wup, wdown)
    out = call(
        functools.partial(forward_kernel, layer=layer), (N_TILE,),
        shapes + MLP_OUTS[0],
        [input_spec(layer), whole((2, D))] + [ANY] * 20,
        specs + [rows_spec(D), cols_spec(FF), cols_spec(FF)],
        attn_scratch() + weight_scratch(*weights),
        LINEAR * (4 * D + 2 * FF) * 1.5,
        (meta, x, gains, *flat(weights)),
    )
    return out[:11], out[11:]


def forward_attn(meta, x, gains, wqkv, wout, layer):
    shapes, specs = attn_outputs()
    weights = (wqkv, wout)
    out = call(
        functools.partial(forward_attn_kernel, layer=layer), (N_TILE,),
        shapes + [col(D, F32), col(D)],
        [input_spec(layer), whole((2, D))] + [ANY] * 10,
        specs + [cols_spec(D), cols_spec(D)],
        attn_scratch() + weight_scratch(*weights),
        LINEAR * 4 * D * 2,
        (meta, x, gains, *flat(weights)),
    )
    return out[:11], out[11], out[12]


def forward_mlp(meta, hidden, second, wup, wdown, layer):
    weights = (wup, wdown)
    return call(
        functools.partial(forward_mlp_kernel, layer=layer), (N_TILE,),
        MLP_OUTS[0],
        [cols_spec(D), cols_spec(D)] + [ANY] * 10,
        [rows_spec(D), cols_spec(FF), cols_spec(FF)],
        weight_scratch(*weights),
        LINEAR * 2 * FF * 1.5,
        (meta, hidden, second, *flat(weights)),
    )


def mlp_back(meta, seed, act, gp, xh2, r2, att, gains, wdown, wup, wout, layer):
    masked = layer == 1
    if masked:
        seed_spec = pl.BlockSpec((TILE, D), lambda t, m: (m[6] * N_TILE + N_TILE - 1 - t, 0))
    else:
        seed_spec = rev_rows(D)
    weights = (wdown, wup, wout)
    half = 8 * sum(MLP_SHARDS)
    return call(
        functools.partial(mlp_back_kernel, layer=layer, masked=masked), (N_TILE,),
        [sds((half, D), BF), sds((half, D), BF), sds((1, D), F32), col(D, F32), col(D)],
        [
            seed_spec, rev_cols(FF), rev_cols(FF), rev_cols(D), rev_cols(1), rev_cols(D),
            whole((2, D)),
        ] + [ANY] * 15,
        [whole((half, D)), whole((half, D)), whole((1, D)), rev_cols(D), rev_cols(D)],
        [
            pltpu.VMEM((FF, D), F32), pltpu.VMEM((FF, D), F32), pltpu.VMEM((D, D), F32),
            pltpu.VMEM((D, SPAN), F32),
        ] + weight_scratch(*weights),
        LINEAR * (4 * FF + 2 * D) * 1.5,
        (meta, seed, act, gp, xh2, r2, att, gains, *flat(weights)),
    )


def attn_back(meta, gh, gatt, xh1, r1, qkv, krow, vrow, lse, ks, vs, gains, gln2, wqkv, layer):
    half = 8 * (sum(QKV_SHARDS) + GAIN_ROWS)
    return call(
        functools.partial(attn_back_kernel, layer=layer), (N_TILE,),
        [sds((MB_TOK, D), BF), sds((half, D), BF), sds((half, D), BF)],
        [
            rev_cols(D), rev_cols(D), rev_cols(D), rev_cols(1), rev_cols(3 * D), rev_rows(D),
            rev_rows(D), rev_cols(HEADS), whole((PAD_BLK, D)), whole((PAD_BLK, D)), whole((2, D)),
            whole((1, D)),
        ] + [ANY] * 5,
        [rev_rows(D), whole((half, D)), whole((half, D))],
        [
            pltpu.VMEM((3 * D, D), F32), pltpu.VMEM((D, SPAN), F32), pltpu.VMEM((D, PAD_BLK), F32),
            pltpu.VMEM((D, PAD_BLK), F32), pltpu.VMEM((3 * D, TILE), F32),
        ] + weight_scratch(wqkv),
        LINEAR * 12 * D * 1.5,
        (meta, gh, gatt, xh1, r1, qkv, krow, vrow, lse, ks, vs, gains, gln2, *wqkv),
    )


def finish_kernel(meta_ref, *refs, widths, flips):
    pieces, refs = refs[:4], refs[4:]
    outs, held, sem = refs[:len(widths)], refs[-2], refs[-1]
    rows = held.shape[0] // 4
    for index, piece in enumerate(pieces):
        place = meta_ref[7] ^ index
        spot = (place & 1) * 2 + (place >> 1)
        pltpu.make_async_copy(
            piece, held.at[pl.ds(pl.multiple_of(spot * rows, rows), rows)], sem
        ).start()
    for index, piece in enumerate(pieces):
        pltpu.make_async_copy(piece, held.at[pl.ds(index * rows, rows)], sem).wait()
    total = sum(widths)
    for i, (width, flip) in enumerate(zip(widths, flips)):
        for s in range(16):
            start = s * total + sum(widths[:i])
            part = held[pl.ds(start, width)].astype(F32)
            if flip:
                outs[i][:, pl.ds(s * width, width)] = part.T
            else:
                outs[i][pl.ds(s * width, width)] = part


def finish(meta, pieces, widths, flips):
    rows = pieces[0].shape[0]
    outs = [
        sds((D, 16 * w), F32) if flip else sds((16 * w, D), F32) for w, flip in zip(widths, flips)
    ]
    return call(
        functools.partial(finish_kernel, widths=widths, flips=flips), (1,),
        outs, [ANY] * 4, [whole(o.shape) for o in outs],
        [pltpu.VMEM((4 * rows, D), BF), pltpu.SemaphoreType.DMA],
        0.0, (meta, *pieces),
    )


def swap_xor(value, mask):
    size = lax.axis_size("dp")
    return lax.ppermute(value, "dp", [(i, i ^ mask) for i in range(size)])


def swap_section(value):
    return lax.ppermute(value, "section", [(0, 1), (1, 0)])


def to_section(value, target):
    return lax.ppermute(value, "section", [(1 - target, target)])


def added(*values):
    total = values[0].astype(F32)
    for value in values[1:]:
        total = total + value.astype(F32)
    return total.astype(BF)


def halves(value, bit):
    half = value.shape[0] // 2
    mine = (lax.axis_index("dp") >> bit) & 1
    return (
        lax.dynamic_slice_in_dim(value, mine * half, half, 0),
        lax.dynamic_slice_in_dim(value, (1 - mine) * half, half, 0),
    )


def half_sum(pair, bit):
    return added(pair[0], swap_xor(pair[1], 1 << bit))


def quarters(value, bit):
    rows = value.shape[0] // 4
    mine = (lax.axis_index("dp") >> bit) & 3
    return tuple(lax.dynamic_slice_in_dim(value, (mine ^ k) * rows, rows, 0) for k in range(4))


def swap_quarters(parts, bit):
    return [swap_xor(parts[k], k << bit) for k in (1, 2, 3)]


def quarter_sum(parts, bit):
    return added(parts[0], *swap_quarters(parts, bit))


def tie(*values):
    return lax.optimization_barrier(values)


def rest_bits():
    return range(4, lax.axis_size("dp").bit_length() - 1)


def reduce_core(halves):
    return added(halves[1], swap_xor(halves[0], 1))


def reduce_rest(value):
    for bit in rest_bits():
        value = half_sum(halves(value, bit), bit)
    return value


def gather_bit(value, bit):
    mine = (lax.axis_index("dp") >> bit) & 1
    other = swap_xor(value, 1 << bit)
    return jnp.where(
        mine == 0,
        jnp.concatenate([value, other], axis=0),
        jnp.concatenate([other, value], axis=0),
    )


def gather_quad(value, bit):
    mine = (lax.axis_index("dp") >> bit) & 3
    got = [value] + [swap_xor(value, k << bit) for k in (1, 2, 3)]
    parts = []
    for p in range(4):
        which = mine ^ p
        part = got[3]
        for k in (2, 1, 0):
            part = jnp.where(which == k, got[k], part)
        parts.append(part)
    return jnp.concatenate(parts, axis=0)


def gather_pieces(value):
    for bit in reversed(rest_bits()):
        value = gather_bit(value, bit)
    value = gather_quad(value, 2)
    across = swap_xor(value, 2)
    return value, swap_xor(value, 1), across, swap_xor(across, 1)


def fetch_pieces(value):
    piece = swap_section(value)
    across = swap_xor(piece, 2)
    return piece, swap_xor(piece, 1), across, swap_xor(across, 1)


def sum_rest(value):
    for bit in rest_bits():
        value = added(value, swap_xor(value, 1 << bit))
    return value


def per_device(
    tokens, cotangent, span_counts, tail_lens, ln1_gain, w_qkv, w_out, ln2_gain, w_up, w_down
):
    section = lax.axis_index("section")
    first = section == 0
    place = lax.axis_index("dp") & 3
    meta = jnp.concatenate([
        lax.dynamic_index_in_dim(span_counts, section, 0, keepdims=False),
        lax.dynamic_index_in_dim(tail_lens, section, 0, keepdims=False),
        section.astype(jnp.int32)[None], place.astype(jnp.int32)[None],
    ])
    own = (w_qkv[0], w_out[0], w_up[0], w_down[0])

    def quarter(weight):
        rows = weight.shape[0] // 4
        return lax.dynamic_slice_in_dim(weight, place * rows, rows, 0)

    own_gains = jnp.concatenate([ln1_gain, ln2_gain], axis=0)
    other_gains = swap_section(own_gains)
    wqkv = (own[0],) + fetch_pieces(quarter(own[0]))
    wout = (own[1],) + fetch_pieces(quarter(own[1]))
    up = swap_section(quarter(own[2]))
    down = swap_section(quarter(own[3]))
    up_x, up_c = swap_xor(up, 2), swap_xor(up, 1)
    gains = [jnp.where(first, own_gains, other_gains), jnp.where(first, other_gains, own_gains)]

    keep0, hidden, second = forward_attn(meta, tokens, gains[0], wqkv, wout, 0)
    keep0, hidden, second, up_x, up_c, down = tie(keep0, hidden, second, up_x, up_c, down)
    down_x = swap_xor(down, 2)
    wup = (own[2], up, up_c, up_x, swap_xor(up_x, 1))
    wdown = (own[3], down, swap_xor(down, 1), down_x, swap_xor(down_x, 1))
    act_out0, act0, gp0 = forward_mlp(meta, hidden, second, wup, wdown, 0)
    half = MB_TOK // 2
    out0_a = to_section(act_out0[:half], 0)
    forward1 = forward(meta, act_out0, gains[1], wqkv, wout, wup, wdown, 1)
    (keep1, (act_out1, act1, gp1)), out0_a, act_out0 = tie(forward1, out0_a, act_out0)
    out0_b = to_section(act_out0[half:], 0)
    out1_a = to_section(act_out1[:half], 1)

    def back_mlp(layer, seed, keep, act, gp):
        att, xh2, r2 = keep[6:9]
        return mlp_back(meta, seed, act, gp, xh2, r2, att, gains[layer], wdown, wup, wout, layer)

    def back_attn(layer, gh, gatt, keep, gln2):
        xh1, r1, qkv, krow, vrow, lse = keep[:6]
        return attn_back(
            meta, gh, gatt, xh1, r1, qkv, krow, vrow, lse, keep[9], keep[10], gains[layer], gln2,
            wqkv, layer,
        )

    back = back_mlp(1, cotangent, keep1, act1, gp1)
    (send, kept, gln2, gh, gatt), out0_b, out1_a, act_out1 = tie(back, out0_b, out1_a, act_out1)
    mlp1 = halves(reduce_core((send, kept)), 1)
    gh, mlp1 = tie(gh, mlp1)
    mlp1_x = swap_xor(mlp1[1], 2)
    out1_b = to_section(act_out1[half:], 1)
    back = back_attn(1, gh, gatt, keep1, gln2)
    (ig1, send, kept), mlp1_x, out1_b = tie(back, mlp1_x, out1_b)
    qkv1 = halves(reduce_core((send, kept)), 1)
    mlp1 = quarters(added(mlp1[0], mlp1_x), 2)
    ig1, mlp1, qkv1 = tie(ig1, mlp1, qkv1)
    mlp1_z = swap_quarters(mlp1, 2)
    qkv1_x = swap_xor(qkv1[1], 2)
    ig1_a = to_section(ig1[:half], 1)
    back = back_mlp(0, ig1, keep0, act0, gp0)
    (send, kept, gln2, gh, gatt), mlp1_z, qkv1_x, ig1_a, ig1 = tie(
        back, mlp1_z, qkv1_x, ig1_a, ig1
    )
    mlp0 = halves(reduce_core((send, kept)), 1)
    mlp1 = added(mlp1[0], *mlp1_z)
    qkv1 = quarters(added(qkv1[0], qkv1_x), 2)
    gh, mlp0, mlp1, qkv1 = tie(gh, mlp0, mlp1, qkv1)
    mlp0_x = swap_xor(mlp0[1], 2)
    qkv1_z = swap_quarters(qkv1, 2)
    ig1_b = to_section(ig1[half:], 1)
    back = back_attn(0, gh, gatt, keep0, gln2)
    (ig0, send, kept), mlp0_x, qkv1_z, ig1_b = tie(back, mlp0_x, qkv1_z, ig1_b)
    ig0_in = to_section(ig0, 0)
    qkv0 = halves(reduce_core((send, kept)), 1)
    mlp0 = quarter_sum(quarters(added(mlp0[0], mlp0_x), 2), 2)
    qkv1 = added(qkv1[0], *qkv1_z)
    qkv0 = quarter_sum(quarters(half_sum(qkv0, 1), 2), 2)

    def own_sum(grad0, grad1):
        got = swap_section(jnp.where(first, grad1, grad0))
        return added(jnp.where(first, grad0, grad1), got)

    mlp = gather_pieces(own_sum(reduce_rest(mlp0), reduce_rest(mlp1)))
    cut = sum(QKV_SHARDS)
    qkv = jnp.concatenate([reduce_rest(qkv0[:cut]), sum_rest(qkv0[cut:])], axis=0)
    qkv = own_sum(qkv, jnp.concatenate([reduce_rest(qkv1[:cut]), sum_rest(qkv1[cut:])], axis=0))
    lns = qkv[-GAIN_ROWS:][:2].astype(F32)
    qkv = gather_pieces(qkv[:-GAIN_ROWS])
    grad_down, grad_up, grad_out = finish(meta, mlp, MLP_SHARDS, (False, True, False))
    (grad_qkv,) = finish(meta, qkv, QKV_SHARDS, (True,))
    out0_in = jnp.concatenate([out0_a, out0_b], axis=0)
    out1_in = jnp.concatenate([out1_a, out1_b], axis=0)
    ig1_in = jnp.concatenate([ig1_a, ig1_b], axis=0)
    activations = jnp.concatenate(
        [jnp.where(first, act_out0, out1_in), jnp.where(first, out0_in, act_out1)], axis=0
    )
    input_grads = jnp.concatenate(
        [jnp.where(first, ig0, ig1_in), jnp.where(first, ig0_in, ig1)], axis=0
    )
    return (
        activations[None],
        input_grads[None],
        lns[:1],
        grad_qkv[None],
        grad_out[None],
        lns[1:],
        grad_up[None],
        grad_down[None],
    )


def solution(mesh):
    return jax.shard_map(
        per_device,
        mesh=mesh,
        in_specs=(
            P("dp", None),
            P("dp", None),
            P("dp", None),
            P("dp", None),
            P("section", None),
            P("section", None, None),
            P("section", None, None),
            P("section", None),
            P("section", None, None),
            P("section", None, None),
        ),
        out_specs=(
            P("section", "dp", None),
            P("section", "dp", None),
            P("section", None),
            P("section", None, None),
            P("section", None, None),
            P("section", None),
            P("section", None, None),
            P("section", None, None),
        ),
        check_vma=False,
    )
```

```python
import functools

import jax
import jax.numpy as jnp
from jax import lax
from jax.experimental import pallas as pl
from jax.experimental.pallas import tpu as pltpu
from jax.sharding import PartitionSpec as P

D = 512
HEADS = 8
HEAD_DIM = 64
FF = 2048
SPAN = 128
MB_BLK = 12
MB_TOK = MB_BLK * SPAN
PAD_BLK = 16
EPSILON = 1e-05
NEG_FILL = -1e30
BF = jnp.bfloat16
F32 = jnp.float32
VMEM_LIMIT = 58 * 2**20

TILE = 512
TILE_BLK = TILE // SPAN
N_TILE = MB_TOK // TILE
FF_STEP = 512
FWD_STEP = 512
FWD_GROUP = 2
BACK_GROUP = 2


def dot(left, right, left_dim, right_dim):
    return lax.dot_general(
        left, right, (((left_dim,), (right_dim,)), ((), ())), preferred_element_type=F32
    )


def block_facts(meta_ref, block):
    end_one = meta_ref[0]
    end_two = end_one + meta_ref[1]
    in_one = block < end_one
    in_two = block < end_two
    first = jnp.where(in_one, 0, jnp.where(in_two, end_one, end_two))
    last = jnp.where(in_one, end_one, jnp.where(in_two, end_two, MB_BLK)) - 1
    tail = jnp.where(in_one, meta_ref[3], jnp.where(in_two, meta_ref[4], meta_ref[5]))
    filled = jnp.where(block == last, tail, SPAN)
    return filled, first


def filled_column(meta_ref, width):
    rows = lax.broadcasted_iota(jnp.int32, (PAD_BLK, width), 0)
    out = jnp.full((PAD_BLK, width), SPAN, jnp.int32)
    for block in range(MB_BLK):
        filled, _ = block_facts(meta_ref, block)
        out = jnp.where(rows == block, filled, out)
    return out.astype(F32)


def filled_row(meta_ref):
    cols = lax.broadcasted_iota(jnp.int32, (1, PAD_BLK), 1)
    out = jnp.full((1, PAD_BLK), SPAN, jnp.int32)
    for block in range(MB_BLK):
        filled, _ = block_facts(meta_ref, block)
        out = jnp.where(cols == block, filled, out)
    return out.astype(F32)


def member_mask(meta_ref, tile_start):
    parts = []
    rows = lax.broadcasted_iota(jnp.int32, (PAD_BLK, SPAN), 0)
    cols = lax.broadcasted_iota(jnp.int32, (PAD_BLK, SPAN), 1)
    for j in range(TILE_BLK):
        block = tile_start + j
        filled, _ = block_facts(meta_ref, block)
        parts.append(jnp.where((rows == block) & (cols < filled), 1.0, 0.0).astype(BF))
    return jnp.concatenate(parts, axis=1)


def pair_diag(rows_two):
    zero = jnp.zeros((HEAD_DIM, SPAN), rows_two.dtype)
    top = jnp.concatenate([rows_two[:HEAD_DIM], zero], axis=1)
    low = jnp.concatenate([zero, rows_two[HEAD_DIM:]], axis=1)
    return jnp.concatenate([top, low], axis=0)


def diag_rows(square):
    return jnp.concatenate([square[:HEAD_DIM, :SPAN], square[HEAD_DIM:, SPAN:]], axis=0)


def gain_column(gains_ref, index):
    return jnp.broadcast_to(gains_ref[index:index + 1], (SPAN, D)).T


def times_gain(values, gain):
    return jnp.concatenate(
        [values[:, i * SPAN:(i + 1) * SPAN] * gain for i in range(values.shape[1] // SPAN)], axis=1
    )


def normalize(values):
    mean = jnp.sum(values, axis=0, keepdims=True) * (1.0 / D)
    center = values - mean
    spread = jnp.sum(center * center, axis=0, keepdims=True) * (1.0 / D)
    factor = lax.rsqrt(spread + EPSILON)
    return center * factor, factor


def score_mask(block, filled, first):
    rows = lax.broadcasted_iota(jnp.int32, (SPAN + PAD_BLK, 2 * SPAN), 0)
    cols = lax.broadcasted_iota(jnp.int32, (SPAN + PAD_BLK, 2 * SPAN), 1) % SPAN
    local = (rows <= cols) & (rows < filled)
    earlier = (rows >= SPAN + first) & (rows < SPAN + block)
    return local | earlier


def attention_items(meta_ref, tile_start, blocks):
    items = []
    for j in blocks:
        filled, first = block_facts(meta_ref, tile_start + j)
        mask = score_mask(tile_start + j, filled, first)
        for hp in range(HEADS // 2):
            items.append((slice(j * SPAN, (j + 1) * SPAN), hp, slice(hp * SPAN, (hp + 1) * SPAN), mask))
    return items


class Weight:
    def __init__(self, own, *groups):
        self.own = own
        self.groups = [(tuple(p), lane, at, width or own.shape[1]) for p, lane, at, width in groups]

    def flat(self):
        return (self.own,) + sum((group[0] for group in self.groups), ())

    def bind(self, refs):
        own, refs, groups = refs[0], refs[1:], []
        for pieces, *rest in self.groups:
            groups.append((refs[:len(pieces)], *rest))
            refs = refs[len(pieces):]
        return Weight(own, *groups), refs


def start_weight(meta_ref, layer, weight, target, sem):
    @pl.when(meta_ref[6] == layer)
    def _():
        pltpu.make_async_copy(weight.own, target, sem).start()

    @pl.when(meta_ref[6] != layer)
    def _():
        for pieces, lane, at, width in weight.groups:
            count = len(pieces)
            rows = target.shape[0] // count
            for index, piece in enumerate(pieces):
                spot = (meta_ref[7] & (count - 1)) ^ index
                pltpu.make_async_copy(
                    piece.at[:, pl.ds(lane, width)],
                    target.at[pl.ds(pl.multiple_of(spot * rows, rows), rows), pl.ds(at, width)], sem,
                ).start()


def wait_weight(weight, target, sem):
    pltpu.make_async_copy(weight.own, target, sem).wait()


def forward_attn_part(meta_ref, tile, x_ref, gains_ref, outs, scratch, wqkv_ref, wout_ref, wait):
    (xh1_ref, r1_ref, qkv_ref, krow_ref, vrow_ref, lse_ref, att_ref, xh2_ref, r2_ref, ks_ref,
     vs_ref) = outs
    (attf_ref,) = scratch
    tile_start = tile * TILE_BLK

    @pl.when(tile == 0)
    def _():
        ks_ref[...] = jnp.zeros_like(ks_ref)
        vs_ref[...] = jnp.zeros_like(vs_ref)

    x_t = x_ref[...].T.astype(F32)
    xhat, r1 = normalize(x_t)
    xh1_ref[...] = xhat.astype(BF)
    r1_ref[...] = r1
    normed = times_gain(xhat, gain_column(gains_ref, 0)).astype(BF)
    wait(0)
    q_t = (dot(wqkv_ref[:, :D], normed, 0, 0) * HEAD_DIM ** (-0.5)).astype(BF)
    k_t = dot(wqkv_ref[:, D:2 * D], normed, 0, 0).astype(BF)
    v_t = dot(wqkv_ref[:, 2 * D:], normed, 0, 0).astype(BF)
    qkv_ref[:D] = q_t
    qkv_ref[D:2 * D] = k_t
    qkv_ref[2 * D:] = v_t
    krow = k_t.T
    vrow = v_t.T
    krow_ref[...] = krow
    vrow_ref[...] = vrow
    members = member_mask(meta_ref, tile_start)
    fill = filled_column(meta_ref, D)
    block_rows = lax.broadcasted_iota(jnp.int32, (PAD_BLK, D), 0)
    fresh = (block_rows >= tile_start) & (block_rows < tile_start + TILE_BLK)
    key_sums = jnp.where(fresh, (dot(members, krow, 1, 0) / fill).astype(BF), ks_ref[...])
    value_sums = jnp.where(fresh, (dot(members, vrow, 1, 0) / fill).astype(BF), vs_ref[...])
    ks_ref[...] = key_sums
    vs_ref[...] = value_sums
    vs_t = value_sums.T
    for j in range(0, TILE_BLK, FWD_GROUP):
        items = attention_items(meta_ref, tile_start, range(j, j + FWD_GROUP))
        scores = [
            dot(
                jnp.concatenate([krow[cols, feats], key_sums[:, feats]], axis=0),
                pair_diag(q_t[feats, cols]), 1, 0,
            )
            for cols, _, feats, _ in items
        ]
        probs = []
        for (cols, hp, feats, mask), score in zip(items, scores):
            score = jnp.where(mask, score, NEG_FILL)
            top = jnp.max(score, axis=0, keepdims=True)
            prob = jnp.exp(score - top)
            total = jnp.sum(prob, axis=0, keepdims=True)
            logs = top + jnp.log(total)
            lse_ref[2 * hp:2 * hp + 1, cols] = logs[:, :SPAN]
            lse_ref[2 * hp + 1:2 * hp + 2, cols] = logs[:, SPAN:]
            probs.append((prob * (1.0 / total)).astype(BF))
        for (cols, _, feats, _), prob in zip(items, probs):
            values = jnp.concatenate([v_t[feats, cols], vs_t[feats]], axis=1)
            attf_ref[feats, cols] = diag_rows(dot(values, prob, 1, 0)).astype(BF)
    att = attf_ref[...]
    att_ref[...] = att
    wait(1)
    hidden = x_t + dot(wout_ref[...], att, 0, 0)
    xhat2, r2 = normalize(hidden)
    xh2_ref[...] = xhat2.astype(BF)
    r2_ref[...] = r2
    return hidden, times_gain(xhat2, gain_column(gains_ref, 1)).astype(BF)


def forward_mlp_part(hidden, second, outs, wup_ref, wdown_ref):
    out_ref, act_ref, gp_ref = outs
    total_out = hidden
    up = dot(wup_ref[:, :FWD_STEP], second, 0, 0)
    for f in range(FF // FWD_STEP):
        part = slice(f * FWD_STEP, (f + 1) * FWD_STEP)
        later = slice((f + 1) * FWD_STEP, (f + 2) * FWD_STEP)
        ahead = dot(wup_ref[:, later], second, 0, 0) if later.stop <= FF else None
        bell = jnp.exp(up * up * -0.5)
        phi = 0.5 + 0.5 * lax.erf(up * (0.5 ** 0.5))
        act = (up * phi).astype(BF)
        act_ref[part] = act
        gp_ref[part] = (phi + up * bell * 0.3989422804014327).astype(BF)
        total_out = total_out + dot(wdown_ref[part], act, 0, 0)
        up = ahead
    out_ref[...] = total_out.astype(BF).T


def weight_waits(meta_ref, layer, weights, targets, sems):
    begin = pl.program_id(0) == 0

    @pl.when(begin)
    def _():
        for i, (weight, target) in enumerate(zip(weights, targets)):
            start_weight(meta_ref, layer, weight, target, sems.at[i])

    def wait(i):
        @pl.when(begin)
        def _():
            wait_weight(weights[i], targets[i], sems.at[i])

    return wait


def bound(weights, refs):
    out = []
    for weight in weights:
        weight, refs = weight.bind(refs)
        out.append(weight)
    return out, refs


def forward_attn_kernel(meta_ref, x_ref, gains_ref, *refs, layer, weights):
    weights, refs = bound(weights, refs)
    attn_outs, (hid_ref, sec_ref), scratch, targets, sems = (
        refs[:11], refs[11:13], refs[13:14], refs[14:16], refs[16]
    )
    wait = weight_waits(meta_ref, layer, weights, targets, sems)
    hidden, second = forward_attn_part(
        meta_ref, pl.program_id(0), x_ref, gains_ref, attn_outs, scratch, targets[0], targets[1], wait
    )
    hid_ref[...] = hidden
    sec_ref[...] = second


def forward_mlp_kernel(meta_ref, hid_ref, sec_ref, *refs, layer, weights):
    weights, refs = bound(weights, refs)
    outs, targets, sems = refs[:3], refs[3:5], refs[5]
    wait = weight_waits(meta_ref, layer, weights, targets, sems)
    wait(0)
    wait(1)
    forward_mlp_part(hid_ref[...], sec_ref[...], outs, *targets)


def write_halves(meta_ref, parts, send_ref, keep_ref, start=0, z_first=False):
    core = meta_ref[7] & 1
    total = sum(rows for _, _, rows in parts)
    for target, side in ((send_ref, 1 - core), (keep_ref, core)):
        for s in range(8):
            spot = start + ((s % 4) * 2 + s // 4 if z_first else s) * total
            for acc, base, rows in parts:
                if acc.shape[0] == rows:
                    value = acc[...]
                else:
                    first = base + pl.multiple_of(side * (8 * rows), 8 * rows) + s * rows
                    value = acc[pl.ds(first, rows)]
                target[pl.ds(spot, rows)] = value.astype(BF)
                spot += rows


def write_shards(parts, target):
    for place in range(16):
        s = (place & 1) * 8 + ((place >> 1) & 1) * 4 + (place >> 2)
        spot = 0
        for acc, base, rows in parts:
            value = acc[...] if acc.shape[0] == rows else acc[pl.ds(base + s * rows, rows)]
            target[place, pl.ds(spot, rows)] = value.astype(BF)
            spot += rows


DOWN_ROWS, OUT_ROWS, QKV_ROWS, GAIN_ROWS = FF // 16, D // 16, 3 * D // 16, 16
UP_A = FF // 4
UP_B = FF - UP_A
PART_A, PART_B = DOWN_ROWS + UP_A // 16 + OUT_ROWS, UP_B // 16
PART_C = QKV_ROWS + GAIN_ROWS


def norm_back(grad, gain, xhat, factor, gln_acc):
    prod = grad * xhat
    for j in range(TILE_BLK):
        gln_acc[...] += prod[:, j * SPAN:(j + 1) * SPAN]
    scaled = times_gain(grad, gain)
    mean = jnp.sum(scaled, axis=0, keepdims=True) * (1.0 / D)
    mean_x = jnp.sum(scaled * xhat, axis=0, keepdims=True) * (1.0 / D)
    return factor * (scaled - mean - xhat * mean_x)


def masked_low(meta_ref, tile, low):
    parts = []
    cols = lax.broadcasted_iota(jnp.int32, (D, SPAN), 1)
    for j in range(TILE_BLK):
        filled, _ = block_facts(meta_ref, tile * TILE_BLK + j)
        part = low[:, j * SPAN:(j + 1) * SPAN]
        parts.append(jnp.where(cols < filled, part, jnp.zeros((), BF)))
    return jnp.concatenate(parts, axis=1)


def zero_all(refs):
    for ref in refs:
        ref[...] = jnp.zeros_like(ref)


def mlp_back_part(low, data, gains_ref, weights, accs, wait, gh_ref, gatt_ref):
    act_ref, gp_ref, xh2_ref, r2_ref, att_ref = data
    wdown_ref, wup_ref, wout_ref = weights
    gdown_acc, gup_acc, gout_acc, gln_acc = accs
    gain = gain_column(gains_ref, 1)
    xhat = xh2_ref[...].astype(F32)
    second = times_gain(xhat, gain).astype(BF)
    wait(0)
    wait(1)
    e = None
    for f in range(FF // FF_STEP):
        part = slice(f * FF_STEP, (f + 1) * FF_STEP)
        gdown_acc[part] += dot(act_ref[part], low, 1, 1)
        ga = dot(wdown_ref[part], low, 1, 0)
        gui = (ga * gp_ref[part].astype(F32)).astype(BF)
        gup_acc[part] += dot(gui, second, 1, 1)
        term = dot(wup_ref[:, part], gui, 1, 0)
        e = term if e is None else e + term
    gh = low.astype(F32) + norm_back(e, gain, xhat, r2_ref[...], gln_acc)
    gh_ref[...] = gh
    ghb = gh.astype(BF)
    gout_acc[...] += dot(att_ref[...], ghb, 1, 1)
    wait(2)
    gatt_ref[...] = dot(wout_ref[...], ghb, 1, 0).astype(BF)


def mlp_parts(gdown_acc, gup_acc, gout_acc):
    part_a = ((gdown_acc, 0, DOWN_ROWS), (gup_acc, UP_B, UP_A // 16), (gout_acc, 0, OUT_ROWS))
    return part_a, ((gup_acc, 0, UP_B // 16),)


def mlp_back_kernel(
    meta_ref, seed_ref, act_ref, gp_ref, xh2_ref, r2_ref, att_ref, gains_ref, *refs, layer, weights,
):
    weights, refs = bound(weights, refs)
    (send_ref, keep_ref, gln_ref, gh_ref, gatt_ref, gdown_acc, gup_acc, gout_acc, gln_acc,
     wdown_ref, wup_ref, wout_ref, sems) = refs
    step = pl.program_id(0)
    targets = (wdown_ref, wup_ref, wout_ref)
    accs = (gdown_acc, gup_acc, gout_acc, gln_acc)
    wait = weight_waits(meta_ref, layer, weights, targets, sems)

    @pl.when(step == 0)
    def _():
        zero_all(accs)

    mlp_back_part(
        seed_ref[...].T, (act_ref, gp_ref, xh2_ref, r2_ref, att_ref), gains_ref, targets, accs, wait,
        gh_ref, gatt_ref,
    )

    @pl.when(step == N_TILE - 1)
    def _():
        part_a, part_b = mlp_parts(*accs[:3])
        write_halves(meta_ref, part_a, send_ref, keep_ref)
        write_halves(meta_ref, part_b, send_ref, keep_ref, 8 * PART_A, True)
        gln_ref[...] = jnp.sum(gln_acc[...].T, axis=0, keepdims=True)


def attn_back_part(meta_ref, tile, gh_ref, gatt_ref, data, gains_ref, wqkv_ref, accs, rows_ref, wait):
    xh1_ref, r1_ref, qkv_ref, krow_ref, vrow_ref, lse_ref, ks_ref, vs_ref = data
    gqkv_acc, gln_acc, gks_acc, gvs_acc = accs
    tile_start = tile * TILE_BLK
    q_t = qkv_ref[:D]
    gatt = gatt_ref[...]
    key_sums, value_sums = ks_ref[...], vs_ref[...]
    ks_t = key_sums.T
    for j in range(0, TILE_BLK, BACK_GROUP):
        items = attention_items(meta_ref, tile_start, range(j, j + BACK_GROUP))
        q_diags = [pair_diag(q_t[feats, cols]) for cols, _, feats, _ in items]
        g_diags = [pair_diag(gatt[feats, cols]) for cols, _, feats, _ in items]
        scores = [
            dot(jnp.concatenate([krow_ref[cols, feats], key_sums[:, feats]], axis=0), q, 1, 0)
            for (cols, _, feats, _), q in zip(items, q_diags)
        ]
        dps = [
            dot(jnp.concatenate([vrow_ref[cols, feats], value_sums[:, feats]], axis=0), g, 1, 0)
            for (cols, _, feats, _), g in zip(items, g_diags)
        ]
        grads, probs = [], []
        for (cols, hp, feats, mask), score, dp in zip(items, scores, dps):
            logs = jnp.concatenate(
                [lse_ref[2 * hp:2 * hp + 1, cols], lse_ref[2 * hp + 1:2 * hp + 2, cols]], axis=1
            )
            prob = jnp.exp(jnp.where(mask, score, NEG_FILL) - logs)
            weighted = prob * dp
            delta = jnp.sum(weighted, axis=0, keepdims=True)
            grads.append((weighted - prob * delta).astype(BF))
            probs.append(prob.astype(BF))
        for (cols, hp, feats, _), grad, prob, q, g in zip(items, grads, probs, q_diags, g_diags):
            key_feats = slice(D + hp * SPAN, D + (hp + 1) * SPAN)
            value_feats = slice(2 * D + hp * SPAN, 2 * D + (hp + 1) * SPAN)
            keys = jnp.concatenate([qkv_ref[key_feats, cols], ks_t[feats]], axis=1)
            rows_ref[feats, cols] = diag_rows(dot(keys, grad, 1, 0))
            key_grad = dot(q, grad, 1, 1)
            value_grad = dot(g, prob, 1, 1)
            rows_ref[key_feats, cols] = key_grad[:, :SPAN]
            rows_ref[value_feats, cols] = value_grad[:, :SPAN]
            gks_acc[feats] += key_grad[:, SPAN:]
            gvs_acc[feats] += value_grad[:, SPAN:]
    members = member_mask(meta_ref, tile_start)
    fill = filled_row(meta_ref)

    def spread_back(acc_ref):
        back = (acc_ref[...].astype(BF).astype(F32) / fill).astype(BF)
        return dot(back, members, 1, 0)

    grad_q = rows_ref[:D] * HEAD_DIM ** (-0.5)
    grad_k = rows_ref[D:2 * D] + spread_back(gks_acc)
    grad_v = rows_ref[2 * D:] + spread_back(gvs_acc)
    gain = gain_column(gains_ref, 0)
    xhat = xh1_ref[...].astype(F32)
    normed = times_gain(xhat, gain).astype(BF)
    wait(0)
    e = None
    for i, rows in enumerate((grad_q, grad_k, grad_v)):
        rows = rows.astype(BF)
        part = slice(i * D, (i + 1) * D)
        gqkv_acc[part] += dot(rows, normed, 1, 1)
        term = dot(wqkv_ref[:, part], rows, 1, 0)
        e = term if e is None else e + term
    return (gh_ref[...] + norm_back(e, gain, xhat, r1_ref[...], gln_acc)).astype(BF).T


def gain_rows(gln_acc, gln2):
    gln = jnp.sum(gln_acc[...].T, axis=0, keepdims=True)
    rest = jnp.zeros((GAIN_ROWS - 2, D), F32)
    return jnp.concatenate([gln, gln2, rest], axis=0).astype(BF)


def attn_back_kernel(
    meta_ref, gh_ref, gatt_ref, xh1_ref, r1_ref, qkv_ref, krow_ref, vrow_ref, lse_ref, ks_ref,
    vs_ref, gains_ref, gln2_ref, *refs, layer, weights,
):
    weights, refs = bound(weights, refs)
    (gin_ref, send_ref, keep_ref, gqkv_acc, gln_acc, gks_acc, gvs_acc, rows_ref, wqkv_ref,
     sems) = refs
    step = pl.program_id(0)
    wait = weight_waits(meta_ref, layer, weights, (wqkv_ref,), sems)
    accs = (gqkv_acc, gln_acc, gks_acc, gvs_acc)

    @pl.when(step == 0)
    def _():
        zero_all(accs)

    data = (xh1_ref, r1_ref, qkv_ref, krow_ref, vrow_ref, lse_ref, ks_ref, vs_ref)
    gin_ref[...] = attn_back_part(
        meta_ref, N_TILE - 1 - step, gh_ref, gatt_ref, data, gains_ref, wqkv_ref, accs, rows_ref, wait
    )

    @pl.when(step == N_TILE - 1)
    def _():
        parts = ((gqkv_acc, 0, QKV_ROWS), (gain_rows(gln_acc, gln2_ref[...]), 0, GAIN_ROWS))
        write_halves(meta_ref, parts, send_ref, keep_ref)


def layer_kernel(meta_ref, x_ref, cot_ref, gains_ref, *refs, layer, weights):
    weights, refs = bound(weights, refs)
    out_ref, gin_ref, sums_ref, *refs = refs
    keep, refs = refs[:13], refs[13:]
    (xh1, r1, qkv, krow, vrow, lse, att_ref, xh2_ref, r2_ref, ks_ref, vs_ref, gh, gatt) = keep
    act_ref, gp_ref, attf_ref, rows_ref, *refs = refs
    mlp_accs, attn_accs, refs = refs[:4], refs[4:8], refs[8:]
    held_mlp, held_qkv, *refs = refs
    targets, sems, copies = refs[:4], refs[4], refs[5]
    wqkv_ref, wout_ref, wup_ref, wdown_ref = targets
    step = pl.program_id(0)
    wait = weight_waits(meta_ref, layer, weights, targets, sems)
    mlp_rows = PART_A + PART_B
    mlp_copy = pltpu.make_async_copy(held_mlp, sums_ref.at[:, pl.ds(0, mlp_rows)], copies.at[0])
    qkv_copy = pltpu.make_async_copy(held_qkv, sums_ref.at[:, pl.ds(mlp_rows, PART_C)], copies.at[1])

    @pl.when(step == 0)
    def _():
        zero_all(mlp_accs)
        zero_all(attn_accs)

    @pl.when(step < N_TILE)
    def _():
        tile = step
        outs = (
            xh1.at[tile], r1.at[tile], qkv.at[tile], krow.at[tile], vrow.at[tile], lse.at[tile],
            att_ref, xh2_ref, r2_ref, ks_ref, vs_ref,
        )
        hidden, second = forward_attn_part(
            meta_ref, tile, x_ref, gains_ref, outs, (attf_ref,), wqkv_ref, wout_ref, wait
        )
        wait(2)
        wait(3)
        forward_mlp_part(hidden, second, (out_ref, act_ref, gp_ref), wup_ref, wdown_ref)
        mlp_back_part(
            masked_low(meta_ref, tile, cot_ref[...].T), (act_ref, gp_ref, xh2_ref, r2_ref, att_ref),
            gains_ref, (wdown_ref, wup_ref, wout_ref), mlp_accs, lambda i: None, gh.at[tile],
            gatt.at[tile],
        )

    @pl.when(step == N_TILE)
    def _():
        part_a, part_b = mlp_parts(*mlp_accs[:3])
        write_shards(part_a + part_b, held_mlp)
        mlp_copy.start()

    @pl.when(step >= N_TILE)
    def _():
        tile = 2 * N_TILE - 1 - step
        data = (
            xh1.at[tile], r1.at[tile], qkv.at[tile], krow.at[tile], vrow.at[tile], lse.at[tile],
            ks_ref, vs_ref,
        )
        gin_ref[...] = attn_back_part(
            meta_ref, tile, gh.at[tile], gatt.at[tile], data, gains_ref, wqkv_ref, attn_accs,
            rows_ref, lambda i: None,
        )

    @pl.when(step == 2 * N_TILE - 1)
    def _():
        gln2 = jnp.sum(mlp_accs[3][...].T, axis=0, keepdims=True)
        parts = (
            (attn_accs[0], 0, QKV_ROWS), (gain_rows(attn_accs[1], gln2), 0, GAIN_ROWS)
        )
        write_shards(parts, held_qkv)
        qkv_copy.start()
        mlp_copy.wait()
        qkv_copy.wait()


ANY = pl.BlockSpec(memory_space=pl.ANY)
sds = jax.ShapeDtypeStruct


def whole(shape):
    return pl.BlockSpec(shape, lambda t, *_: (0,) * len(shape), pipeline_mode=pl.Buffered(1))


def rows_spec(width):
    return pl.BlockSpec((TILE, width), lambda t, *_: (t, 0))


def cols_spec(height):
    return pl.BlockSpec((height, TILE), lambda t, *_: (0, t))


def rev_rows(width):
    return pl.BlockSpec((TILE, width), lambda t, *_: (N_TILE - 1 - t, 0))


def rev_cols(height):
    return pl.BlockSpec((height, TILE), lambda t, *_: (0, N_TILE - 1 - t))


def call(kernel, grid, outs, in_specs, out_specs, scratch, args):
    return pl.pallas_call(
        kernel,
        out_shape=tuple(outs),
        grid_spec=pltpu.PrefetchScalarGridSpec(
            num_scalar_prefetch=1, grid=grid, in_specs=in_specs, out_specs=out_specs,
            scratch_shapes=scratch,
        ),
        cost_estimate=pl.CostEstimate(flops=0, bytes_accessed=0, transcendentals=0),
        compiler_params=pltpu.CompilerParams(vmem_limit_bytes=VMEM_LIMIT),
    )(*args)


def col(height, kind=BF):
    return sds((height, MB_TOK), kind)


def attn_outputs():
    shapes = [
        col(D), col(1, F32), col(3 * D), sds((MB_TOK, D), BF), sds((MB_TOK, D), BF),
        col(HEADS, F32), col(D), col(D), col(1, F32), sds((PAD_BLK, D), BF), sds((PAD_BLK, D), BF),
    ]
    specs = [
        cols_spec(D), cols_spec(1), cols_spec(3 * D), rows_spec(D), rows_spec(D), cols_spec(HEADS),
        cols_spec(D), cols_spec(D), cols_spec(1), whole((PAD_BLK, D)), whole((PAD_BLK, D)),
    ]
    return shapes, specs


MLP_OUTS = ([sds((MB_TOK, D), BF), col(FF), col(FF)], [(D, 0), (FF, 1), (FF, 1)])


def weight_scratch(*weights):
    return [pltpu.VMEM(w.own.shape, BF) for w in weights] + [
        pltpu.SemaphoreType.DMA((len(weights),))
    ]


def flat(weights):
    return [ref for weight in weights for ref in weight.flat()]


def attn_scratch():
    return [pltpu.VMEM((D, TILE), BF)]


def forward_attn(meta, x, gains, wqkv, wout, layer):
    shapes, specs = attn_outputs()
    weights = (wqkv, wout)
    out = call(
        functools.partial(forward_attn_kernel, layer=layer, weights=weights), (N_TILE,),
        shapes + [col(D, F32), col(D)],
        [
            pl.BlockSpec((TILE, D), lambda t, m: (m[6] * N_TILE + t, 0)), whole((2, D)),
        ] + [ANY] * len(flat(weights)),
        specs + [cols_spec(D), cols_spec(D)],
        attn_scratch() + weight_scratch(*weights),
        (meta, x, gains, *flat(weights)),
    )
    return out[:11], out[11], out[12]


def forward_mlp(meta, hidden, second, wup, wdown, layer):
    weights = (wup, wdown)
    return call(
        functools.partial(forward_mlp_kernel, layer=layer, weights=weights), (N_TILE,),
        MLP_OUTS[0],
        [cols_spec(D), cols_spec(D)] + [ANY] * len(flat(weights)),
        [rows_spec(D), cols_spec(FF), cols_spec(FF)],
        weight_scratch(*weights),
        (meta, hidden, second, *flat(weights)),
    )


def mlp_scratch():
    return [
        pltpu.VMEM((FF, D), F32), pltpu.VMEM((FF, D), F32), pltpu.VMEM((D, D), F32),
        pltpu.VMEM((D, SPAN), F32),
    ]


def attn_back_scratch():
    return [
        pltpu.VMEM((3 * D, D), F32), pltpu.VMEM((D, SPAN), F32), pltpu.VMEM((D, PAD_BLK), F32),
        pltpu.VMEM((D, PAD_BLK), F32),
    ]


def mlp_back(meta, seed, act, gp, xh2, r2, att, gains, wdown, wup, wout, layer):
    weights = (wdown, wup, wout)
    half = 8 * (PART_A + PART_B)
    return call(
        functools.partial(mlp_back_kernel, layer=layer, weights=weights), (N_TILE,),
        [sds((half, D), BF), sds((half, D), BF), sds((1, D), F32), col(D, F32), col(D)],
        [
            rev_rows(D), rev_cols(FF), rev_cols(FF), rev_cols(D), rev_cols(1), rev_cols(D),
            whole((2, D)),
        ] + [ANY] * len(flat(weights)),
        [whole((half, D)), whole((half, D)), whole((1, D)), rev_cols(D), rev_cols(D)],
        mlp_scratch() + weight_scratch(*weights),
        (meta, seed, act, gp, xh2, r2, att, gains, *flat(weights)),
    )


def attn_back(meta, gh, gatt, xh1, r1, qkv, krow, vrow, lse, ks, vs, gains, gln2, wqkv, layer):
    half = 8 * PART_C
    return call(
        functools.partial(attn_back_kernel, layer=layer, weights=(wqkv,)), (N_TILE,),
        [sds((MB_TOK, D), BF), sds((half, D), BF), sds((half, D), BF)],
        [
            rev_cols(D), rev_cols(D), rev_cols(D), rev_cols(1), rev_cols(3 * D), rev_rows(D),
            rev_rows(D), rev_cols(HEADS), whole((PAD_BLK, D)), whole((PAD_BLK, D)), whole((2, D)),
            whole((1, D)),
        ] + [ANY] * len(wqkv.flat()),
        [rev_rows(D), whole((half, D)), whole((half, D))],
        attn_back_scratch() + [pltpu.VMEM((3 * D, TILE), F32)] + weight_scratch(wqkv),
        (meta, gh, gatt, xh1, r1, qkv, krow, vrow, lse, ks, vs, gains, gln2, *wqkv.flat()),
    )


def whole_layer(meta, x, cotangent, gains, wqkv, wout, wup, wdown, layer):
    weights = (wqkv, wout, wup, wdown)
    tiled = lambda *shape: pltpu.VMEM((N_TILE,) + shape, BF)
    sums = sds((16, PART_A + PART_B + PART_C, D), BF)
    forth = lambda t: jnp.minimum(t, N_TILE - 1)
    back = lambda t, *_: (jnp.where(t < N_TILE, N_TILE - 1, 2 * N_TILE - 1 - t), 0)
    return call(
        functools.partial(layer_kernel, layer=layer, weights=weights), (2 * N_TILE,),
        [sds((MB_TOK, D), BF), sds((MB_TOK, D), BF), sums],
        [
            pl.BlockSpec((TILE, D), lambda t, *_: (forth(t), 0)),
            pl.BlockSpec((TILE, D), lambda t, m: (m[6] * N_TILE + forth(t), 0)),
            whole((2, D)),
        ] + [ANY] * len(flat(weights)),
        [
            pl.BlockSpec((TILE, D), lambda t, *_: (forth(t), 0)),
            pl.BlockSpec((TILE, D), back), ANY,
        ],
        [
            tiled(D, TILE), pltpu.VMEM((N_TILE, 1, TILE), F32), tiled(3 * D, TILE), tiled(TILE, D),
            tiled(TILE, D), pltpu.VMEM((N_TILE, HEADS, TILE), F32), pltpu.VMEM((D, TILE), BF),
            pltpu.VMEM((D, TILE), BF), pltpu.VMEM((1, TILE), F32), pltpu.VMEM((PAD_BLK, D), BF),
            pltpu.VMEM((PAD_BLK, D), BF), pltpu.VMEM((N_TILE, D, TILE), F32), tiled(D, TILE),
            pltpu.VMEM((FF, TILE), BF), pltpu.VMEM((FF, TILE), BF), pltpu.VMEM((D, TILE), BF),
            pltpu.VMEM((3 * D, TILE), F32),
        ] + mlp_scratch() + attn_back_scratch() + [
            pltpu.VMEM((16, PART_A + PART_B, D), BF), pltpu.VMEM((16, PART_C, D), BF),
        ] + weight_scratch(*weights) + [pltpu.SemaphoreType.DMA((2,))],
        (meta, x, cotangent, gains, *flat(weights)),
    )


def finish_whole_kernel(held, *outs, widths, flips):
    total = sum(widths)
    for i, (width, flip) in enumerate(zip(widths, flips)):
        start = sum(widths[:i])
        places = [(s & 3) * 4 + ((s >> 2) & 1) * 2 + (s >> 3) for s in range(16)]
        value = jnp.concatenate(
            [held[pl.ds(p * total + start, width)] for p in places], axis=0
        )
        outs[i][...] = (value.T if flip else value).astype(F32)


def finish_whole(value, widths, flips, shapes, specs):
    return pl.pallas_call(
        functools.partial(finish_whole_kernel, widths=widths, flips=flips),
        out_shape=tuple(sds(shape, F32) for shape in shapes),
        grid=(1,), in_specs=[part_spec(value.shape, (0, 0))], out_specs=specs,
        compiler_params=pltpu.CompilerParams(vmem_limit_bytes=VMEM_LIMIT),
    )(value)


def finish_kernel(meta_ref, *refs, widths, targets, extra):
    pieces, refs = refs[:4], refs[4 + extra:]
    outs, held, sem = refs[:len(widths)], refs[-2], refs[-1]
    rows = held.shape[0] // 4
    for index, piece in enumerate(pieces):
        place = meta_ref[7] ^ index
        spot = (place & 1) * 2 + (place >> 1)
        pltpu.make_async_copy(
            piece, held.at[pl.ds(pl.multiple_of(spot * rows, rows), rows)], sem
        ).start()
    for index, piece in enumerate(pieces):
        pltpu.make_async_copy(piece, held.at[pl.ds(index * rows, rows)], sem).wait()
    total = sum(widths)
    for i, (width, flip) in enumerate(zip(widths, targets)):
        start = sum(widths[:i])
        value = jnp.concatenate(
            [held[pl.ds(s * total + start, width)] for s in range(16)], axis=0
        )
        outs[i][...] = (value.T if flip else value).astype(F32)


def finish(meta, pieces, widths, flips, shapes, specs, more=(), alias=None):
    rows = pieces[0].shape[0]
    return pl.pallas_call(
        functools.partial(finish_kernel, widths=widths, targets=flips, extra=len(more)),
        out_shape=tuple(sds(shape, F32) for shape in shapes),
        grid_spec=pltpu.PrefetchScalarGridSpec(
            num_scalar_prefetch=1, grid=(1,), in_specs=[ANY] * (4 + len(more)), out_specs=specs,
            scratch_shapes=[pltpu.VMEM((4 * rows, D), BF), pltpu.SemaphoreType.DMA],
        ),
        input_output_aliases=alias or {},
        compiler_params=pltpu.CompilerParams(vmem_limit_bytes=VMEM_LIMIT),
    )(meta, *pieces, *more)


def part_spec(shape, index):
    return pl.BlockSpec(shape, lambda t, *_: index)


def swap_xor(value, mask):
    size = lax.axis_size("dp")
    return lax.ppermute(value, "dp", [(i, i ^ mask) for i in range(size)])


def swap_section(value):
    return lax.ppermute(value, "section", [(0, 1), (1, 0)])


def to_section(value, target):
    return lax.ppermute(value, "section", [(1 - target, target)])


def exchange(value0, value1):
    return swap_section(jnp.where(lax.axis_index("section") == 0, value1, value0))


def low_groups():
    size = lax.axis_size("dp")
    return None if size == 16 else [list(range(i, i + 16)) for i in range(0, size, 16)]


def added(*values):
    total = values[0].astype(F32)
    for value in values[1:]:
        total = total + value.astype(F32)
    return total.astype(BF)


def halves(value, bit):
    half = value.shape[0] // 2
    mine = (lax.axis_index("dp") >> bit) & 1
    return (
        lax.dynamic_slice_in_dim(value, mine * half, half, 0),
        lax.dynamic_slice_in_dim(value, (1 - mine) * half, half, 0),
    )


def half_sum(pair, bit):
    return added(pair[0], swap_xor(pair[1], 1 << bit))


def quarters(value, bit):
    rows = value.shape[0] // 4
    mine = (lax.axis_index("dp") >> bit) & 3
    return tuple(lax.dynamic_slice_in_dim(value, (mine ^ k) * rows, rows, 0) for k in range(4))


def swap_quarters(parts, bit):
    return [swap_xor(parts[k], k << bit) for k in (1, 2, 3)]


def quarter_sum(parts, bit):
    return added(parts[0], *swap_quarters(parts, bit))


def tie(*values):
    return lax.optimization_barrier(values)


def rest_bits():
    return range(4, lax.axis_size("dp").bit_length() - 1)


def reduce_core(halves):
    return added(halves[1], swap_xor(halves[0], 1))


def reduce_rest(value):
    for bit in rest_bits():
        value = half_sum(halves(value, bit), bit)
    return value


def gather_bit(value, bit):
    mine = (lax.axis_index("dp") >> bit) & 1
    other = swap_xor(value, 1 << bit)
    return jnp.where(
        mine == 0,
        jnp.concatenate([value, other], axis=0),
        jnp.concatenate([other, value], axis=0),
    )


def gather_quad(value, bit):
    mine = (lax.axis_index("dp") >> bit) & 3
    got = [value] + [swap_xor(value, k << bit) for k in (1, 2, 3)]
    parts = []
    for p in range(4):
        which = mine ^ p
        part = got[3]
        for k in (2, 1, 0):
            part = jnp.where(which == k, got[k], part)
        parts.append(part)
    return jnp.concatenate(parts, axis=0)


def gather_rest(value):
    for bit in reversed(rest_bits()):
        value = gather_bit(value, bit)
    return value


def spread_pieces(value):
    across = swap_xor(value, 2)
    return value, swap_xor(value, 1), across, swap_xor(across, 1)


def sum_rest(value):
    for bit in rest_bits():
        value = added(value, swap_xor(value, 1 << bit))
    return value


def per_device(
    tokens, cotangent, span_counts, tail_lens, ln1_gain, w_qkv, w_out, ln2_gain, w_up, w_down
):
    section = lax.axis_index("section")
    first = section == 0
    place = lax.axis_index("dp") & 3
    meta = jnp.concatenate([
        lax.dynamic_index_in_dim(span_counts, section, 0, keepdims=False),
        lax.dynamic_index_in_dim(tail_lens, section, 0, keepdims=False),
        section.astype(jnp.int32)[None], place.astype(jnp.int32)[None],
    ])
    own = (w_qkv[0], w_out[0], w_up[0], w_down[0])

    def part(weight, spot, count):
        rows = weight.shape[0] // count
        return lax.dynamic_slice_in_dim(weight, spot * rows, rows, 0)

    own_gains = jnp.concatenate([ln1_gain, ln2_gain], axis=0)
    other_gains = swap_section(own_gains)
    attn = [
        part(own[0][:, :2 * D], place, 4),
        jnp.concatenate([part(own[0][:, 2 * D:], place, 4), part(own[1], place, 4)], axis=1),
    ]
    attn = [swap_section(value) for value in attn]
    late = part(own[2], place, 4), part(own[3], place & 1, 2)
    attn[1], other_gains, late = tie(attn[1], other_gains, late)
    up, down = swap_section(late[0]), swap_section(late[1])
    gains = [jnp.where(first, own_gains, other_gains), jnp.where(first, other_gains, own_gains)]
    attn_x = [swap_xor(value, 2) for value in attn]
    front, rest = [(v, swap_xor(v, 1), x, swap_xor(x, 1)) for v, x in zip(attn, attn_x)]
    wqkv = Weight(own[0], (front, 0, 0, 2 * D), (rest, 0, 2 * D, D))
    wout = Weight(own[1], (rest, D, 0, D))
    up_x, up_c = swap_xor(up, 2), swap_xor(up, 1)

    keep0, hidden, second = forward_attn(meta, tokens, gains[0], wqkv, wout, 0)
    keep0, hidden, second, up_x, up_c, down = tie(keep0, hidden, second, up_x, up_c, down)
    wup = Weight(own[2], ((up, up_c, up_x, swap_xor(up_x, 1)), 0, 0, None))
    wdown = Weight(own[3], ((down, swap_xor(down, 1)), 0, 0, None))
    act_out0, act0, gp0 = forward_mlp(meta, hidden, second, wup, wdown, 0)
    act_out1, ig1, sums1 = whole_layer(
        meta, act_out0, cotangent, gains[1], wqkv, wout, wup, wdown, 1
    )
    cut = 2 * MB_TOK // 3
    acts_a = exchange(act_out0[:cut], act_out1[:cut])
    sums1 = lax.psum_scatter(
        sums1.reshape(-1, D), "dp", scatter_dimension=0, axis_index_groups=low_groups(), tiled=True
    )
    xh1, r1, qkv, krow, vrow, lse, att, xh2, r2, ks, vs = keep0
    back = mlp_back(meta, ig1, act0, gp0, xh2, r2, att, gains[0], wdown, wup, wout, 0)
    (send, kept, gln2, gh, gatt), acts_a, act_out0, act_out1 = tie(back, acts_a, act_out0, act_out1)
    mlp0 = added(kept, swap_xor(send, 1))
    a0, b0 = halves(mlp0[:8 * PART_A], 1), quarters(mlp0[8 * PART_A:], 2)
    gh, a0, b0 = tie(gh, a0, b0)
    acts_b = exchange(act_out0[cut:], act_out1[cut:])
    a0_x, b0_z = swap_xor(a0[1], 2), swap_quarters(b0, 2)
    back = attn_back(
        meta, gh, gatt, xh1, r1, qkv, krow, vrow, lse, ks, vs, gains[0], gln2, wqkv, 0
    )
    (ig0, send, kept), a0_x, b0_z, acts_b = tie(back, a0_x, b0_z, acts_b)
    acts_in = jnp.concatenate([acts_a, acts_b], axis=0)
    grads_in = exchange(ig0, ig1)
    c0 = swap_xor(send, 1)
    a0 = quarters(added(a0[0], a0_x), 2)
    a0, c0 = tie(a0, c0)
    a0_z = swap_quarters(a0, 2)
    c0 = halves(added(kept, c0), 1)
    b0 = halves(added(b0[0], *b0_z), 1)
    bc0_x = swap_xor(jnp.concatenate([b0[1], c0[1]], axis=0), 2)

    def own_sum(grad0, grad1):
        return added(jnp.where(first, grad0, grad1), swap_section(jnp.where(first, grad1, grad0)))

    b0 = added(b0[0], bc0_x[:PART_B])
    c0 = quarters(added(c0[0], bc0_x[PART_B:]), 2)
    c0_z = swap_quarters(c0, 2)
    a0_z, b0, c0_1, grads_in = tie(a0_z, b0, c0[1], grads_in)
    a0 = added(a0[0], *a0_z)
    spots = (0, PART_A, PART_A + PART_B, PART_A + PART_B + QKV_ROWS)
    a1, b1, c1, gains1 = [sums1[i:j] for i, j in zip(spots, spots[1:] + (sums1.shape[0],))]
    ab = own_sum(
        jnp.concatenate([reduce_rest(a0), reduce_rest(b0)], axis=0),
        jnp.concatenate([reduce_rest(a1), reduce_rest(b1)], axis=0),
    )
    a_rows = ab.shape[0] * PART_A // (PART_A + PART_B)
    a_full = lax.all_gather(
        gather_rest(ab[:a_rows]), "dp", axis=0, axis_index_groups=low_groups(), tiled=True
    )
    c0 = added(c0[0], *c0_z)
    c_own = own_sum(
        jnp.concatenate([reduce_rest(c0[:QKV_ROWS]), sum_rest(c0[QKV_ROWS:])], axis=0),
        jnp.concatenate([reduce_rest(c1), sum_rest(gains1)], axis=0),
    )
    lns = c_own[-GAIN_ROWS:][:2].astype(F32)
    bc_own = jnp.concatenate([gather_rest(ab[a_rows:]), gather_rest(c_own[:-GAIN_ROWS])], axis=0)
    bc_pieces = spread_pieces(gather_quad(bc_own, 2))
    grad_down, grad_up, grad_out = finish_whole(
        a_full, (DOWN_ROWS, UP_A // 16, OUT_ROWS), (False, True, False),
        [(FF, D), (D, FF), (D, D)],
        [
            part_spec((FF, D), (0, 0)), part_spec((D, UP_A), (0, UP_B // UP_A)),
            part_spec((D, D), (0, 0)),
        ],
    )
    grad_up, grad_qkv = finish(
        meta, bc_pieces, (UP_B // 16, QKV_ROWS), (True, True), [(D, FF), (D, 3 * D)],
        [part_spec((D, UP_B), (0, 0)), part_spec((D, 3 * D), (0, 0))],
        (grad_up,), {5: 0},
    )

    def assemble(value0, value1, got):
        return jnp.concatenate(
            [jnp.where(first, value0, got), jnp.where(first, got, value1)], axis=0
        )

    activations = assemble(act_out0, act_out1, acts_in)
    input_grads = assemble(ig0, ig1, grads_in)
    return (
        activations[None],
        input_grads[None],
        lns[:1],
        grad_qkv[None],
        grad_out[None],
        lns[1:],
        grad_up[None],
        grad_down[None],
    )


def solution(mesh):
    return jax.shard_map(
        per_device,
        mesh=mesh,
        in_specs=(
            P("dp", None),
            P("dp", None),
            P("dp", None),
            P("dp", None),
            P("section", None),
            P("section", None, None),
            P("section", None, None),
            P("section", None),
            P("section", None, None),
            P("section", None, None),
        ),
        out_specs=(
            P("section", "dp", None),
            P("section", "dp", None),
            P("section", None),
            P("section", None, None),
            P("section", None, None),
            P("section", None),
            P("section", None, None),
            P("section", None, None),
        ),
        check_vma=False,
    )
```

```python
import functools

import jax
import jax.numpy as jnp
from jax import lax
from jax.experimental import pallas as pl
from jax.experimental.pallas import tpu as pltpu
from jax.sharding import PartitionSpec as P

D = 512
HEADS = 8
HEAD_DIM = 64
FF = 2048
SPAN = 128
MB_BLK = 12
MB_TOK = MB_BLK * SPAN
PAD_BLK = 16
EPSILON = 1e-05
NEG_FILL = -1e30
BF = jnp.bfloat16
F32 = jnp.float32
VMEM_LIMIT = 58 * 2**20

TILE = 512
TILE_BLK = TILE // SPAN
N_TILE = MB_TOK // TILE
FF_STEP = 512
FWD_STEP = 512
FWD_GROUP = 2
BACK_GROUP = 2


def dot(left, right, left_dim, right_dim):
    return lax.dot_general(
        left, right, (((left_dim,), (right_dim,)), ((), ())), preferred_element_type=F32
    )


def block_facts(meta_ref, block):
    end_one = meta_ref[0]
    end_two = end_one + meta_ref[1]
    in_one = block < end_one
    in_two = block < end_two
    first = jnp.where(in_one, 0, jnp.where(in_two, end_one, end_two))
    last = jnp.where(in_one, end_one, jnp.where(in_two, end_two, MB_BLK)) - 1
    tail = jnp.where(in_one, meta_ref[3], jnp.where(in_two, meta_ref[4], meta_ref[5]))
    filled = jnp.where(block == last, tail, SPAN)
    return filled, first


def filled_column(meta_ref, width):
    rows = lax.broadcasted_iota(jnp.int32, (PAD_BLK, width), 0)
    out = jnp.full((PAD_BLK, width), SPAN, jnp.int32)
    for block in range(MB_BLK):
        filled, _ = block_facts(meta_ref, block)
        out = jnp.where(rows == block, filled, out)
    return out.astype(F32)


def filled_row(meta_ref):
    cols = lax.broadcasted_iota(jnp.int32, (1, PAD_BLK), 1)
    out = jnp.full((1, PAD_BLK), SPAN, jnp.int32)
    for block in range(MB_BLK):
        filled, _ = block_facts(meta_ref, block)
        out = jnp.where(cols == block, filled, out)
    return out.astype(F32)


def member_mask(meta_ref, tile_start):
    parts = []
    rows = lax.broadcasted_iota(jnp.int32, (PAD_BLK, SPAN), 0)
    cols = lax.broadcasted_iota(jnp.int32, (PAD_BLK, SPAN), 1)
    for j in range(TILE_BLK):
        block = tile_start + j
        filled, _ = block_facts(meta_ref, block)
        parts.append(jnp.where((rows == block) & (cols < filled), 1.0, 0.0).astype(BF))
    return jnp.concatenate(parts, axis=1)


def pair_diag(rows_two):
    zero = jnp.zeros((HEAD_DIM, SPAN), rows_two.dtype)
    top = jnp.concatenate([rows_two[:HEAD_DIM], zero], axis=1)
    low = jnp.concatenate([zero, rows_two[HEAD_DIM:]], axis=1)
    return jnp.concatenate([top, low], axis=0)


def diag_rows(square):
    return jnp.concatenate([square[:HEAD_DIM, :SPAN], square[HEAD_DIM:, SPAN:]], axis=0)


def gain_column(gains_ref, index):
    return jnp.broadcast_to(gains_ref[index:index + 1], (SPAN, D)).T


def times_gain(values, gain):
    return jnp.concatenate(
        [values[:, i * SPAN:(i + 1) * SPAN] * gain for i in range(values.shape[1] // SPAN)], axis=1
    )


def normalize(values):
    mean = jnp.sum(values, axis=0, keepdims=True) * (1.0 / D)
    center = values - mean
    spread = jnp.sum(center * center, axis=0, keepdims=True) * (1.0 / D)
    factor = lax.rsqrt(spread + EPSILON)
    return center * factor, factor


def score_mask(block, filled, first):
    rows = lax.broadcasted_iota(jnp.int32, (SPAN + PAD_BLK, 2 * SPAN), 0)
    cols = lax.broadcasted_iota(jnp.int32, (SPAN + PAD_BLK, 2 * SPAN), 1) % SPAN
    local = (rows <= cols) & (rows < filled)
    earlier = (rows >= SPAN + first) & (rows < SPAN + block)
    return local | earlier


def attention_items(meta_ref, tile_start, blocks):
    items = []
    for j in blocks:
        filled, first = block_facts(meta_ref, tile_start + j)
        mask = score_mask(tile_start + j, filled, first)
        for hp in range(HEADS // 2):
            items.append((slice(j * SPAN, (j + 1) * SPAN), hp, slice(hp * SPAN, (hp + 1) * SPAN), mask))
    return items


class Weight:
    def __init__(self, own, *groups):
        self.own = own
        self.groups = [(tuple(p), lane, at, width or own.shape[1]) for p, lane, at, width in groups]

    def flat(self):
        return (self.own,) + sum((group[0] for group in self.groups), ())

    def bind(self, refs):
        own, refs, groups = refs[0], refs[1:], []
        for pieces, *rest in self.groups:
            groups.append((refs[:len(pieces)], *rest))
            refs = refs[len(pieces):]
        return Weight(own, *groups), refs


def start_weight(meta_ref, layer, weight, target, sem):
    @pl.when(meta_ref[6] == layer)
    def _():
        pltpu.make_async_copy(weight.own, target, sem).start()

    @pl.when(meta_ref[6] != layer)
    def _():
        for pieces, lane, at, width in weight.groups:
            count = len(pieces)
            rows = target.shape[0] // count
            for index, piece in enumerate(pieces):
                spot = (meta_ref[7] & (count - 1)) ^ index
                pltpu.make_async_copy(
                    piece.at[:, pl.ds(lane, width)],
                    target.at[pl.ds(pl.multiple_of(spot * rows, rows), rows), pl.ds(at, width)], sem,
                ).start()


def wait_weight(weight, target, sem):
    pltpu.make_async_copy(weight.own, target, sem).wait()


def forward_attn_part(meta_ref, tile, x_ref, gains_ref, outs, scratch, wqkv_ref, wout_ref, wait):
    (xh1_ref, r1_ref, qkv_ref, krow_ref, vrow_ref, lse_ref, att_ref, xh2_ref, r2_ref, ks_ref,
     vs_ref) = outs
    (attf_ref,) = scratch
    tile_start = tile * TILE_BLK

    @pl.when(tile == 0)
    def _():
        ks_ref[...] = jnp.zeros_like(ks_ref)
        vs_ref[...] = jnp.zeros_like(vs_ref)

    x_t = x_ref[...].T.astype(F32)
    xhat, r1 = normalize(x_t)
    xh1_ref[...] = xhat.astype(BF)
    r1_ref[...] = r1
    normed = times_gain(xhat, gain_column(gains_ref, 0)).astype(BF)
    wait(0)
    q_t = (dot(wqkv_ref[:, :D], normed, 0, 0) * HEAD_DIM ** (-0.5)).astype(BF)
    k_t = dot(wqkv_ref[:, D:2 * D], normed, 0, 0).astype(BF)
    v_t = dot(wqkv_ref[:, 2 * D:], normed, 0, 0).astype(BF)
    qkv_ref[:D] = q_t
    qkv_ref[D:2 * D] = k_t
    qkv_ref[2 * D:] = v_t
    krow = k_t.T
    vrow = v_t.T
    krow_ref[...] = krow
    vrow_ref[...] = vrow
    members = member_mask(meta_ref, tile_start)
    fill = filled_column(meta_ref, D)
    block_rows = lax.broadcasted_iota(jnp.int32, (PAD_BLK, D), 0)
    fresh = (block_rows >= tile_start) & (block_rows < tile_start + TILE_BLK)
    key_sums = jnp.where(fresh, (dot(members, krow, 1, 0) / fill).astype(BF), ks_ref[...])
    value_sums = jnp.where(fresh, (dot(members, vrow, 1, 0) / fill).astype(BF), vs_ref[...])
    ks_ref[...] = key_sums
    vs_ref[...] = value_sums
    vs_t = value_sums.T
    for j in range(0, TILE_BLK, FWD_GROUP):
        items = attention_items(meta_ref, tile_start, range(j, j + FWD_GROUP))
        scores = [
            dot(
                jnp.concatenate([krow[cols, feats], key_sums[:, feats]], axis=0),
                pair_diag(q_t[feats, cols]), 1, 0,
            )
            for cols, _, feats, _ in items
        ]
        probs = []
        for (cols, hp, feats, mask), score in zip(items, scores):
            score = jnp.where(mask, score, NEG_FILL)
            top = jnp.max(score, axis=0, keepdims=True)
            prob = jnp.exp(score - top)
            total = jnp.sum(prob, axis=0, keepdims=True)
            logs = top + jnp.log(total)
            lse_ref[2 * hp:2 * hp + 1, cols] = logs[:, :SPAN]
            lse_ref[2 * hp + 1:2 * hp + 2, cols] = logs[:, SPAN:]
            probs.append((prob * (1.0 / total)).astype(BF))
        for (cols, _, feats, _), prob in zip(items, probs):
            values = jnp.concatenate([v_t[feats, cols], vs_t[feats]], axis=1)
            attf_ref[feats, cols] = diag_rows(dot(values, prob, 1, 0)).astype(BF)
    att = attf_ref[...]
    att_ref[...] = att
    wait(1)
    hidden = x_t + dot(wout_ref[...], att, 0, 0)
    xhat2, r2 = normalize(hidden)
    xh2_ref[...] = xhat2.astype(BF)
    r2_ref[...] = r2
    return hidden, times_gain(xhat2, gain_column(gains_ref, 1)).astype(BF)


def forward_mlp_part(hidden, second, outs, wup_ref, wdown_ref):
    out_ref, act_ref, gp_ref = outs
    total_out = hidden
    up = dot(wup_ref[:, :FWD_STEP], second, 0, 0)
    for f in range(FF // FWD_STEP):
        part = slice(f * FWD_STEP, (f + 1) * FWD_STEP)
        later = slice((f + 1) * FWD_STEP, (f + 2) * FWD_STEP)
        ahead = dot(wup_ref[:, later], second, 0, 0) if later.stop <= FF else None
        bell = jnp.exp(up * up * -0.5)
        phi = 0.5 + 0.5 * lax.erf(up * (0.5 ** 0.5))
        act = (up * phi).astype(BF)
        act_ref[part] = act
        gp_ref[part] = (phi + up * bell * 0.3989422804014327).astype(BF)
        total_out = total_out + dot(wdown_ref[part], act, 0, 0)
        up = ahead
    out_ref[...] = total_out.astype(BF).T


def weight_waits(meta_ref, layer, weights, targets, sems):
    begin = pl.program_id(0) == 0

    @pl.when(begin)
    def _():
        for i, (weight, target) in enumerate(zip(weights, targets)):
            start_weight(meta_ref, layer, weight, target, sems.at[i])

    def wait(i):
        @pl.when(begin)
        def _():
            wait_weight(weights[i], targets[i], sems.at[i])

    return wait


def bound(weights, refs):
    out = []
    for weight in weights:
        weight, refs = weight.bind(refs)
        out.append(weight)
    return out, refs


def forward_attn_kernel(meta_ref, x_ref, gains_ref, *refs, layer, weights):
    weights, refs = bound(weights, refs)
    attn_outs, (hid_ref, sec_ref), scratch, targets, sems = (
        refs[:11], refs[11:13], refs[13:14], refs[14:16], refs[16]
    )
    wait = weight_waits(meta_ref, layer, weights, targets, sems)
    hidden, second = forward_attn_part(
        meta_ref, pl.program_id(0), x_ref, gains_ref, attn_outs, scratch, targets[0], targets[1], wait
    )
    hid_ref[...] = hidden
    sec_ref[...] = second


def forward_mlp_kernel(meta_ref, hid_ref, sec_ref, *refs, layer, weights):
    weights, refs = bound(weights, refs)
    outs, targets, sems = refs[:3], refs[3:5], refs[5]
    wait = weight_waits(meta_ref, layer, weights, targets, sems)
    wait(0)
    wait(1)
    forward_mlp_part(hid_ref[...], sec_ref[...], outs, *targets)


def write_halves(meta_ref, parts, send_ref, keep_ref, start=0, z_first=False):
    core = meta_ref[7] & 1
    total = sum(rows for _, _, rows in parts)
    for target, side in ((send_ref, 1 - core), (keep_ref, core)):
        for s in range(8):
            spot = start + ((s % 4) * 2 + s // 4 if z_first else s) * total
            for acc, base, rows in parts:
                if acc.shape[0] == rows:
                    value = acc[...]
                else:
                    first = base + pl.multiple_of(side * (8 * rows), 8 * rows) + s * rows
                    value = acc[pl.ds(first, rows)]
                target[pl.ds(spot, rows)] = value.astype(BF)
                spot += rows


def write_shards(parts, target):
    for place in range(16):
        s = (place & 1) * 8 + ((place >> 1) & 1) * 4 + (place >> 2)
        spot = 0
        for acc, base, rows in parts:
            value = acc[...] if acc.shape[0] == rows else acc[pl.ds(base + s * rows, rows)]
            target[place, pl.ds(spot, rows)] = value.astype(BF)
            spot += rows


DOWN_ROWS, OUT_ROWS, QKV_ROWS, GAIN_ROWS = FF // 16, D // 16, 3 * D // 16, 16
UP_A = FF // 2
UP_B = FF - UP_A
PART_A, PART_B = DOWN_ROWS + UP_A // 16 + OUT_ROWS, UP_B // 16
PART_C = QKV_ROWS + GAIN_ROWS


def norm_back(grad, gain, xhat, factor, gln_acc):
    prod = grad * xhat
    for j in range(TILE_BLK):
        gln_acc[...] += prod[:, j * SPAN:(j + 1) * SPAN]
    scaled = times_gain(grad, gain)
    mean = jnp.sum(scaled, axis=0, keepdims=True) * (1.0 / D)
    mean_x = jnp.sum(scaled * xhat, axis=0, keepdims=True) * (1.0 / D)
    return factor * (scaled - mean - xhat * mean_x)


def masked_low(meta_ref, tile, low):
    parts = []
    cols = lax.broadcasted_iota(jnp.int32, (D, SPAN), 1)
    for j in range(TILE_BLK):
        filled, _ = block_facts(meta_ref, tile * TILE_BLK + j)
        part = low[:, j * SPAN:(j + 1) * SPAN]
        parts.append(jnp.where(cols < filled, part, jnp.zeros((), BF)))
    return jnp.concatenate(parts, axis=1)


def zero_all(refs):
    for ref in refs:
        ref[...] = jnp.zeros_like(ref)


def mlp_back_part(low, data, gains_ref, weights, accs, wait, gh_ref, gatt_ref):
    act_ref, gp_ref, xh2_ref, r2_ref, att_ref = data
    wdown_ref, wup_ref, wout_ref = weights
    gdown_acc, gup_acc, gout_acc, gln_acc = accs
    gain = gain_column(gains_ref, 1)
    xhat = xh2_ref[...].astype(F32)
    second = times_gain(xhat, gain).astype(BF)
    wait(0)
    wait(1)
    e = None
    for f in range(FF // FF_STEP):
        part = slice(f * FF_STEP, (f + 1) * FF_STEP)
        gdown_acc[part] += dot(act_ref[part], low, 1, 1)
        ga = dot(wdown_ref[part], low, 1, 0)
        gui = (ga * gp_ref[part].astype(F32)).astype(BF)
        gup_acc[part] += dot(gui, second, 1, 1)
        term = dot(wup_ref[:, part], gui, 1, 0)
        e = term if e is None else e + term
    gh = low.astype(F32) + norm_back(e, gain, xhat, r2_ref[...], gln_acc)
    gh_ref[...] = gh
    ghb = gh.astype(BF)
    gout_acc[...] += dot(att_ref[...], ghb, 1, 1)
    wait(2)
    gatt_ref[...] = dot(wout_ref[...], ghb, 1, 0).astype(BF)


def mlp_parts(gdown_acc, gup_acc, gout_acc):
    part_a = ((gdown_acc, 0, DOWN_ROWS), (gup_acc, UP_B, UP_A // 16), (gout_acc, 0, OUT_ROWS))
    return part_a, ((gup_acc, 0, UP_B // 16),)


def mlp_back_kernel(
    meta_ref, seed_ref, act_ref, gp_ref, xh2_ref, r2_ref, att_ref, gains_ref, *refs, layer, weights,
):
    weights, refs = bound(weights, refs)
    (send_ref, keep_ref, gln_ref, gh_ref, gatt_ref, gdown_acc, gup_acc, gout_acc, gln_acc,
     wdown_ref, wup_ref, wout_ref, sems) = refs
    step = pl.program_id(0)
    targets = (wdown_ref, wup_ref, wout_ref)
    accs = (gdown_acc, gup_acc, gout_acc, gln_acc)
    wait = weight_waits(meta_ref, layer, weights, targets, sems)

    @pl.when(step == 0)
    def _():
        zero_all(accs)

    mlp_back_part(
        seed_ref[...].T, (act_ref, gp_ref, xh2_ref, r2_ref, att_ref), gains_ref, targets, accs, wait,
        gh_ref, gatt_ref,
    )

    @pl.when(step == N_TILE - 1)
    def _():
        part_a, part_b = mlp_parts(*accs[:3])
        write_halves(meta_ref, part_a, send_ref, keep_ref)
        write_halves(meta_ref, part_b, send_ref, keep_ref, 8 * PART_A, True)
        gln_ref[...] = jnp.sum(gln_acc[...].T, axis=0, keepdims=True)


def attn_back_part(meta_ref, tile, gh_ref, gatt_ref, data, gains_ref, wqkv_ref, accs, rows_ref, wait):
    xh1_ref, r1_ref, qkv_ref, krow_ref, vrow_ref, lse_ref, ks_ref, vs_ref = data
    gqkv_acc, gln_acc, gks_acc, gvs_acc = accs
    tile_start = tile * TILE_BLK
    q_t = qkv_ref[:D]
    gatt = gatt_ref[...]
    key_sums, value_sums = ks_ref[...], vs_ref[...]
    ks_t = key_sums.T
    for j in range(0, TILE_BLK, BACK_GROUP):
        items = attention_items(meta_ref, tile_start, range(j, j + BACK_GROUP))
        q_diags = [pair_diag(q_t[feats, cols]) for cols, _, feats, _ in items]
        g_diags = [pair_diag(gatt[feats, cols]) for cols, _, feats, _ in items]
        scores = [
            dot(jnp.concatenate([krow_ref[cols, feats], key_sums[:, feats]], axis=0), q, 1, 0)
            for (cols, _, feats, _), q in zip(items, q_diags)
        ]
        dps = [
            dot(jnp.concatenate([vrow_ref[cols, feats], value_sums[:, feats]], axis=0), g, 1, 0)
            for (cols, _, feats, _), g in zip(items, g_diags)
        ]
        grads, probs = [], []
        for (cols, hp, feats, mask), score, dp in zip(items, scores, dps):
            logs = jnp.concatenate(
                [lse_ref[2 * hp:2 * hp + 1, cols], lse_ref[2 * hp + 1:2 * hp + 2, cols]], axis=1
            )
            prob = jnp.exp(jnp.where(mask, score, NEG_FILL) - logs)
            weighted = prob * dp
            delta = jnp.sum(weighted, axis=0, keepdims=True)
            grads.append((weighted - prob * delta).astype(BF))
            probs.append(prob.astype(BF))
        for (cols, hp, feats, _), grad, prob, q, g in zip(items, grads, probs, q_diags, g_diags):
            key_feats = slice(D + hp * SPAN, D + (hp + 1) * SPAN)
            value_feats = slice(2 * D + hp * SPAN, 2 * D + (hp + 1) * SPAN)
            keys = jnp.concatenate([qkv_ref[key_feats, cols], ks_t[feats]], axis=1)
            rows_ref[feats, cols] = diag_rows(dot(keys, grad, 1, 0))
            key_grad = dot(q, grad, 1, 1)
            value_grad = dot(g, prob, 1, 1)
            rows_ref[key_feats, cols] = key_grad[:, :SPAN]
            rows_ref[value_feats, cols] = value_grad[:, :SPAN]
            gks_acc[feats] += key_grad[:, SPAN:]
            gvs_acc[feats] += value_grad[:, SPAN:]
    members = member_mask(meta_ref, tile_start)
    fill = filled_row(meta_ref)

    def spread_back(acc_ref):
        back = (acc_ref[...].astype(BF).astype(F32) / fill).astype(BF)
        return dot(back, members, 1, 0)

    grad_q = rows_ref[:D] * HEAD_DIM ** (-0.5)
    grad_k = rows_ref[D:2 * D] + spread_back(gks_acc)
    grad_v = rows_ref[2 * D:] + spread_back(gvs_acc)
    gain = gain_column(gains_ref, 0)
    xhat = xh1_ref[...].astype(F32)
    normed = times_gain(xhat, gain).astype(BF)
    wait(0)
    e = None
    for i, rows in enumerate((grad_q, grad_k, grad_v)):
        rows = rows.astype(BF)
        part = slice(i * D, (i + 1) * D)
        gqkv_acc[part] += dot(rows, normed, 1, 1)
        term = dot(wqkv_ref[:, part], rows, 1, 0)
        e = term if e is None else e + term
    return (gh_ref[...] + norm_back(e, gain, xhat, r1_ref[...], gln_acc)).astype(BF).T


def gain_rows(gln_acc, gln2):
    gln = jnp.sum(gln_acc[...].T, axis=0, keepdims=True)
    rest = jnp.zeros((GAIN_ROWS - 2, D), F32)
    return jnp.concatenate([gln, gln2, rest], axis=0).astype(BF)


def attn_back_kernel(
    meta_ref, gh_ref, gatt_ref, xh1_ref, r1_ref, qkv_ref, krow_ref, vrow_ref, lse_ref, ks_ref,
    vs_ref, gains_ref, gln2_ref, *refs, layer, weights,
):
    weights, refs = bound(weights, refs)
    (gin_ref, send_ref, keep_ref, gqkv_acc, gln_acc, gks_acc, gvs_acc, rows_ref, wqkv_ref,
     sems) = refs
    step = pl.program_id(0)
    wait = weight_waits(meta_ref, layer, weights, (wqkv_ref,), sems)
    accs = (gqkv_acc, gln_acc, gks_acc, gvs_acc)

    @pl.when(step == 0)
    def _():
        zero_all(accs)

    data = (xh1_ref, r1_ref, qkv_ref, krow_ref, vrow_ref, lse_ref, ks_ref, vs_ref)
    gin_ref[...] = attn_back_part(
        meta_ref, N_TILE - 1 - step, gh_ref, gatt_ref, data, gains_ref, wqkv_ref, accs, rows_ref, wait
    )

    @pl.when(step == N_TILE - 1)
    def _():
        parts = ((gqkv_acc, 0, QKV_ROWS), (gain_rows(gln_acc, gln2_ref[...]), 0, GAIN_ROWS))
        write_halves(meta_ref, parts, send_ref, keep_ref)


def layer_kernel(meta_ref, x_ref, cot_ref, gains_ref, *refs, layer, weights):
    weights, refs = bound(weights, refs)
    out_ref, gin_ref, sums_ref, *refs = refs
    keep, refs = refs[:13], refs[13:]
    (xh1, r1, qkv, krow, vrow, lse, att_ref, xh2_ref, r2_ref, ks_ref, vs_ref, gh, gatt) = keep
    act_ref, gp_ref, attf_ref, rows_ref, *refs = refs
    mlp_accs, attn_accs, refs = refs[:4], refs[4:8], refs[8:]
    held_mlp, held_qkv, *refs = refs
    targets, sems, copies = refs[:4], refs[4], refs[5]
    wqkv_ref, wout_ref, wup_ref, wdown_ref = targets
    step = pl.program_id(0)
    wait = weight_waits(meta_ref, layer, weights, targets, sems)
    mlp_rows = PART_A + PART_B
    mlp_copy = pltpu.make_async_copy(held_mlp, sums_ref.at[:, pl.ds(0, mlp_rows)], copies.at[0])
    qkv_copy = pltpu.make_async_copy(held_qkv, sums_ref.at[:, pl.ds(mlp_rows, PART_C)], copies.at[1])

    @pl.when(step == 0)
    def _():
        zero_all(mlp_accs)
        zero_all(attn_accs)

    @pl.when(step < N_TILE)
    def _():
        tile = step
        outs = (
            xh1.at[tile], r1.at[tile], qkv.at[tile], krow.at[tile], vrow.at[tile], lse.at[tile],
            att_ref, xh2_ref, r2_ref, ks_ref, vs_ref,
        )
        hidden, second = forward_attn_part(
            meta_ref, tile, x_ref, gains_ref, outs, (attf_ref,), wqkv_ref, wout_ref, wait
        )
        wait(2)
        wait(3)
        forward_mlp_part(hidden, second, (out_ref, act_ref, gp_ref), wup_ref, wdown_ref)
        mlp_back_part(
            masked_low(meta_ref, tile, cot_ref[...].T), (act_ref, gp_ref, xh2_ref, r2_ref, att_ref),
            gains_ref, (wdown_ref, wup_ref, wout_ref), mlp_accs, lambda i: None, gh.at[tile],
            gatt.at[tile],
        )

    @pl.when(step == N_TILE)
    def _():
        part_a, part_b = mlp_parts(*mlp_accs[:3])
        write_shards(part_a + part_b, held_mlp)
        mlp_copy.start()

    @pl.when(step >= N_TILE)
    def _():
        tile = 2 * N_TILE - 1 - step
        data = (
            xh1.at[tile], r1.at[tile], qkv.at[tile], krow.at[tile], vrow.at[tile], lse.at[tile],
            ks_ref, vs_ref,
        )
        gin_ref[...] = attn_back_part(
            meta_ref, tile, gh.at[tile], gatt.at[tile], data, gains_ref, wqkv_ref, attn_accs,
            rows_ref, lambda i: None,
        )

    @pl.when(step == 2 * N_TILE - 1)
    def _():
        gln2 = jnp.sum(mlp_accs[3][...].T, axis=0, keepdims=True)
        parts = (
            (attn_accs[0], 0, QKV_ROWS), (gain_rows(attn_accs[1], gln2), 0, GAIN_ROWS)
        )
        write_shards(parts, held_qkv)
        qkv_copy.start()
        mlp_copy.wait()
        qkv_copy.wait()


ANY = pl.BlockSpec(memory_space=pl.ANY)
sds = jax.ShapeDtypeStruct


def whole(shape):
    return pl.BlockSpec(shape, lambda t, *_: (0,) * len(shape), pipeline_mode=pl.Buffered(1))


def rows_spec(width):
    return pl.BlockSpec((TILE, width), lambda t, *_: (t, 0))


def cols_spec(height):
    return pl.BlockSpec((height, TILE), lambda t, *_: (0, t))


def rev_rows(width):
    return pl.BlockSpec((TILE, width), lambda t, *_: (N_TILE - 1 - t, 0))


def rev_cols(height):
    return pl.BlockSpec((height, TILE), lambda t, *_: (0, N_TILE - 1 - t))


def call(kernel, grid, outs, in_specs, out_specs, scratch, args):
    return pl.pallas_call(
        kernel,
        out_shape=tuple(outs),
        grid_spec=pltpu.PrefetchScalarGridSpec(
            num_scalar_prefetch=1, grid=grid, in_specs=in_specs, out_specs=out_specs,
            scratch_shapes=scratch,
        ),
        cost_estimate=pl.CostEstimate(flops=0, bytes_accessed=0, transcendentals=0),
        compiler_params=pltpu.CompilerParams(vmem_limit_bytes=VMEM_LIMIT),
    )(*args)


def col(height, kind=BF):
    return sds((height, MB_TOK), kind)


def attn_outputs():
    shapes = [
        col(D), col(1, F32), col(3 * D), sds((MB_TOK, D), BF), sds((MB_TOK, D), BF),
        col(HEADS, F32), col(D), col(D), col(1, F32), sds((PAD_BLK, D), BF), sds((PAD_BLK, D), BF),
    ]
    specs = [
        cols_spec(D), cols_spec(1), cols_spec(3 * D), rows_spec(D), rows_spec(D), cols_spec(HEADS),
        cols_spec(D), cols_spec(D), cols_spec(1), whole((PAD_BLK, D)), whole((PAD_BLK, D)),
    ]
    return shapes, specs


MLP_OUTS = ([sds((MB_TOK, D), BF), col(FF), col(FF)], [(D, 0), (FF, 1), (FF, 1)])


def weight_scratch(*weights):
    return [pltpu.VMEM(w.own.shape, BF) for w in weights] + [
        pltpu.SemaphoreType.DMA((len(weights),))
    ]


def flat(weights):
    return [ref for weight in weights for ref in weight.flat()]


def attn_scratch():
    return [pltpu.VMEM((D, TILE), BF)]


def forward_attn(meta, x, gains, wqkv, wout, layer):
    shapes, specs = attn_outputs()
    weights = (wqkv, wout)
    out = call(
        functools.partial(forward_attn_kernel, layer=layer, weights=weights), (N_TILE,),
        shapes + [col(D, F32), col(D)],
        [
            pl.BlockSpec((TILE, D), lambda t, m: (m[6] * N_TILE + t, 0)), whole((2, D)),
        ] + [ANY] * len(flat(weights)),
        specs + [cols_spec(D), cols_spec(D)],
        attn_scratch() + weight_scratch(*weights),
        (meta, x, gains, *flat(weights)),
    )
    return out[:11], out[11], out[12]


def forward_mlp(meta, hidden, second, wup, wdown, layer):
    weights = (wup, wdown)
    return call(
        functools.partial(forward_mlp_kernel, layer=layer, weights=weights), (N_TILE,),
        MLP_OUTS[0],
        [cols_spec(D), cols_spec(D)] + [ANY] * len(flat(weights)),
        [rows_spec(D), cols_spec(FF), cols_spec(FF)],
        weight_scratch(*weights),
        (meta, hidden, second, *flat(weights)),
    )


def mlp_scratch():
    return [
        pltpu.VMEM((FF, D), F32), pltpu.VMEM((FF, D), F32), pltpu.VMEM((D, D), F32),
        pltpu.VMEM((D, SPAN), F32),
    ]


def attn_back_scratch():
    return [
        pltpu.VMEM((3 * D, D), F32), pltpu.VMEM((D, SPAN), F32), pltpu.VMEM((D, PAD_BLK), F32),
        pltpu.VMEM((D, PAD_BLK), F32),
    ]


def mlp_back(meta, seed, act, gp, xh2, r2, att, gains, wdown, wup, wout, layer):
    weights = (wdown, wup, wout)
    half = 8 * (PART_A + PART_B)
    return call(
        functools.partial(mlp_back_kernel, layer=layer, weights=weights), (N_TILE,),
        [sds((half, D), BF), sds((half, D), BF), sds((1, D), F32), col(D, F32), col(D)],
        [
            rev_rows(D), rev_cols(FF), rev_cols(FF), rev_cols(D), rev_cols(1), rev_cols(D),
            whole((2, D)),
        ] + [ANY] * len(flat(weights)),
        [whole((half, D)), whole((half, D)), whole((1, D)), rev_cols(D), rev_cols(D)],
        mlp_scratch() + weight_scratch(*weights),
        (meta, seed, act, gp, xh2, r2, att, gains, *flat(weights)),
    )


def attn_back(meta, gh, gatt, xh1, r1, qkv, krow, vrow, lse, ks, vs, gains, gln2, wqkv, layer):
    half = 8 * PART_C
    return call(
        functools.partial(attn_back_kernel, layer=layer, weights=(wqkv,)), (N_TILE,),
        [sds((MB_TOK, D), BF), sds((half, D), BF), sds((half, D), BF)],
        [
            rev_cols(D), rev_cols(D), rev_cols(D), rev_cols(1), rev_cols(3 * D), rev_rows(D),
            rev_rows(D), rev_cols(HEADS), whole((PAD_BLK, D)), whole((PAD_BLK, D)), whole((2, D)),
            whole((1, D)),
        ] + [ANY] * len(wqkv.flat()),
        [rev_rows(D), whole((half, D)), whole((half, D))],
        attn_back_scratch() + [pltpu.VMEM((3 * D, TILE), F32)] + weight_scratch(wqkv),
        (meta, gh, gatt, xh1, r1, qkv, krow, vrow, lse, ks, vs, gains, gln2, *wqkv.flat()),
    )


def whole_layer(meta, x, cotangent, gains, wqkv, wout, wup, wdown, layer):
    weights = (wqkv, wout, wup, wdown)
    tiled = lambda *shape: pltpu.VMEM((N_TILE,) + shape, BF)
    sums = sds((16, PART_A + PART_B + PART_C, D), BF)
    forth = lambda t: jnp.minimum(t, N_TILE - 1)
    back = lambda t, *_: (jnp.where(t < N_TILE, N_TILE - 1, 2 * N_TILE - 1 - t), 0)
    return call(
        functools.partial(layer_kernel, layer=layer, weights=weights), (2 * N_TILE,),
        [sds((MB_TOK, D), BF), sds((MB_TOK, D), BF), sums],
        [
            pl.BlockSpec((TILE, D), lambda t, *_: (forth(t), 0)),
            pl.BlockSpec((TILE, D), lambda t, m: (m[6] * N_TILE + forth(t), 0)),
            whole((2, D)),
        ] + [ANY] * len(flat(weights)),
        [
            pl.BlockSpec((TILE, D), lambda t, *_: (forth(t), 0)),
            pl.BlockSpec((TILE, D), back), ANY,
        ],
        [
            tiled(D, TILE), pltpu.VMEM((N_TILE, 1, TILE), F32), tiled(3 * D, TILE), tiled(TILE, D),
            tiled(TILE, D), pltpu.VMEM((N_TILE, HEADS, TILE), F32), pltpu.VMEM((D, TILE), BF),
            pltpu.VMEM((D, TILE), BF), pltpu.VMEM((1, TILE), F32), pltpu.VMEM((PAD_BLK, D), BF),
            pltpu.VMEM((PAD_BLK, D), BF), pltpu.VMEM((N_TILE, D, TILE), F32), tiled(D, TILE),
            pltpu.VMEM((FF, TILE), BF), pltpu.VMEM((FF, TILE), BF), pltpu.VMEM((D, TILE), BF),
            pltpu.VMEM((3 * D, TILE), F32),
        ] + mlp_scratch() + attn_back_scratch() + [
            pltpu.VMEM((16, PART_A + PART_B, D), BF), pltpu.VMEM((16, PART_C, D), BF),
        ] + weight_scratch(*weights) + [pltpu.SemaphoreType.DMA((2,))],
        (meta, x, cotangent, gains, *flat(weights)),
    )


def combine_kernel(meta_ref, *refs, count, cuts):
    values, outs = refs[:count], refs[count:]
    x, z = (meta_ref[7] >> 1) & 1, meta_ref[8]
    for out, (start, kind, k) in zip(outs, cuts):
        rows = out.shape[0]
        spot = {"x": x ^ k, "z": z ^ k, "all": 0}[kind]
        part = pl.ds(pl.multiple_of(start + spot * rows, 16), rows)
        total = values[0][part].astype(F32)
        for value in values[1:]:
            total = total + value[part].astype(F32)
        out[...] = total.astype(BF)


def combine(meta, values, cuts):
    return pl.pallas_call(
        functools.partial(
            combine_kernel, count=len(values), cuts=tuple((c[0],) + c[2:] for c in cuts)
        ),
        out_shape=tuple(sds((c[1], D), BF) for c in cuts),
        grid_spec=pltpu.PrefetchScalarGridSpec(
            num_scalar_prefetch=1, grid=(1,),
            in_specs=[part_spec(v.shape, (0, 0)) for v in values],
            out_specs=[part_spec((c[1], D), (0, 0)) for c in cuts],
        ),
        cost_estimate=pl.CostEstimate(flops=10**10, bytes_accessed=10**7, transcendentals=0),
        compiler_params=pltpu.CompilerParams(vmem_limit_bytes=VMEM_LIMIT // 4),
    )(meta, *values)


def by_x(start, rows):
    return [(start, rows, "x", 0), (start, rows, "x", 1)]


def by_z(start, rows):
    return [(start, rows, "z", k) for k in range(4)]


def finish_whole_kernel(held, _, up_ref, down_ref, out_ref, *, widths):
    total = sum(widths)
    places = [(s & 3) * 4 + ((s >> 2) & 1) * 2 + (s >> 3) for s in range(16)]

    def take(i):
        start = (widths[1], 0, widths[1] + widths[0])[i]
        return jnp.concatenate(
            [held[pl.ds(p * total + start, widths[i])] for p in places], axis=0
        )

    up_ref[...] = take(0).T.astype(F32)
    down_ref[...] = take(1).astype(F32)
    out_ref[...] = take(2).astype(F32)


def finish_whole(value, widths, shapes, specs, up):
    return pl.pallas_call(
        functools.partial(finish_whole_kernel, widths=widths),
        out_shape=tuple(sds(shape, F32) for shape in shapes),
        grid=(1,), in_specs=[part_spec(value.shape, (0, 0)), ANY], out_specs=specs,
        input_output_aliases={1: 0},
        compiler_params=pltpu.CompilerParams(vmem_limit_bytes=VMEM_LIMIT),
    )(value, up)


def finish_kernel(meta_ref, *refs, widths, targets, extra):
    pieces, refs = refs[:4], refs[4 + extra:]
    outs, held, sem = refs[:len(widths)], refs[-2], refs[-1]
    rows = held.shape[0] // 4
    for index, piece in enumerate(pieces):
        place = meta_ref[7] ^ index
        spot = (place & 1) * 2 + (place >> 1)
        pltpu.make_async_copy(
            piece, held.at[pl.ds(pl.multiple_of(spot * rows, rows), rows)], sem
        ).start()
    for index, piece in enumerate(pieces):
        pltpu.make_async_copy(piece, held.at[pl.ds(index * rows, rows)], sem).wait()
    total = sum(widths)
    for i, (width, flip) in enumerate(zip(widths, targets)):
        start = sum(widths[:i])
        value = jnp.concatenate(
            [held[pl.ds(s * total + start, width)] for s in range(16)], axis=0
        )
        outs[i][...] = (value.T if flip else value).astype(F32)


def finish(meta, pieces, widths, flips, shapes, specs, more=(), alias=None):
    rows = pieces[0].shape[0]
    return pl.pallas_call(
        functools.partial(finish_kernel, widths=widths, targets=flips, extra=len(more)),
        out_shape=tuple(sds(shape, F32) for shape in shapes),
        grid_spec=pltpu.PrefetchScalarGridSpec(
            num_scalar_prefetch=1, grid=(1,), in_specs=[ANY] * (4 + len(more)), out_specs=specs,
            scratch_shapes=[pltpu.VMEM((4 * rows, D), BF), pltpu.SemaphoreType.DMA],
        ),
        input_output_aliases=alias or {},
        compiler_params=pltpu.CompilerParams(vmem_limit_bytes=VMEM_LIMIT),
    )(meta, *pieces, *more)


def part_spec(shape, index):
    return pl.BlockSpec(shape, lambda t, *_: index)


def swap_xor(value, mask):
    size = lax.axis_size("dp")
    return lax.ppermute(value, "dp", [(i, i ^ mask) for i in range(size)])


def swap_section(value):
    return lax.ppermute(value, "section", [(0, 1), (1, 0)])


def to_section(value, target):
    return lax.ppermute(value, "section", [(1 - target, target)])


def exchange(value0, value1):
    return swap_section(jnp.where(lax.axis_index("section") == 0, value1, value0))


def low_groups():
    size = lax.axis_size("dp")
    return None if size == 16 else [list(range(i, i + 16)) for i in range(0, size, 16)]


def added(*values):
    total = values[0].astype(F32)
    for value in values[1:]:
        total = total + value.astype(F32)
    return total.astype(BF)


def halves(value, bit):
    half = value.shape[0] // 2
    mine = (lax.axis_index("dp") >> bit) & 1
    return (
        lax.dynamic_slice_in_dim(value, mine * half, half, 0),
        lax.dynamic_slice_in_dim(value, (1 - mine) * half, half, 0),
    )


def half_sum(pair, bit):
    return added(pair[0], swap_xor(pair[1], 1 << bit))


def quarters(value, bit):
    rows = value.shape[0] // 4
    mine = (lax.axis_index("dp") >> bit) & 3
    return tuple(lax.dynamic_slice_in_dim(value, (mine ^ k) * rows, rows, 0) for k in range(4))


def swap_quarters(parts, bit):
    return [swap_xor(parts[k], k << bit) for k in (1, 2, 3)]


def quarter_sum(parts, bit):
    return added(parts[0], *swap_quarters(parts, bit))


def tie(*values):
    return lax.optimization_barrier(values)


def rest_bits():
    return range(4, lax.axis_size("dp").bit_length() - 1)


def reduce_core(halves):
    return added(halves[1], swap_xor(halves[0], 1))


def reduce_rest(value):
    for bit in rest_bits():
        value = half_sum(halves(value, bit), bit)
    return value


def gather_bit(value, bit):
    mine = (lax.axis_index("dp") >> bit) & 1
    other = swap_xor(value, 1 << bit)
    return jnp.where(
        mine == 0,
        jnp.concatenate([value, other], axis=0),
        jnp.concatenate([other, value], axis=0),
    )


def gather_quad(value, bit):
    mine = (lax.axis_index("dp") >> bit) & 3
    got = [value] + [swap_xor(value, k << bit) for k in (1, 2, 3)]
    parts = []
    for p in range(4):
        which = mine ^ p
        part = got[3]
        for k in (2, 1, 0):
            part = jnp.where(which == k, got[k], part)
        parts.append(part)
    return jnp.concatenate(parts, axis=0)


def gather_rest(value):
    for bit in reversed(rest_bits()):
        value = gather_bit(value, bit)
    return value


def spread_pieces(value):
    across = swap_xor(value, 2)
    return value, swap_xor(value, 1), across, swap_xor(across, 1)


def sum_rest(value):
    for bit in rest_bits():
        value = added(value, swap_xor(value, 1 << bit))
    return value


def per_device(
    tokens, cotangent, span_counts, tail_lens, ln1_gain, w_qkv, w_out, ln2_gain, w_up, w_down
):
    section = lax.axis_index("section")
    first = section == 0
    place = lax.axis_index("dp") & 3
    meta = jnp.concatenate([
        lax.dynamic_index_in_dim(span_counts, section, 0, keepdims=False),
        lax.dynamic_index_in_dim(tail_lens, section, 0, keepdims=False),
        section.astype(jnp.int32)[None], place.astype(jnp.int32)[None],
        ((lax.axis_index("dp") >> 2) & 3).astype(jnp.int32)[None],
    ])
    own = (w_qkv[0], w_out[0], w_up[0], w_down[0])

    def part(weight, spot, count):
        rows = weight.shape[0] // count
        return lax.dynamic_slice_in_dim(weight, spot * rows, rows, 0)

    own_gains = jnp.concatenate([ln1_gain, ln2_gain], axis=0)
    attn = swap_section(
        jnp.concatenate([part(own[0], place, 4), part(own[1], place, 4)], axis=1)
    )
    other_gains = swap_section(own_gains)
    attn, other_gains = tie(attn, other_gains)
    gains = [jnp.where(first, own_gains, other_gains), jnp.where(first, other_gains, own_gains)]
    attn_x = swap_xor(attn, 2)
    attn = (attn, swap_xor(attn, 1), attn_x, swap_xor(attn_x, 1))
    wqkv, wout = Weight(own[0], (attn, 0, 0, None)), Weight(own[1], (attn, 3 * D, 0, None))
    up = swap_section(part(own[2], place, 4))
    down = swap_section(part(own[3], place & 1, 2))
    up_x, up_c = swap_xor(up, 2), swap_xor(up, 1)

    keep0, hidden, second = forward_attn(meta, tokens, gains[0], wqkv, wout, 0)
    keep0, hidden, second, up_x, up_c, down = tie(keep0, hidden, second, up_x, up_c, down)
    wup = Weight(own[2], ((up, up_c, up_x, swap_xor(up_x, 1)), 0, 0, None))
    wdown = Weight(own[3], ((down, swap_xor(down, 1)), 0, 0, None))
    act_out0, act0, gp0 = forward_mlp(meta, hidden, second, wup, wdown, 0)
    act_out1, ig1, sums1 = whole_layer(
        meta, act_out0, cotangent, gains[1], wqkv, wout, wup, wdown, 1
    )
    cut = 2 * MB_TOK // 3
    acts_a = exchange(act_out0[:cut], act_out1[:cut])
    sums1 = lax.psum_scatter(
        sums1.reshape(-1, D), "dp", scatter_dimension=0, axis_index_groups=low_groups(), tiled=True
    )
    xh1, r1, qkv, krow, vrow, lse, att, xh2, r2, ks, vs = keep0
    back = mlp_back(meta, ig1, act0, gp0, xh2, r2, att, gains[0], wdown, wup, wout, 0)
    (send, kept, gln2, gh, gatt), acts_a, act_out0, act_out1 = tie(back, acts_a, act_out0, act_out1)
    mlp0 = combine(
        meta, (kept, swap_xor(send, 1)), by_x(0, 4 * PART_A) + by_z(8 * PART_A, 2 * PART_B)
    )
    a0, b0 = mlp0[:2], mlp0[2:]
    gh, a0, b0 = tie(gh, a0, b0)
    acts_b = exchange(act_out0[cut:], act_out1[cut:])
    a0_x, b0_z = swap_xor(a0[1], 2), swap_quarters(b0, 2)
    back = attn_back(
        meta, gh, gatt, xh1, r1, qkv, krow, vrow, lse, ks, vs, gains[0], gln2, wqkv, 0
    )
    (ig0, send, kept), a0_x, b0_z, acts_b = tie(back, a0_x, b0_z, acts_b)
    acts_in = jnp.concatenate([acts_a, acts_b], axis=0)
    c0 = swap_xor(send, 1)
    a0 = [added(*pair) for pair in zip(quarters(a0[0], 2), quarters(a0_x, 2))]
    a0, c0 = tie(a0, c0)
    a0_z = swap_quarters(a0, 2)
    c0 = combine(meta, (kept, c0), by_x(0, 4 * PART_C))
    b0 = halves(added(b0[0], *b0_z), 1)
    bc0_x = swap_xor(jnp.concatenate([b0[1], c0[1]], axis=0), 2)

    def own_sum(grad0, grad1):
        return added(jnp.where(first, grad0, grad1), swap_section(jnp.where(first, grad1, grad0)))

    b0 = added(b0[0], bc0_x[:PART_B])
    c0 = quarters(added(c0[0], bc0_x[PART_B:]), 2)
    c0_z = swap_quarters(c0, 2)
    a0_z, b0, c0_1 = tie(a0_z, b0, c0[1])
    (a0,) = combine(meta, (a0[0], *a0_z), [(0, PART_A, "all", 0)])
    spots = (0, PART_A, PART_A + PART_B, PART_A + PART_B + QKV_ROWS)
    a1, b1, c1, gains1 = [sums1[i:j] for i, j in zip(spots, spots[1:] + (sums1.shape[0],))]
    ab = own_sum(
        jnp.concatenate([reduce_rest(a0), reduce_rest(b0)], axis=0),
        jnp.concatenate([reduce_rest(a1), reduce_rest(b1)], axis=0),
    )
    ab, c0_z = tie(ab, c0_z)
    a_rows = ab.shape[0] * PART_A // (PART_A + PART_B)
    a_full = lax.all_gather(
        gather_rest(ab[:a_rows]), "dp", axis=0, axis_index_groups=low_groups(), tiled=True
    )
    c0 = added(c0[0], *c0_z)
    c_own = own_sum(
        jnp.concatenate([reduce_rest(c0[:QKV_ROWS]), sum_rest(c0[QKV_ROWS:])], axis=0),
        jnp.concatenate([reduce_rest(c1), sum_rest(gains1)], axis=0),
    )
    c_own, ig0 = tie(c_own, ig0)
    grads_in = exchange(ig0, ig1)
    lns = c_own[-GAIN_ROWS:][:2].astype(F32)
    bc_own = jnp.concatenate([gather_rest(ab[a_rows:]), gather_rest(c_own[:-GAIN_ROWS])], axis=0)
    bc_pieces = spread_pieces(gather_quad(bc_own, 2))
    grad_up, grad_qkv = finish(
        meta, bc_pieces, (UP_B // 16, QKV_ROWS), (True, True), [(D, FF), (D, 3 * D)],
        [part_spec((D, UP_B), (0, 0)), part_spec((D, 3 * D), (0, 0))],
    )
    grad_up, a_full = tie(grad_up, a_full)
    grad_up, grad_down, grad_out = finish_whole(
        a_full, (UP_A // 16, DOWN_ROWS, OUT_ROWS), [(D, FF), (FF, D), (D, D)],
        [
            part_spec((D, UP_A), (0, UP_B // UP_A)), part_spec((FF, D), (0, 0)),
            part_spec((D, D), (0, 0)),
        ],
        grad_up,
    )

    def assemble(value0, value1, got):
        return jnp.concatenate(
            [jnp.where(first, value0, got), jnp.where(first, got, value1)], axis=0
        )

    activations = assemble(act_out0, act_out1, acts_in)
    input_grads = assemble(ig0, ig1, grads_in)
    return (
        activations[None],
        input_grads[None],
        lns[:1],
        grad_qkv[None],
        grad_out[None],
        lns[1:],
        grad_up[None],
        grad_down[None],
    )


def solution(mesh):
    return jax.shard_map(
        per_device,
        mesh=mesh,
        in_specs=(
            P("dp", None),
            P("dp", None),
            P("dp", None),
            P("dp", None),
            P("section", None),
            P("section", None, None),
            P("section", None, None),
            P("section", None),
            P("section", None, None),
            P("section", None, None),
        ),
        out_specs=(
            P("section", "dp", None),
            P("section", "dp", None),
            P("section", None),
            P("section", None, None),
            P("section", None, None),
            P("section", None),
            P("section", None, None),
            P("section", None, None),
        ),
        check_vma=False,
    )
```

```python
import functools

import jax
import jax.numpy as jnp
from jax import lax
from jax.experimental import pallas as pl
from jax.experimental.pallas import tpu as pltpu
from jax.sharding import PartitionSpec as P

D = 512
HEADS = 8
HEAD_DIM = 64
FF = 2048
SPAN = 128
MB_BLK = 12
MB_TOK = MB_BLK * SPAN
PAD_BLK = 16
EPSILON = 1e-05
NEG_FILL = -1e30
BF = jnp.bfloat16
F32 = jnp.float32
VMEM_LIMIT = 58 * 2**20

TILE = 512
TILE_BLK = TILE // SPAN
N_TILE = MB_TOK // TILE
FF_STEP = 512
FWD_STEP = 512
FWD_GROUP = 2
BACK_GROUP = 2


def dot(left, right, left_dim, right_dim):
    return lax.dot_general(
        left, right, (((left_dim,), (right_dim,)), ((), ())), preferred_element_type=F32
    )


def block_facts(meta_ref, block):
    end_one = meta_ref[0]
    end_two = end_one + meta_ref[1]
    in_one = block < end_one
    in_two = block < end_two
    first = jnp.where(in_one, 0, jnp.where(in_two, end_one, end_two))
    last = jnp.where(in_one, end_one, jnp.where(in_two, end_two, MB_BLK)) - 1
    tail = jnp.where(in_one, meta_ref[3], jnp.where(in_two, meta_ref[4], meta_ref[5]))
    filled = jnp.where(block == last, tail, SPAN)
    return filled, first


def filled_column(meta_ref, width):
    rows = lax.broadcasted_iota(jnp.int32, (PAD_BLK, width), 0)
    out = jnp.full((PAD_BLK, width), SPAN, jnp.int32)
    for block in range(MB_BLK):
        filled, _ = block_facts(meta_ref, block)
        out = jnp.where(rows == block, filled, out)
    return out.astype(F32)


def filled_row(meta_ref):
    cols = lax.broadcasted_iota(jnp.int32, (1, PAD_BLK), 1)
    out = jnp.full((1, PAD_BLK), SPAN, jnp.int32)
    for block in range(MB_BLK):
        filled, _ = block_facts(meta_ref, block)
        out = jnp.where(cols == block, filled, out)
    return out.astype(F32)


def member_mask(meta_ref, tile_start):
    parts = []
    rows = lax.broadcasted_iota(jnp.int32, (PAD_BLK, SPAN), 0)
    cols = lax.broadcasted_iota(jnp.int32, (PAD_BLK, SPAN), 1)
    for j in range(TILE_BLK):
        block = tile_start + j
        filled, _ = block_facts(meta_ref, block)
        parts.append(jnp.where((rows == block) & (cols < filled), 1.0, 0.0).astype(BF))
    return jnp.concatenate(parts, axis=1)


def pair_diag(rows_two):
    zero = jnp.zeros((HEAD_DIM, SPAN), rows_two.dtype)
    top = jnp.concatenate([rows_two[:HEAD_DIM], zero], axis=1)
    low = jnp.concatenate([zero, rows_two[HEAD_DIM:]], axis=1)
    return jnp.concatenate([top, low], axis=0)


def diag_rows(square):
    return jnp.concatenate([square[:HEAD_DIM, :SPAN], square[HEAD_DIM:, SPAN:]], axis=0)


def gain_column(gains_ref, index):
    return jnp.broadcast_to(gains_ref[index:index + 1], (SPAN, D)).T


def times_gain(values, gain):
    return jnp.concatenate(
        [values[:, i * SPAN:(i + 1) * SPAN] * gain for i in range(values.shape[1] // SPAN)], axis=1
    )


def normalize(values):
    mean = jnp.sum(values, axis=0, keepdims=True) * (1.0 / D)
    center = values - mean
    spread = jnp.sum(center * center, axis=0, keepdims=True) * (1.0 / D)
    factor = lax.rsqrt(spread + EPSILON)
    return center * factor, factor


def score_mask(block, filled, first):
    rows = lax.broadcasted_iota(jnp.int32, (SPAN + PAD_BLK, 2 * SPAN), 0)
    cols = lax.broadcasted_iota(jnp.int32, (SPAN + PAD_BLK, 2 * SPAN), 1) % SPAN
    local = (rows <= cols) & (rows < filled)
    earlier = (rows >= SPAN + first) & (rows < SPAN + block)
    return local | earlier


def attention_items(meta_ref, tile_start, blocks):
    items = []
    for j in blocks:
        filled, first = block_facts(meta_ref, tile_start + j)
        mask = score_mask(tile_start + j, filled, first)
        for hp in range(HEADS // 2):
            items.append((slice(j * SPAN, (j + 1) * SPAN), hp, slice(hp * SPAN, (hp + 1) * SPAN), mask))
    return items


class Weight:
    def __init__(self, own, *groups):
        self.own = own
        self.groups = [(tuple(p), lane, at, width or own.shape[1]) for p, lane, at, width in groups]

    def flat(self):
        return (self.own,) + sum((group[0] for group in self.groups), ())

    def bind(self, refs):
        own, refs, groups = refs[0], refs[1:], []
        for pieces, *rest in self.groups:
            groups.append((refs[:len(pieces)], *rest))
            refs = refs[len(pieces):]
        return Weight(own, *groups), refs


def start_weight(meta_ref, layer, weight, target, sem):
    @pl.when(meta_ref[6] == layer)
    def _():
        pltpu.make_async_copy(weight.own, target, sem).start()

    @pl.when(meta_ref[6] != layer)
    def _():
        for pieces, lane, at, width in weight.groups:
            count = len(pieces)
            rows = target.shape[0] // count
            for index, piece in enumerate(pieces):
                spot = (meta_ref[7] & (count - 1)) ^ index
                pltpu.make_async_copy(
                    piece.at[:, pl.ds(lane, width)],
                    target.at[pl.ds(pl.multiple_of(spot * rows, rows), rows), pl.ds(at, width)], sem,
                ).start()


def wait_weight(weight, target, sem):
    pltpu.make_async_copy(weight.own, target, sem).wait()


def forward_attn_part(meta_ref, tile, x_ref, gains_ref, outs, scratch, wqkv_ref, wout_ref, wait):
    (xh1_ref, r1_ref, qkv_ref, krow_ref, vrow_ref, lse_ref, att_ref, xh2_ref, r2_ref, ks_ref,
     vs_ref) = outs
    (attf_ref,) = scratch
    tile_start = tile * TILE_BLK

    @pl.when(tile == 0)
    def _():
        ks_ref[...] = jnp.zeros_like(ks_ref)
        vs_ref[...] = jnp.zeros_like(vs_ref)

    x_t = x_ref[...].T.astype(F32)
    xhat, r1 = normalize(x_t)
    xh1_ref[...] = xhat.astype(BF)
    r1_ref[...] = r1
    normed = times_gain(xhat, gain_column(gains_ref, 0)).astype(BF)
    wait(0)
    q_t = (dot(wqkv_ref[:, :D], normed, 0, 0) * HEAD_DIM ** (-0.5)).astype(BF)
    k_t = dot(wqkv_ref[:, D:2 * D], normed, 0, 0).astype(BF)
    v_t = dot(wqkv_ref[:, 2 * D:], normed, 0, 0).astype(BF)
    qkv_ref[:D] = q_t
    qkv_ref[D:2 * D] = k_t
    qkv_ref[2 * D:] = v_t
    krow = k_t.T
    vrow = v_t.T
    krow_ref[...] = krow
    vrow_ref[...] = vrow
    members = member_mask(meta_ref, tile_start)
    fill = filled_column(meta_ref, D)
    block_rows = lax.broadcasted_iota(jnp.int32, (PAD_BLK, D), 0)
    fresh = (block_rows >= tile_start) & (block_rows < tile_start + TILE_BLK)
    key_sums = jnp.where(fresh, (dot(members, krow, 1, 0) / fill).astype(BF), ks_ref[...])
    value_sums = jnp.where(fresh, (dot(members, vrow, 1, 0) / fill).astype(BF), vs_ref[...])
    ks_ref[...] = key_sums
    vs_ref[...] = value_sums
    vs_t = value_sums.T
    for j in range(0, TILE_BLK, FWD_GROUP):
        items = attention_items(meta_ref, tile_start, range(j, j + FWD_GROUP))
        scores = [
            dot(
                jnp.concatenate([krow[cols, feats], key_sums[:, feats]], axis=0),
                pair_diag(q_t[feats, cols]), 1, 0,
            )
            for cols, _, feats, _ in items
        ]
        probs = []
        for (cols, hp, feats, mask), score in zip(items, scores):
            score = jnp.where(mask, score, NEG_FILL)
            top = jnp.max(score, axis=0, keepdims=True)
            prob = jnp.exp(score - top)
            total = jnp.sum(prob, axis=0, keepdims=True)
            logs = top + jnp.log(total)
            lse_ref[2 * hp:2 * hp + 1, cols] = logs[:, :SPAN]
            lse_ref[2 * hp + 1:2 * hp + 2, cols] = logs[:, SPAN:]
            probs.append((prob * (1.0 / total)).astype(BF))
        for (cols, _, feats, _), prob in zip(items, probs):
            values = jnp.concatenate([v_t[feats, cols], vs_t[feats]], axis=1)
            attf_ref[feats, cols] = diag_rows(dot(values, prob, 1, 0)).astype(BF)
    att = attf_ref[...]
    att_ref[...] = att
    wait(1)
    hidden = x_t + dot(wout_ref[...], att, 0, 0)
    xhat2, r2 = normalize(hidden)
    xh2_ref[...] = xhat2.astype(BF)
    r2_ref[...] = r2
    return hidden, times_gain(xhat2, gain_column(gains_ref, 1)).astype(BF)


def forward_mlp_part(hidden, second, outs, wup_ref, wdown_ref):
    out_ref, act_ref, gp_ref = outs
    total_out = hidden
    up = dot(wup_ref[:, :FWD_STEP], second, 0, 0)
    for f in range(FF // FWD_STEP):
        part = slice(f * FWD_STEP, (f + 1) * FWD_STEP)
        later = slice((f + 1) * FWD_STEP, (f + 2) * FWD_STEP)
        ahead = dot(wup_ref[:, later], second, 0, 0) if later.stop <= FF else None
        bell = jnp.exp(up * up * -0.5)
        phi = 0.5 + 0.5 * lax.erf(up * (0.5 ** 0.5))
        act = (up * phi).astype(BF)
        act_ref[part] = act
        gp_ref[part] = (phi + up * bell * 0.3989422804014327).astype(BF)
        total_out = total_out + dot(wdown_ref[part], act, 0, 0)
        up = ahead
    out_ref[...] = total_out.astype(BF).T


def weight_waits(meta_ref, layer, weights, targets, sems):
    begin = pl.program_id(0) == 0

    @pl.when(begin)
    def _():
        for i, (weight, target) in enumerate(zip(weights, targets)):
            start_weight(meta_ref, layer, weight, target, sems.at[i])

    def wait(i):
        @pl.when(begin)
        def _():
            wait_weight(weights[i], targets[i], sems.at[i])

    return wait


def bound(weights, refs):
    out = []
    for weight in weights:
        weight, refs = weight.bind(refs)
        out.append(weight)
    return out, refs


def forward_attn_kernel(meta_ref, x_ref, gains_ref, *refs, layer, weights):
    weights, refs = bound(weights, refs)
    attn_outs, (hid_ref, sec_ref), scratch, targets, sems = (
        refs[:11], refs[11:13], refs[13:14], refs[14:16], refs[16]
    )
    wait = weight_waits(meta_ref, layer, weights, targets, sems)
    hidden, second = forward_attn_part(
        meta_ref, pl.program_id(0), x_ref, gains_ref, attn_outs, scratch, targets[0], targets[1], wait
    )
    hid_ref[...] = hidden
    sec_ref[...] = second


def forward_mlp_kernel(meta_ref, hid_ref, sec_ref, *refs, layer, weights):
    weights, refs = bound(weights, refs)
    outs, targets, sems = refs[:3], refs[3:5], refs[5]
    wait = weight_waits(meta_ref, layer, weights, targets, sems)
    wait(0)
    wait(1)
    forward_mlp_part(hid_ref[...], sec_ref[...], outs, *targets)


def write_halves(meta_ref, parts, send_ref, keep_ref, start=0, z_first=False):
    core = meta_ref[7] & 1
    total = sum(rows for _, _, rows in parts)
    for target, side in ((send_ref, 1 - core), (keep_ref, core)):
        for s in range(8):
            spot = start + ((s % 4) * 2 + s // 4 if z_first else s) * total
            for acc, base, rows in parts:
                if acc.shape[0] == rows:
                    value = acc[...]
                else:
                    first = base + pl.multiple_of(side * (8 * rows), 8 * rows) + s * rows
                    value = acc[pl.ds(first, rows)]
                target[pl.ds(spot, rows)] = value.astype(BF)
                spot += rows


def write_shards(parts, target):
    for place in range(16):
        s = (place & 1) * 8 + ((place >> 1) & 1) * 4 + (place >> 2)
        spot = 0
        for acc, base, rows in parts:
            value = acc[...] if acc.shape[0] == rows else acc[pl.ds(base + s * rows, rows)]
            target[place, pl.ds(spot, rows)] = value.astype(BF)
            spot += rows


DOWN_ROWS, OUT_ROWS, QKV_ROWS, GAIN_ROWS = FF // 16, D // 16, 3 * D // 16, 16
UP_A = FF // 2
UP_B = FF - UP_A
PART_A, PART_B = DOWN_ROWS + UP_A // 16 + OUT_ROWS, UP_B // 16
PART_C = QKV_ROWS + GAIN_ROWS
OVERLAPPED = 4 * 10**9


def norm_back(grad, gain, xhat, factor, gln_acc):
    prod = grad * xhat
    for j in range(TILE_BLK):
        gln_acc[...] += prod[:, j * SPAN:(j + 1) * SPAN]
    scaled = times_gain(grad, gain)
    mean = jnp.sum(scaled, axis=0, keepdims=True) * (1.0 / D)
    mean_x = jnp.sum(scaled * xhat, axis=0, keepdims=True) * (1.0 / D)
    return factor * (scaled - mean - xhat * mean_x)


def masked_low(meta_ref, tile, low):
    parts = []
    cols = lax.broadcasted_iota(jnp.int32, (D, SPAN), 1)
    for j in range(TILE_BLK):
        filled, _ = block_facts(meta_ref, tile * TILE_BLK + j)
        part = low[:, j * SPAN:(j + 1) * SPAN]
        parts.append(jnp.where(cols < filled, part, jnp.zeros((), BF)))
    return jnp.concatenate(parts, axis=1)


def zero_all(refs):
    for ref in refs:
        ref[...] = jnp.zeros_like(ref)


def mlp_back_part(low, data, gains_ref, weights, accs, wait, gh_ref, gatt_ref):
    act_ref, gp_ref, xh2_ref, r2_ref, att_ref = data
    wdown_ref, wup_ref, wout_ref = weights
    gdown_acc, gup_acc, gout_acc, gln_acc = accs
    gain = gain_column(gains_ref, 1)
    xhat = xh2_ref[...].astype(F32)
    second = times_gain(xhat, gain).astype(BF)
    wait(0)
    wait(1)
    e = None
    for f in range(FF // FF_STEP):
        part = slice(f * FF_STEP, (f + 1) * FF_STEP)
        gdown_acc[part] += dot(act_ref[part], low, 1, 1)
        ga = dot(wdown_ref[part], low, 1, 0)
        gui = (ga * gp_ref[part].astype(F32)).astype(BF)
        gup_acc[part] += dot(gui, second, 1, 1)
        term = dot(wup_ref[:, part], gui, 1, 0)
        e = term if e is None else e + term
    gh = low.astype(F32) + norm_back(e, gain, xhat, r2_ref[...], gln_acc)
    gh_ref[...] = gh
    ghb = gh.astype(BF)
    gout_acc[...] += dot(att_ref[...], ghb, 1, 1)
    wait(2)
    gatt_ref[...] = dot(wout_ref[...], ghb, 1, 0).astype(BF)


def mlp_parts(gdown_acc, gup_acc, gout_acc):
    part_a = ((gdown_acc, 0, DOWN_ROWS), (gup_acc, UP_B, UP_A // 16), (gout_acc, 0, OUT_ROWS))
    return part_a, ((gup_acc, 0, UP_B // 16),)


def mlp_back_kernel(
    meta_ref, seed_ref, act_ref, gp_ref, xh2_ref, r2_ref, att_ref, gains_ref, *refs, layer, weights,
):
    weights, refs = bound(weights, refs)
    (send_ref, keep_ref, gln_ref, gh_ref, gatt_ref, gdown_acc, gup_acc, gout_acc, gln_acc,
     wdown_ref, wup_ref, wout_ref, sems) = refs
    step = pl.program_id(0)
    targets = (wdown_ref, wup_ref, wout_ref)
    accs = (gdown_acc, gup_acc, gout_acc, gln_acc)
    wait = weight_waits(meta_ref, layer, weights, targets, sems)

    @pl.when(step == 0)
    def _():
        zero_all(accs)

    mlp_back_part(
        seed_ref[...].T, (act_ref, gp_ref, xh2_ref, r2_ref, att_ref), gains_ref, targets, accs, wait,
        gh_ref, gatt_ref,
    )

    @pl.when(step == N_TILE - 1)
    def _():
        part_a, part_b = mlp_parts(*accs[:3])
        write_halves(meta_ref, part_a, send_ref, keep_ref)
        write_halves(meta_ref, part_b, send_ref, keep_ref, 8 * PART_A, True)
        gln_ref[...] = jnp.sum(gln_acc[...].T, axis=0, keepdims=True)


def attn_back_part(meta_ref, tile, gh_ref, gatt_ref, data, gains_ref, wqkv_ref, accs, rows_ref, wait):
    xh1_ref, r1_ref, qkv_ref, krow_ref, vrow_ref, lse_ref, ks_ref, vs_ref = data
    gqkv_acc, gln_acc, gks_acc, gvs_acc = accs
    tile_start = tile * TILE_BLK
    q_t = qkv_ref[:D]
    gatt = gatt_ref[...]
    key_sums, value_sums = ks_ref[...], vs_ref[...]
    ks_t = key_sums.T
    for j in range(0, TILE_BLK, BACK_GROUP):
        items = attention_items(meta_ref, tile_start, range(j, j + BACK_GROUP))
        q_diags = [pair_diag(q_t[feats, cols]) for cols, _, feats, _ in items]
        g_diags = [pair_diag(gatt[feats, cols]) for cols, _, feats, _ in items]
        scores = [
            dot(jnp.concatenate([krow_ref[cols, feats], key_sums[:, feats]], axis=0), q, 1, 0)
            for (cols, _, feats, _), q in zip(items, q_diags)
        ]
        dps = [
            dot(jnp.concatenate([vrow_ref[cols, feats], value_sums[:, feats]], axis=0), g, 1, 0)
            for (cols, _, feats, _), g in zip(items, g_diags)
        ]
        grads, probs = [], []
        for (cols, hp, feats, mask), score, dp in zip(items, scores, dps):
            logs = jnp.concatenate(
                [lse_ref[2 * hp:2 * hp + 1, cols], lse_ref[2 * hp + 1:2 * hp + 2, cols]], axis=1
            )
            prob = jnp.exp(jnp.where(mask, score, NEG_FILL) - logs)
            weighted = prob * dp
            delta = jnp.sum(weighted, axis=0, keepdims=True)
            grads.append((weighted - prob * delta).astype(BF))
            probs.append(prob.astype(BF))
        for (cols, hp, feats, _), grad, prob, q, g in zip(items, grads, probs, q_diags, g_diags):
            key_feats = slice(D + hp * SPAN, D + (hp + 1) * SPAN)
            value_feats = slice(2 * D + hp * SPAN, 2 * D + (hp + 1) * SPAN)
            keys = jnp.concatenate([qkv_ref[key_feats, cols], ks_t[feats]], axis=1)
            rows_ref[feats, cols] = diag_rows(dot(keys, grad, 1, 0))
            key_grad = dot(q, grad, 1, 1)
            value_grad = dot(g, prob, 1, 1)
            rows_ref[key_feats, cols] = key_grad[:, :SPAN]
            rows_ref[value_feats, cols] = value_grad[:, :SPAN]
            gks_acc[feats] += key_grad[:, SPAN:]
            gvs_acc[feats] += value_grad[:, SPAN:]
    members = member_mask(meta_ref, tile_start)
    fill = filled_row(meta_ref)

    def spread_back(acc_ref):
        back = (acc_ref[...].astype(BF).astype(F32) / fill).astype(BF)
        return dot(back, members, 1, 0)

    grad_q = rows_ref[:D] * HEAD_DIM ** (-0.5)
    grad_k = rows_ref[D:2 * D] + spread_back(gks_acc)
    grad_v = rows_ref[2 * D:] + spread_back(gvs_acc)
    gain = gain_column(gains_ref, 0)
    xhat = xh1_ref[...].astype(F32)
    normed = times_gain(xhat, gain).astype(BF)
    wait(0)
    e = None
    for i, rows in enumerate((grad_q, grad_k, grad_v)):
        rows = rows.astype(BF)
        part = slice(i * D, (i + 1) * D)
        gqkv_acc[part] += dot(rows, normed, 1, 1)
        term = dot(wqkv_ref[:, part], rows, 1, 0)
        e = term if e is None else e + term
    return (gh_ref[...] + norm_back(e, gain, xhat, r1_ref[...], gln_acc)).astype(BF).T


def gain_rows(gln_acc, gln2):
    gln = jnp.sum(gln_acc[...].T, axis=0, keepdims=True)
    rest = jnp.zeros((GAIN_ROWS - 2, D), F32)
    return jnp.concatenate([gln, gln2, rest], axis=0).astype(BF)


def attn_back_kernel(
    meta_ref, gh_ref, gatt_ref, xh1_ref, r1_ref, qkv_ref, krow_ref, vrow_ref, lse_ref, ks_ref,
    vs_ref, gains_ref, gln2_ref, *refs, layer, weights,
):
    weights, refs = bound(weights, refs)
    (gin_ref, send_ref, keep_ref, gqkv_acc, gln_acc, gks_acc, gvs_acc, rows_ref, wqkv_ref,
     sems) = refs
    step = pl.program_id(0)
    wait = weight_waits(meta_ref, layer, weights, (wqkv_ref,), sems)
    accs = (gqkv_acc, gln_acc, gks_acc, gvs_acc)

    @pl.when(step == 0)
    def _():
        zero_all(accs)

    data = (xh1_ref, r1_ref, qkv_ref, krow_ref, vrow_ref, lse_ref, ks_ref, vs_ref)
    gin_ref[...] = attn_back_part(
        meta_ref, N_TILE - 1 - step, gh_ref, gatt_ref, data, gains_ref, wqkv_ref, accs, rows_ref, wait
    )

    @pl.when(step == N_TILE - 1)
    def _():
        parts = ((gqkv_acc, 0, QKV_ROWS), (gain_rows(gln_acc, gln2_ref[...]), 0, GAIN_ROWS))
        write_halves(meta_ref, parts, send_ref, keep_ref)


def layer_kernel(meta_ref, x_ref, cot_ref, gains_ref, *refs, layer, weights):
    weights, refs = bound(weights, refs)
    out_ref, gin_ref, sums_ref, send_ref, keep_ref, *refs = refs
    keep, refs = refs[:13], refs[13:]
    (xh1, r1, qkv, krow, vrow, lse, att_ref, xh2_ref, r2_ref, ks_ref, vs_ref, gh, gatt) = keep
    act_ref, gp_ref, attf_ref, rows_ref, *refs = refs
    mlp_accs, attn_accs, refs = refs[:4], refs[4:8], refs[8:]
    held_mlp, *refs = refs
    targets, sems, copied = refs[:4], refs[4], refs[5]
    wqkv_ref, wout_ref, wup_ref, wdown_ref = targets
    step = pl.program_id(0)
    wait = weight_waits(meta_ref, layer, weights, targets, sems)
    copy = pltpu.make_async_copy(held_mlp, sums_ref, copied)

    @pl.when(step == 0)
    def _():
        zero_all(mlp_accs)
        zero_all(attn_accs)

    @pl.when(step < N_TILE)
    def _():
        tile = step
        outs = (
            xh1.at[tile], r1.at[tile], qkv.at[tile], krow.at[tile], vrow.at[tile], lse.at[tile],
            att_ref, xh2_ref, r2_ref, ks_ref, vs_ref,
        )
        hidden, second = forward_attn_part(
            meta_ref, tile, x_ref, gains_ref, outs, (attf_ref,), wqkv_ref, wout_ref, wait
        )
        wait(2)
        wait(3)
        forward_mlp_part(hidden, second, (out_ref, act_ref, gp_ref), wup_ref, wdown_ref)
        mlp_back_part(
            masked_low(meta_ref, tile, cot_ref[...].T), (act_ref, gp_ref, xh2_ref, r2_ref, att_ref),
            gains_ref, (wdown_ref, wup_ref, wout_ref), mlp_accs, lambda i: None, gh.at[tile],
            gatt.at[tile],
        )

    @pl.when(step == N_TILE)
    def _():
        part_a, part_b = mlp_parts(*mlp_accs[:3])
        write_shards(part_a + part_b, held_mlp)
        copy.start()

    @pl.when(step >= N_TILE)
    def _():
        tile = 2 * N_TILE - 1 - step
        data = (
            xh1.at[tile], r1.at[tile], qkv.at[tile], krow.at[tile], vrow.at[tile], lse.at[tile],
            ks_ref, vs_ref,
        )
        gin_ref[...] = attn_back_part(
            meta_ref, tile, gh.at[tile], gatt.at[tile], data, gains_ref, wqkv_ref, attn_accs,
            rows_ref, lambda i: None,
        )

    @pl.when(step == 2 * N_TILE - 1)
    def _():
        gln2 = jnp.sum(mlp_accs[3][...].T, axis=0, keepdims=True)
        parts = (
            (attn_accs[0], 0, QKV_ROWS), (gain_rows(attn_accs[1], gln2), 0, GAIN_ROWS)
        )
        write_halves(meta_ref, parts, send_ref, keep_ref)
        copy.wait()


ANY = pl.BlockSpec(memory_space=pl.ANY)
sds = jax.ShapeDtypeStruct


def whole(shape):
    return pl.BlockSpec(shape, lambda t, *_: (0,) * len(shape), pipeline_mode=pl.Buffered(1))


def rows_spec(width):
    return pl.BlockSpec((TILE, width), lambda t, *_: (t, 0))


def cols_spec(height):
    return pl.BlockSpec((height, TILE), lambda t, *_: (0, t))


def rev_rows(width):
    return pl.BlockSpec((TILE, width), lambda t, *_: (N_TILE - 1 - t, 0))


def rev_cols(height):
    return pl.BlockSpec((height, TILE), lambda t, *_: (0, N_TILE - 1 - t))


def call(kernel, grid, outs, in_specs, out_specs, scratch, args):
    return pl.pallas_call(
        kernel,
        out_shape=tuple(outs),
        grid_spec=pltpu.PrefetchScalarGridSpec(
            num_scalar_prefetch=1, grid=grid, in_specs=in_specs, out_specs=out_specs,
            scratch_shapes=scratch,
        ),
        cost_estimate=pl.CostEstimate(flops=0, bytes_accessed=0, transcendentals=0),
        compiler_params=pltpu.CompilerParams(vmem_limit_bytes=VMEM_LIMIT),
    )(*args)


def col(height, kind=BF):
    return sds((height, MB_TOK), kind)


def attn_outputs():
    shapes = [
        col(D), col(1, F32), col(3 * D), sds((MB_TOK, D), BF), sds((MB_TOK, D), BF),
        col(HEADS, F32), col(D), col(D), col(1, F32), sds((PAD_BLK, D), BF), sds((PAD_BLK, D), BF),
    ]
    specs = [
        cols_spec(D), cols_spec(1), cols_spec(3 * D), rows_spec(D), rows_spec(D), cols_spec(HEADS),
        cols_spec(D), cols_spec(D), cols_spec(1), whole((PAD_BLK, D)), whole((PAD_BLK, D)),
    ]
    return shapes, specs


MLP_OUTS = ([sds((MB_TOK, D), BF), col(FF), col(FF)], [(D, 0), (FF, 1), (FF, 1)])


def weight_scratch(*weights):
    return [pltpu.VMEM(w.own.shape, BF) for w in weights] + [
        pltpu.SemaphoreType.DMA((len(weights),))
    ]


def flat(weights):
    return [ref for weight in weights for ref in weight.flat()]


def attn_scratch():
    return [pltpu.VMEM((D, TILE), BF)]


def forward_attn(meta, x, gains, wqkv, wout, layer):
    shapes, specs = attn_outputs()
    weights = (wqkv, wout)
    out = call(
        functools.partial(forward_attn_kernel, layer=layer, weights=weights), (N_TILE,),
        shapes + [col(D, F32), col(D)],
        [
            pl.BlockSpec((TILE, D), lambda t, m: (m[6] * N_TILE + t, 0)), whole((2, D)),
        ] + [ANY] * len(flat(weights)),
        specs + [cols_spec(D), cols_spec(D)],
        attn_scratch() + weight_scratch(*weights),
        (meta, x, gains, *flat(weights)),
    )
    return out[:11], out[11], out[12]


def forward_mlp(meta, hidden, second, wup, wdown, layer):
    weights = (wup, wdown)
    return call(
        functools.partial(forward_mlp_kernel, layer=layer, weights=weights), (N_TILE,),
        MLP_OUTS[0],
        [cols_spec(D), cols_spec(D)] + [ANY] * len(flat(weights)),
        [rows_spec(D), cols_spec(FF), cols_spec(FF)],
        weight_scratch(*weights),
        (meta, hidden, second, *flat(weights)),
    )


def mlp_scratch():
    return [
        pltpu.VMEM((FF, D), F32), pltpu.VMEM((FF, D), F32), pltpu.VMEM((D, D), F32),
        pltpu.VMEM((D, SPAN), F32),
    ]


def attn_back_scratch():
    return [
        pltpu.VMEM((3 * D, D), F32), pltpu.VMEM((D, SPAN), F32), pltpu.VMEM((D, PAD_BLK), F32),
        pltpu.VMEM((D, PAD_BLK), F32),
    ]


def mlp_back(meta, seed, act, gp, xh2, r2, att, gains, wdown, wup, wout, layer):
    weights = (wdown, wup, wout)
    half = 8 * (PART_A + PART_B)
    return call(
        functools.partial(mlp_back_kernel, layer=layer, weights=weights), (N_TILE,),
        [sds((half, D), BF), sds((half, D), BF), sds((1, D), F32), col(D, F32), col(D)],
        [
            rev_rows(D), rev_cols(FF), rev_cols(FF), rev_cols(D), rev_cols(1), rev_cols(D),
            whole((2, D)),
        ] + [ANY] * len(flat(weights)),
        [whole((half, D)), whole((half, D)), whole((1, D)), rev_cols(D), rev_cols(D)],
        mlp_scratch() + weight_scratch(*weights),
        (meta, seed, act, gp, xh2, r2, att, gains, *flat(weights)),
    )


def attn_back(meta, gh, gatt, xh1, r1, qkv, krow, vrow, lse, ks, vs, gains, gln2, wqkv, layer):
    half = 8 * PART_C
    return call(
        functools.partial(attn_back_kernel, layer=layer, weights=(wqkv,)), (N_TILE,),
        [sds((MB_TOK, D), BF), sds((half, D), BF), sds((half, D), BF)],
        [
            rev_cols(D), rev_cols(D), rev_cols(D), rev_cols(1), rev_cols(3 * D), rev_rows(D),
            rev_rows(D), rev_cols(HEADS), whole((PAD_BLK, D)), whole((PAD_BLK, D)), whole((2, D)),
            whole((1, D)),
        ] + [ANY] * len(wqkv.flat()),
        [rev_rows(D), whole((half, D)), whole((half, D))],
        attn_back_scratch() + [pltpu.VMEM((3 * D, TILE), F32)] + weight_scratch(wqkv),
        (meta, gh, gatt, xh1, r1, qkv, krow, vrow, lse, ks, vs, gains, gln2, *wqkv.flat()),
    )


def whole_layer(meta, x, cotangent, gains, wqkv, wout, wup, wdown, layer):
    weights = (wqkv, wout, wup, wdown)
    tiled = lambda *shape: pltpu.VMEM((N_TILE,) + shape, BF)
    sums, half = sds((16, PART_A + PART_B, D), BF), 8 * PART_C
    forth = lambda t: jnp.minimum(t, N_TILE - 1)
    back = lambda t, *_: (jnp.where(t < N_TILE, N_TILE - 1, 2 * N_TILE - 1 - t), 0)
    return call(
        functools.partial(layer_kernel, layer=layer, weights=weights), (2 * N_TILE,),
        [
            sds((MB_TOK, D), BF), sds((MB_TOK, D), BF), sums, sds((half, D), BF),
            sds((half, D), BF),
        ],
        [
            pl.BlockSpec((TILE, D), lambda t, *_: (forth(t), 0)),
            pl.BlockSpec((TILE, D), lambda t, m: (m[6] * N_TILE + forth(t), 0)),
            whole((2, D)),
        ] + [ANY] * len(flat(weights)),
        [
            pl.BlockSpec((TILE, D), lambda t, *_: (forth(t), 0)),
            pl.BlockSpec((TILE, D), back), ANY, whole((half, D)), whole((half, D)),
        ],
        [
            tiled(D, TILE), pltpu.VMEM((N_TILE, 1, TILE), F32), tiled(3 * D, TILE), tiled(TILE, D),
            tiled(TILE, D), pltpu.VMEM((N_TILE, HEADS, TILE), F32), pltpu.VMEM((D, TILE), BF),
            pltpu.VMEM((D, TILE), BF), pltpu.VMEM((1, TILE), F32), pltpu.VMEM((PAD_BLK, D), BF),
            pltpu.VMEM((PAD_BLK, D), BF), pltpu.VMEM((N_TILE, D, TILE), F32), tiled(D, TILE),
            pltpu.VMEM((FF, TILE), BF), pltpu.VMEM((FF, TILE), BF), pltpu.VMEM((D, TILE), BF),
            pltpu.VMEM((3 * D, TILE), F32),
        ] + mlp_scratch() + attn_back_scratch() + [
            pltpu.VMEM((16, PART_A + PART_B, D), BF),
        ] + weight_scratch(*weights) + [pltpu.SemaphoreType.DMA],
        (meta, x, cotangent, gains, *flat(weights)),
    )


def combine_kernel(meta_ref, *refs, count, cuts):
    values, outs = refs[:count], refs[count:]
    x, z = (meta_ref[7] >> 1) & 1, meta_ref[8]
    for out, (start, kind, k) in zip(outs, cuts):
        rows = out.shape[0]
        spot = {"x": x ^ k, "z": z ^ k, "all": 0}[kind]
        part = pl.ds(pl.multiple_of(start + spot * rows, 16), rows)
        total = values[0][part].astype(F32)
        for value in values[1:]:
            total = total + value[part].astype(F32)
        out[...] = total.astype(BF)


def combine(meta, values, cuts, work=0):
    return pl.pallas_call(
        functools.partial(
            combine_kernel, count=len(values), cuts=tuple((c[0],) + c[2:] for c in cuts)
        ),
        out_shape=tuple(sds((c[1], D), BF) for c in cuts),
        grid_spec=pltpu.PrefetchScalarGridSpec(
            num_scalar_prefetch=1, grid=(1,),
            in_specs=[part_spec(v.shape, (0, 0)) for v in values],
            out_specs=[part_spec((c[1], D), (0, 0)) for c in cuts],
        ),
        cost_estimate=pl.CostEstimate(flops=work, bytes_accessed=0, transcendentals=0),
        compiler_params=pltpu.CompilerParams(vmem_limit_bytes=VMEM_LIMIT // 4),
    )(meta, *values)


def by_x(start, rows):
    return [(start, rows, "x", 0), (start, rows, "x", 1)]


def by_z(start, rows):
    return [(start, rows, "z", k) for k in range(4)]


def finish_kernel(meta_ref, *refs, widths, targets, extra):
    pieces, refs = refs[:4], refs[4 + extra:]
    outs, held, sem = refs[:len(widths)], refs[-2], refs[-1]
    rows = held.shape[0] // 4
    for index, piece in enumerate(pieces):
        place = meta_ref[7] ^ index
        spot = (place & 1) * 2 + (place >> 1)
        pltpu.make_async_copy(
            piece, held.at[pl.ds(pl.multiple_of(spot * rows, rows), rows)], sem
        ).start()
    for index, piece in enumerate(pieces):
        pltpu.make_async_copy(piece, held.at[pl.ds(index * rows, rows)], sem).wait()
    total = sum(widths)
    for i, (width, flip) in enumerate(zip(widths, targets)):
        start = sum(widths[:i])
        value = jnp.concatenate(
            [held[pl.ds(s * total + start, width)] for s in range(16)], axis=0
        )
        outs[i][...] = (value.T if flip else value).astype(F32)


def finish(meta, pieces, widths, flips, shapes, specs, more=(), alias=None):
    rows = pieces[0].shape[0]
    return pl.pallas_call(
        functools.partial(finish_kernel, widths=widths, targets=flips, extra=len(more)),
        out_shape=tuple(sds(shape, F32) for shape in shapes),
        grid_spec=pltpu.PrefetchScalarGridSpec(
            num_scalar_prefetch=1, grid=(1,), in_specs=[ANY] * (4 + len(more)), out_specs=specs,
            scratch_shapes=[pltpu.VMEM((4 * rows, D), BF), pltpu.SemaphoreType.DMA],
        ),
        input_output_aliases=alias or {},
        compiler_params=pltpu.CompilerParams(vmem_limit_bytes=VMEM_LIMIT),
    )(meta, *pieces, *more)


def part_spec(shape, index):
    return pl.BlockSpec(shape, lambda t, *_: index)


def swap_xor(value, mask):
    size = lax.axis_size("dp")
    return lax.ppermute(value, "dp", [(i, i ^ mask) for i in range(size)])


def swap_section(value):
    return lax.ppermute(value, "section", [(0, 1), (1, 0)])


def to_section(value, target):
    return lax.ppermute(value, "section", [(1 - target, target)])


def exchange(value0, value1):
    return swap_section(jnp.where(lax.axis_index("section") == 0, value1, value0))


def low_groups():
    size = lax.axis_size("dp")
    return None if size == 16 else [list(range(i, i + 16)) for i in range(0, size, 16)]


def added(*values):
    total = values[0].astype(F32)
    for value in values[1:]:
        total = total + value.astype(F32)
    return total.astype(BF)


def halves(value, bit):
    half = value.shape[0] // 2
    mine = (lax.axis_index("dp") >> bit) & 1
    return (
        lax.dynamic_slice_in_dim(value, mine * half, half, 0),
        lax.dynamic_slice_in_dim(value, (1 - mine) * half, half, 0),
    )


def half_sum(pair, bit):
    return added(pair[0], swap_xor(pair[1], 1 << bit))


def quarters(value, bit):
    rows = value.shape[0] // 4
    mine = (lax.axis_index("dp") >> bit) & 3
    return tuple(lax.dynamic_slice_in_dim(value, (mine ^ k) * rows, rows, 0) for k in range(4))


def swap_quarters(parts, bit):
    return [swap_xor(parts[k], k << bit) for k in (1, 2, 3)]


def quarter_sum(parts, bit):
    return added(parts[0], *swap_quarters(parts, bit))


def tie(*values):
    return lax.optimization_barrier(values)


def rest_bits():
    return range(4, lax.axis_size("dp").bit_length() - 1)


def reduce_core(halves):
    return added(halves[1], swap_xor(halves[0], 1))


def reduce_rest(value):
    for bit in rest_bits():
        value = half_sum(halves(value, bit), bit)
    return value


def gather_bit(value, bit):
    mine = (lax.axis_index("dp") >> bit) & 1
    other = swap_xor(value, 1 << bit)
    return jnp.where(
        mine == 0,
        jnp.concatenate([value, other], axis=0),
        jnp.concatenate([other, value], axis=0),
    )


def gather_quad(value, bit):
    mine = (lax.axis_index("dp") >> bit) & 3
    got = [value] + [swap_xor(value, k << bit) for k in (1, 2, 3)]
    parts = []
    for p in range(4):
        which = mine ^ p
        part = got[3]
        for k in (2, 1, 0):
            part = jnp.where(which == k, got[k], part)
        parts.append(part)
    return jnp.concatenate(parts, axis=0)


def gather_rest(value):
    for bit in reversed(rest_bits()):
        value = gather_bit(value, bit)
    return value


def spread_pieces(value):
    across = swap_xor(value, 2)
    return value, swap_xor(value, 1), across, swap_xor(across, 1)


def sum_rest(value):
    for bit in rest_bits():
        value = added(value, swap_xor(value, 1 << bit))
    return value


def per_device(
    tokens, cotangent, span_counts, tail_lens, ln1_gain, w_qkv, w_out, ln2_gain, w_up, w_down
):
    section = lax.axis_index("section")
    first = section == 0
    place = lax.axis_index("dp") & 3
    meta = jnp.concatenate([
        lax.dynamic_index_in_dim(span_counts, section, 0, keepdims=False),
        lax.dynamic_index_in_dim(tail_lens, section, 0, keepdims=False),
        section.astype(jnp.int32)[None], place.astype(jnp.int32)[None],
        ((lax.axis_index("dp") >> 2) & 3).astype(jnp.int32)[None],
    ])
    own = (w_qkv[0], w_out[0], w_up[0], w_down[0])

    def part(weight, spot, count):
        rows = weight.shape[0] // count
        return lax.dynamic_slice_in_dim(weight, spot * rows, rows, 0)

    own_gains = jnp.concatenate([ln1_gain, ln2_gain], axis=0)
    attn = swap_section(
        jnp.concatenate([part(own[0], place, 4), part(own[1], place, 4)], axis=1)
    )
    other_gains = swap_section(own_gains)
    attn, other_gains = tie(attn, other_gains)
    gains = [jnp.where(first, own_gains, other_gains), jnp.where(first, other_gains, own_gains)]
    attn_x = swap_xor(attn, 2)
    attn = (attn, swap_xor(attn, 1), attn_x, swap_xor(attn_x, 1))
    wqkv, wout = Weight(own[0], (attn, 0, 0, None)), Weight(own[1], (attn, 3 * D, 0, None))
    up = swap_section(part(own[2], place, 4))
    down = swap_section(part(own[3], place & 1, 2))
    up_x, up_c = swap_xor(up, 2), swap_xor(up, 1)

    keep0, hidden, second = forward_attn(meta, tokens, gains[0], wqkv, wout, 0)
    keep0, hidden, second, up_x, up_c, down = tie(keep0, hidden, second, up_x, up_c, down)
    wup = Weight(own[2], ((up, up_c, up_x, swap_xor(up_x, 1)), 0, 0, None))
    wdown = Weight(own[3], ((down, swap_xor(down, 1)), 0, 0, None))
    act_out0, act0, gp0 = forward_mlp(meta, hidden, second, wup, wdown, 0)
    act_out1, ig1, sums1, send1, kept1 = whole_layer(
        meta, act_out0, cotangent, gains[1], wqkv, wout, wup, wdown, 1
    )
    cut = 2 * MB_TOK // 3
    acts_a = exchange(act_out0[:cut], act_out1[:cut])
    sums1 = lax.psum_scatter(
        sums1.reshape(-1, D), "dp", scatter_dimension=0, axis_index_groups=low_groups(), tiled=True
    )
    xh1, r1, qkv, krow, vrow, lse, att, xh2, r2, ks, vs = keep0
    back = mlp_back(meta, ig1, act0, gp0, xh2, r2, att, gains[0], wdown, wup, wout, 0)
    c1 = swap_xor(send1, 1)
    (send, kept, gln2, gh, gatt), acts_a, act_out0, act_out1, c1 = tie(
        back, acts_a, act_out0, act_out1, c1
    )
    mlp0 = combine(
        meta, (kept, swap_xor(send, 1)), by_x(0, 4 * PART_A) + by_z(8 * PART_A, 2 * PART_B)
    )
    a0, b0 = mlp0[:2], mlp0[2:]
    gh, a0, b0 = tie(gh, a0, b0)
    acts_b = exchange(act_out0[cut:], act_out1[cut:])
    a0_x, b0_z = swap_xor(a0[1], 2), swap_quarters(b0, 2)
    back = attn_back(
        meta, gh, gatt, xh1, r1, qkv, krow, vrow, lse, ks, vs, gains[0], gln2, wqkv, 0
    )
    (ig0, send, kept), a0_x, b0_z, acts_b = tie(back, a0_x, b0_z, acts_b)
    acts_in = jnp.concatenate([acts_a, acts_b], axis=0)
    c0 = swap_xor(send, 1)
    a0 = [added(*pair) for pair in zip(quarters(a0[0], 2), quarters(a0_x, 2))]
    a0, c0 = tie(a0, c0)
    a0_z = swap_quarters(a0, 2)
    c0 = combine(meta, (kept, c0), by_x(0, 4 * PART_C), OVERLAPPED)
    c1 = combine(meta, (kept1, c1), by_x(0, 4 * PART_C))
    b0 = halves(added(b0[0], *b0_z), 1)
    bc_x = swap_xor(jnp.concatenate([b0[1], c0[1], c1[1]], axis=0), 2)

    def own_sum(grad0, grad1):
        return added(jnp.where(first, grad0, grad1), swap_section(jnp.where(first, grad1, grad0)))

    bc_x, sums1 = tie(bc_x, sums1)
    cut = PART_B + 4 * PART_C
    b0 = added(b0[0], bc_x[:PART_B])
    c0 = quarters(added(c0[0], bc_x[PART_B:cut]), 2)
    c1 = quarters(added(c1[0], bc_x[cut:]), 2)
    c = [jnp.concatenate(pair, axis=0) for pair in zip(c0, c1)]
    c_z = swap_quarters(c, 2)
    a0_z, b0, c_1 = tie(a0_z, b0, c[1])
    (a0,) = combine(meta, (a0[0], *a0_z), [(0, PART_A, "all", 0)], OVERLAPPED)
    a1, b1 = sums1[:PART_A], sums1[PART_A:]
    ab0 = jnp.concatenate([reduce_rest(a0), reduce_rest(b0)], axis=0)
    ab1 = jnp.concatenate([reduce_rest(a1), reduce_rest(b1)], axis=0)
    ab = jnp.where(first, ab0, ab1), swap_section(jnp.where(first, ab1, ab0))
    if rest_bits():
        ab = added(*ab)
        a_rows = ab.shape[0] * PART_A // (PART_A + PART_B)
        a_own, b_own = ab[:a_rows], ab[a_rows:]
    else:
        a_own, b_own = combine(
            meta, ab, [(0, PART_A, "all", 0), (PART_A, PART_B, "all", 0)], OVERLAPPED
        )
    a_own, b_own, c_z = tie(a_own, b_own, c_z)
    a_full = gather_quad(gather_rest(a_own), 2)
    c = added(c[0], *c_z)
    c_own = own_sum(*[
        jnp.concatenate([reduce_rest(v[:QKV_ROWS]), sum_rest(v[QKV_ROWS:])], axis=0)
        for v in (c[:PART_C], c[PART_C:])
    ])
    c_own, ig0 = tie(c_own, ig0)
    grads_in = exchange(ig0, ig1)
    lns = c_own[-GAIN_ROWS:][:2].astype(F32)
    bc_own = jnp.concatenate([gather_rest(b_own), gather_rest(c_own[:-GAIN_ROWS])], axis=0)
    def assemble(value0, value1, got):
        return jnp.concatenate(
            [jnp.where(first, value0, got), jnp.where(first, got, value1)], axis=0
        )

    activations = assemble(act_out0, act_out1, acts_in)
    input_grads = assemble(ig0, ig1, grads_in)
    a_full, bc_own = tie(a_full, bc_own)
    a_pieces = spread_pieces(a_full)
    bc_full = gather_quad(bc_own, 2)
    grads_a = finish(
        meta, a_pieces, (DOWN_ROWS, UP_A // 16, OUT_ROWS), (False, True, False),
        [(FF, D), (D, FF), (D, D)],
        [
            part_spec((FF, D), (0, 0)), part_spec((D, UP_A), (0, UP_B // UP_A)),
            part_spec((D, D), (0, 0)),
        ],
    )
    across, activations, input_grads, grads_a = tie(
        swap_xor(bc_full, 2), activations, input_grads, grads_a
    )
    grad_down, grad_up, grad_out = grads_a
    bc_pieces = (bc_full, swap_xor(bc_full, 1), across, swap_xor(across, 1))
    grad_up, grad_qkv = finish(
        meta, bc_pieces, (UP_B // 16, QKV_ROWS), (True, True), [(D, FF), (D, 3 * D)],
        [part_spec((D, UP_B), (0, 0)), part_spec((D, 3 * D), (0, 0))],
        (grad_up,), {5: 0},
    )

    return (
        activations[None],
        input_grads[None],
        lns[:1],
        grad_qkv[None],
        grad_out[None],
        lns[1:],
        grad_up[None],
        grad_down[None],
    )


def solution(mesh):
    return jax.shard_map(
        per_device,
        mesh=mesh,
        in_specs=(
            P("dp", None),
            P("dp", None),
            P("dp", None),
            P("dp", None),
            P("section", None),
            P("section", None, None),
            P("section", None, None),
            P("section", None),
            P("section", None, None),
            P("section", None, None),
        ),
        out_specs=(
            P("section", "dp", None),
            P("section", "dp", None),
            P("section", None),
            P("section", None, None),
            P("section", None, None),
            P("section", None),
            P("section", None, None),
            P("section", None, None),
        ),
        check_vma=False,
    )
```

```python
import functools

import jax
import jax.numpy as jnp
from jax import lax
from jax.experimental import pallas as pl
from jax.experimental.pallas import tpu as pltpu
from jax.sharding import PartitionSpec as P

D = 512
HEADS = 8
HEAD_DIM = 64
FF = 2048
SPAN = 128
MB_BLK = 12
MB_TOK = MB_BLK * SPAN
PAD_BLK = 16
EPSILON = 1e-05
NEG_FILL = -1e30
BF = jnp.bfloat16
F32 = jnp.float32
VMEM_LIMIT = 58 * 2**20

TILE = 512
TILE_BLK = TILE // SPAN
N_TILE = MB_TOK // TILE
FF_STEP = 512
FWD_STEP = 512
FWD_GROUP = 2
BACK_GROUP = 2


def dot(left, right, left_dim, right_dim):
    return lax.dot_general(
        left, right, (((left_dim,), (right_dim,)), ((), ())), preferred_element_type=F32
    )


def block_facts(meta_ref, block):
    end_one = meta_ref[0]
    end_two = end_one + meta_ref[1]
    in_one = block < end_one
    in_two = block < end_two
    first = jnp.where(in_one, 0, jnp.where(in_two, end_one, end_two))
    last = jnp.where(in_one, end_one, jnp.where(in_two, end_two, MB_BLK)) - 1
    tail = jnp.where(in_one, meta_ref[3], jnp.where(in_two, meta_ref[4], meta_ref[5]))
    filled = jnp.where(block == last, tail, SPAN)
    return filled, first


def filled_column(meta_ref, width):
    rows = lax.broadcasted_iota(jnp.int32, (PAD_BLK, width), 0)
    out = jnp.full((PAD_BLK, width), SPAN, jnp.int32)
    for block in range(MB_BLK):
        filled, _ = block_facts(meta_ref, block)
        out = jnp.where(rows == block, filled, out)
    return out.astype(F32)


def filled_row(meta_ref):
    cols = lax.broadcasted_iota(jnp.int32, (1, PAD_BLK), 1)
    out = jnp.full((1, PAD_BLK), SPAN, jnp.int32)
    for block in range(MB_BLK):
        filled, _ = block_facts(meta_ref, block)
        out = jnp.where(cols == block, filled, out)
    return out.astype(F32)


def member_mask(meta_ref, tile_start):
    parts = []
    rows = lax.broadcasted_iota(jnp.int32, (PAD_BLK, SPAN), 0)
    cols = lax.broadcasted_iota(jnp.int32, (PAD_BLK, SPAN), 1)
    for j in range(TILE_BLK):
        block = tile_start + j
        filled, _ = block_facts(meta_ref, block)
        parts.append(jnp.where((rows == block) & (cols < filled), 1.0, 0.0).astype(BF))
    return jnp.concatenate(parts, axis=1)


def pair_diag(rows_two):
    zero = jnp.zeros((HEAD_DIM, SPAN), rows_two.dtype)
    top = jnp.concatenate([rows_two[:HEAD_DIM], zero], axis=1)
    low = jnp.concatenate([zero, rows_two[HEAD_DIM:]], axis=1)
    return jnp.concatenate([top, low], axis=0)


def diag_rows(square):
    return jnp.concatenate([square[:HEAD_DIM, :SPAN], square[HEAD_DIM:, SPAN:]], axis=0)


def gain_column(gains_ref, index):
    return jnp.broadcast_to(gains_ref[index:index + 1], (SPAN, D)).T


def times_gain(values, gain):
    return jnp.concatenate(
        [values[:, i * SPAN:(i + 1) * SPAN] * gain for i in range(values.shape[1] // SPAN)], axis=1
    )


def normalize(values):
    mean = jnp.sum(values, axis=0, keepdims=True) * (1.0 / D)
    center = values - mean
    spread = jnp.sum(center * center, axis=0, keepdims=True) * (1.0 / D)
    factor = lax.rsqrt(spread + EPSILON)
    return center * factor, factor


def score_mask(block, filled, first):
    rows = lax.broadcasted_iota(jnp.int32, (SPAN + PAD_BLK, 2 * SPAN), 0)
    cols = lax.broadcasted_iota(jnp.int32, (SPAN + PAD_BLK, 2 * SPAN), 1) % SPAN
    local = (rows <= cols) & (rows < filled)
    earlier = (rows >= SPAN + first) & (rows < SPAN + block)
    return local | earlier


def attention_items(meta_ref, tile_start, blocks):
    items = []
    for j in blocks:
        filled, first = block_facts(meta_ref, tile_start + j)
        mask = score_mask(tile_start + j, filled, first)
        for hp in range(HEADS // 2):
            items.append((slice(j * SPAN, (j + 1) * SPAN), hp, slice(hp * SPAN, (hp + 1) * SPAN), mask))
    return items


class Weight:
    def __init__(self, own, *groups):
        self.own = own
        self.groups = [(tuple(p), lane, at, width or own.shape[1]) for p, lane, at, width in groups]

    def flat(self):
        return (self.own,) + sum((group[0] for group in self.groups), ())

    def bind(self, refs):
        own, refs, groups = refs[0], refs[1:], []
        for pieces, *rest in self.groups:
            groups.append((refs[:len(pieces)], *rest))
            refs = refs[len(pieces):]
        return Weight(own, *groups), refs


def start_weight(meta_ref, layer, weight, target, sem):
    @pl.when(meta_ref[6] == layer)
    def _():
        pltpu.make_async_copy(weight.own, target, sem).start()

    @pl.when(meta_ref[6] != layer)
    def _():
        for pieces, lane, at, width in weight.groups:
            count = len(pieces)
            rows = target.shape[0] // count
            for index, piece in enumerate(pieces):
                spot = (meta_ref[7] & (count - 1)) ^ index
                pltpu.make_async_copy(
                    piece.at[:, pl.ds(lane, width)],
                    target.at[pl.ds(pl.multiple_of(spot * rows, rows), rows), pl.ds(at, width)], sem,
                ).start()


def wait_weight(weight, target, sem):
    pltpu.make_async_copy(weight.own, target, sem).wait()


def forward_attn_part(meta_ref, tile, x_ref, gains_ref, outs, scratch, wqkv_ref, wout_ref, wait):
    (xh1_ref, r1_ref, qkv_ref, krow_ref, vrow_ref, lse_ref, att_ref, xh2_ref, r2_ref, ks_ref,
     vs_ref) = outs
    (attf_ref,) = scratch
    tile_start = tile * TILE_BLK

    @pl.when(tile == 0)
    def _():
        ks_ref[...] = jnp.zeros_like(ks_ref)
        vs_ref[...] = jnp.zeros_like(vs_ref)

    x_t = x_ref[...].T.astype(F32)
    xhat, r1 = normalize(x_t)
    xh1_ref[...] = xhat.astype(BF)
    r1_ref[...] = r1
    normed = times_gain(xhat, gain_column(gains_ref, 0)).astype(BF)
    wait(0)
    q_t = (dot(wqkv_ref[:, :D], normed, 0, 0) * HEAD_DIM ** (-0.5)).astype(BF)
    k_t = dot(wqkv_ref[:, D:2 * D], normed, 0, 0).astype(BF)
    v_t = dot(wqkv_ref[:, 2 * D:], normed, 0, 0).astype(BF)
    qkv_ref[:D] = q_t
    qkv_ref[D:2 * D] = k_t
    qkv_ref[2 * D:] = v_t
    krow = k_t.T
    vrow = v_t.T
    krow_ref[...] = krow
    vrow_ref[...] = vrow
    members = member_mask(meta_ref, tile_start)
    fill = filled_column(meta_ref, D)
    block_rows = lax.broadcasted_iota(jnp.int32, (PAD_BLK, D), 0)
    fresh = (block_rows >= tile_start) & (block_rows < tile_start + TILE_BLK)
    key_sums = jnp.where(fresh, (dot(members, krow, 1, 0) / fill).astype(BF), ks_ref[...])
    value_sums = jnp.where(fresh, (dot(members, vrow, 1, 0) / fill).astype(BF), vs_ref[...])
    ks_ref[...] = key_sums
    vs_ref[...] = value_sums
    vs_t = value_sums.T
    for j in range(0, TILE_BLK, FWD_GROUP):
        items = attention_items(meta_ref, tile_start, range(j, j + FWD_GROUP))
        scores = [
            dot(
                jnp.concatenate([krow[cols, feats], key_sums[:, feats]], axis=0),
                pair_diag(q_t[feats, cols]), 1, 0,
            )
            for cols, _, feats, _ in items
        ]
        probs = []
        for (cols, hp, feats, mask), score in zip(items, scores):
            score = jnp.where(mask, score, NEG_FILL)
            top = jnp.max(score, axis=0, keepdims=True)
            prob = jnp.exp(score - top)
            total = jnp.sum(prob, axis=0, keepdims=True)
            logs = top + jnp.log(total)
            lse_ref[2 * hp:2 * hp + 1, cols] = logs[:, :SPAN]
            lse_ref[2 * hp + 1:2 * hp + 2, cols] = logs[:, SPAN:]
            probs.append((prob * (1.0 / total)).astype(BF))
        for (cols, _, feats, _), prob in zip(items, probs):
            values = jnp.concatenate([v_t[feats, cols], vs_t[feats]], axis=1)
            attf_ref[feats, cols] = diag_rows(dot(values, prob, 1, 0)).astype(BF)
    att = attf_ref[...]
    att_ref[...] = att
    wait(1)
    hidden = x_t + dot(wout_ref[...], att, 0, 0)
    xhat2, r2 = normalize(hidden)
    xh2_ref[...] = xhat2.astype(BF)
    r2_ref[...] = r2
    return hidden, times_gain(xhat2, gain_column(gains_ref, 1)).astype(BF)


def forward_mlp_part(hidden, second, outs, wup_ref, wdown_ref):
    out_ref, act_ref, gp_ref = outs
    total_out = hidden
    up = dot(wup_ref[:, :FWD_STEP], second, 0, 0)
    for f in range(FF // FWD_STEP):
        part = slice(f * FWD_STEP, (f + 1) * FWD_STEP)
        later = slice((f + 1) * FWD_STEP, (f + 2) * FWD_STEP)
        ahead = dot(wup_ref[:, later], second, 0, 0) if later.stop <= FF else None
        bell = jnp.exp(up * up * -0.5)
        phi = 0.5 + 0.5 * lax.erf(up * (0.5 ** 0.5))
        act = (up * phi).astype(BF)
        act_ref[part] = act
        gp_ref[part] = (phi + up * bell * 0.3989422804014327).astype(BF)
        total_out = total_out + dot(wdown_ref[part], act, 0, 0)
        up = ahead
    out_ref[...] = total_out.astype(BF).T


def weight_waits(meta_ref, layer, weights, targets, sems):
    begin = pl.program_id(0) == 0

    @pl.when(begin)
    def _():
        for i, (weight, target) in enumerate(zip(weights, targets)):
            start_weight(meta_ref, layer, weight, target, sems.at[i])

    def wait(i):
        @pl.when(begin)
        def _():
            wait_weight(weights[i], targets[i], sems.at[i])

    return wait


def bound(weights, refs):
    out = []
    for weight in weights:
        weight, refs = weight.bind(refs)
        out.append(weight)
    return out, refs


def forward_attn_kernel(meta_ref, x_ref, gains_ref, *refs, layer, weights):
    weights, refs = bound(weights, refs)
    attn_outs, (hid_ref, sec_ref), scratch, targets, sems = (
        refs[:11], refs[11:13], refs[13:14], refs[14:16], refs[16]
    )
    wait = weight_waits(meta_ref, layer, weights, targets, sems)
    hidden, second = forward_attn_part(
        meta_ref, pl.program_id(0), x_ref, gains_ref, attn_outs, scratch, targets[0], targets[1], wait
    )
    hid_ref[...] = hidden
    sec_ref[...] = second


def forward_mlp_kernel(meta_ref, hid_ref, sec_ref, *refs, layer, weights):
    weights, refs = bound(weights, refs)
    outs, targets, sems = refs[:3], refs[3:5], refs[5]
    wait = weight_waits(meta_ref, layer, weights, targets, sems)
    wait(0)
    wait(1)
    forward_mlp_part(hid_ref[...], sec_ref[...], outs, *targets)


def write_halves(meta_ref, parts, send_ref, keep_ref, start=0, z_first=False):
    core = meta_ref[7] & 1
    total = sum(rows for _, _, rows in parts)
    for target, side in ((send_ref, 1 - core), (keep_ref, core)):
        for s in range(8):
            spot = start + ((s % 4) * 2 + s // 4 if z_first else s) * total
            for acc, base, rows in parts:
                if acc.shape[0] == rows:
                    value = acc[...]
                else:
                    first = base + pl.multiple_of(side * (8 * rows), 8 * rows) + s * rows
                    value = acc[pl.ds(first, rows)]
                target[pl.ds(spot, rows)] = value.astype(BF)
                spot += rows


def write_shards(parts, target):
    for place in range(16):
        s = (place & 1) * 8 + ((place >> 1) & 1) * 4 + (place >> 2)
        spot = 0
        for acc, base, rows in parts:
            value = acc[...] if acc.shape[0] == rows else acc[pl.ds(base + s * rows, rows)]
            target[place, pl.ds(spot, rows)] = value.astype(BF)
            spot += rows


DOWN_ROWS, OUT_ROWS, QKV_ROWS, GAIN_ROWS = FF // 16, D // 16, 3 * D // 16, 16
UP_A = FF // 2
UP_B = FF - UP_A
PART_A, PART_B = DOWN_ROWS + UP_A // 16 + OUT_ROWS, UP_B // 16
PART_C = QKV_ROWS + GAIN_ROWS
OVERLAPPED = 4 * 10**9


def norm_back(grad, gain, xhat, factor, gln_acc):
    prod = grad * xhat
    for j in range(TILE_BLK):
        gln_acc[...] += prod[:, j * SPAN:(j + 1) * SPAN]
    scaled = times_gain(grad, gain)
    mean = jnp.sum(scaled, axis=0, keepdims=True) * (1.0 / D)
    mean_x = jnp.sum(scaled * xhat, axis=0, keepdims=True) * (1.0 / D)
    return factor * (scaled - mean - xhat * mean_x)


def masked_low(meta_ref, tile, low):
    parts = []
    cols = lax.broadcasted_iota(jnp.int32, (D, SPAN), 1)
    for j in range(TILE_BLK):
        filled, _ = block_facts(meta_ref, tile * TILE_BLK + j)
        part = low[:, j * SPAN:(j + 1) * SPAN]
        parts.append(jnp.where(cols < filled, part, jnp.zeros((), BF)))
    return jnp.concatenate(parts, axis=1)


def zero_all(refs):
    for ref in refs:
        ref[...] = jnp.zeros_like(ref)


def mlp_back_part(low, data, gains_ref, weights, accs, wait, gh_ref, gatt_ref):
    act_ref, gp_ref, xh2_ref, r2_ref, att_ref = data
    wdown_ref, wup_ref, wout_ref = weights
    gdown_acc, gup_acc, gout_acc, gln_acc = accs
    gain = gain_column(gains_ref, 1)
    xhat = xh2_ref[...].astype(F32)
    second = times_gain(xhat, gain).astype(BF)
    wait(0)
    wait(1)
    e = None
    for f in range(FF // FF_STEP):
        part = slice(f * FF_STEP, (f + 1) * FF_STEP)
        gdown_acc[part] += dot(act_ref[part], low, 1, 1)
        ga = dot(wdown_ref[part], low, 1, 0)
        gui = (ga * gp_ref[part].astype(F32)).astype(BF)
        gup_acc[part] += dot(gui, second, 1, 1)
        term = dot(wup_ref[:, part], gui, 1, 0)
        e = term if e is None else e + term
    gh = low.astype(F32) + norm_back(e, gain, xhat, r2_ref[...], gln_acc)
    gh_ref[...] = gh
    ghb = gh.astype(BF)
    gout_acc[...] += dot(att_ref[...], ghb, 1, 1)
    wait(2)
    gatt_ref[...] = dot(wout_ref[...], ghb, 1, 0).astype(BF)


def mlp_parts(gdown_acc, gup_acc, gout_acc):
    part_a = ((gdown_acc, 0, DOWN_ROWS), (gup_acc, UP_B, UP_A // 16), (gout_acc, 0, OUT_ROWS))
    return part_a, ((gup_acc, 0, UP_B // 16),)


def mlp_back_kernel(
    meta_ref, seed_ref, act_ref, gp_ref, xh2_ref, r2_ref, att_ref, gains_ref, *refs, layer, weights,
):
    weights, refs = bound(weights, refs)
    (send_ref, keep_ref, gln_ref, gh_ref, gatt_ref, gdown_acc, gup_acc, gout_acc, gln_acc,
     wdown_ref, wup_ref, wout_ref, sems) = refs
    step = pl.program_id(0)
    targets = (wdown_ref, wup_ref, wout_ref)
    accs = (gdown_acc, gup_acc, gout_acc, gln_acc)
    wait = weight_waits(meta_ref, layer, weights, targets, sems)

    @pl.when(step == 0)
    def _():
        zero_all(accs)

    mlp_back_part(
        seed_ref[...].T, (act_ref, gp_ref, xh2_ref, r2_ref, att_ref), gains_ref, targets, accs, wait,
        gh_ref, gatt_ref,
    )

    @pl.when(step == N_TILE - 1)
    def _():
        part_a, part_b = mlp_parts(*accs[:3])
        write_halves(meta_ref, part_a, send_ref, keep_ref)
        write_halves(meta_ref, part_b, send_ref, keep_ref, 8 * PART_A, True)
        gln_ref[...] = jnp.sum(gln_acc[...].T, axis=0, keepdims=True)


def attn_back_part(meta_ref, tile, gh_ref, gatt_ref, data, gains_ref, wqkv_ref, accs, rows_ref, wait):
    xh1_ref, r1_ref, qkv_ref, krow_ref, vrow_ref, lse_ref, ks_ref, vs_ref = data
    gqkv_acc, gln_acc, gks_acc, gvs_acc = accs
    tile_start = tile * TILE_BLK
    q_t = qkv_ref[:D]
    gatt = gatt_ref[...]
    key_sums, value_sums = ks_ref[...], vs_ref[...]
    ks_t = key_sums.T
    for j in range(0, TILE_BLK, BACK_GROUP):
        items = attention_items(meta_ref, tile_start, range(j, j + BACK_GROUP))
        q_diags = [pair_diag(q_t[feats, cols]) for cols, _, feats, _ in items]
        g_diags = [pair_diag(gatt[feats, cols]) for cols, _, feats, _ in items]
        scores = [
            dot(jnp.concatenate([krow_ref[cols, feats], key_sums[:, feats]], axis=0), q, 1, 0)
            for (cols, _, feats, _), q in zip(items, q_diags)
        ]
        dps = [
            dot(jnp.concatenate([vrow_ref[cols, feats], value_sums[:, feats]], axis=0), g, 1, 0)
            for (cols, _, feats, _), g in zip(items, g_diags)
        ]
        grads, probs = [], []
        for (cols, hp, feats, mask), score, dp in zip(items, scores, dps):
            logs = jnp.concatenate(
                [lse_ref[2 * hp:2 * hp + 1, cols], lse_ref[2 * hp + 1:2 * hp + 2, cols]], axis=1
            )
            prob = jnp.exp(jnp.where(mask, score, NEG_FILL) - logs)
            weighted = prob * dp
            delta = jnp.sum(weighted, axis=0, keepdims=True)
            grads.append((weighted - prob * delta).astype(BF))
            probs.append(prob.astype(BF))
        for (cols, hp, feats, _), grad, prob, q, g in zip(items, grads, probs, q_diags, g_diags):
            key_feats = slice(D + hp * SPAN, D + (hp + 1) * SPAN)
            value_feats = slice(2 * D + hp * SPAN, 2 * D + (hp + 1) * SPAN)
            keys = jnp.concatenate([qkv_ref[key_feats, cols], ks_t[feats]], axis=1)
            rows_ref[feats, cols] = diag_rows(dot(keys, grad, 1, 0))
            key_grad = dot(q, grad, 1, 1)
            value_grad = dot(g, prob, 1, 1)
            rows_ref[key_feats, cols] = key_grad[:, :SPAN]
            rows_ref[value_feats, cols] = value_grad[:, :SPAN]
            gks_acc[feats] += key_grad[:, SPAN:]
            gvs_acc[feats] += value_grad[:, SPAN:]
    members = member_mask(meta_ref, tile_start)
    fill = filled_row(meta_ref)

    def spread_back(acc_ref):
        back = (acc_ref[...].astype(BF).astype(F32) / fill).astype(BF)
        return dot(back, members, 1, 0)

    grad_q = rows_ref[:D] * HEAD_DIM ** (-0.5)
    grad_k = rows_ref[D:2 * D] + spread_back(gks_acc)
    grad_v = rows_ref[2 * D:] + spread_back(gvs_acc)
    gain = gain_column(gains_ref, 0)
    xhat = xh1_ref[...].astype(F32)
    normed = times_gain(xhat, gain).astype(BF)
    wait(0)
    e = None
    for i, rows in enumerate((grad_q, grad_k, grad_v)):
        rows = rows.astype(BF)
        part = slice(i * D, (i + 1) * D)
        gqkv_acc[part] += dot(rows, normed, 1, 1)
        term = dot(wqkv_ref[:, part], rows, 1, 0)
        e = term if e is None else e + term
    return (gh_ref[...] + norm_back(e, gain, xhat, r1_ref[...], gln_acc)).astype(BF).T


def gain_rows(gln_acc, gln2):
    gln = jnp.sum(gln_acc[...].T, axis=0, keepdims=True)
    rest = jnp.zeros((GAIN_ROWS - 2, D), F32)
    return jnp.concatenate([gln, gln2, rest], axis=0).astype(BF)


def attn_back_kernel(
    meta_ref, gh_ref, gatt_ref, xh1_ref, r1_ref, qkv_ref, krow_ref, vrow_ref, lse_ref, ks_ref,
    vs_ref, gains_ref, gln2_ref, *refs, layer, weights,
):
    weights, refs = bound(weights, refs)
    (gin_ref, send_ref, keep_ref, gqkv_acc, gln_acc, gks_acc, gvs_acc, rows_ref, wqkv_ref,
     sems) = refs
    step = pl.program_id(0)
    wait = weight_waits(meta_ref, layer, weights, (wqkv_ref,), sems)
    accs = (gqkv_acc, gln_acc, gks_acc, gvs_acc)

    @pl.when(step == 0)
    def _():
        zero_all(accs)

    data = (xh1_ref, r1_ref, qkv_ref, krow_ref, vrow_ref, lse_ref, ks_ref, vs_ref)
    gin_ref[...] = attn_back_part(
        meta_ref, N_TILE - 1 - step, gh_ref, gatt_ref, data, gains_ref, wqkv_ref, accs, rows_ref, wait
    )

    @pl.when(step == N_TILE - 1)
    def _():
        parts = ((gqkv_acc, 0, QKV_ROWS), (gain_rows(gln_acc, gln2_ref[...]), 0, GAIN_ROWS))
        write_halves(meta_ref, parts, send_ref, keep_ref)


def layer_kernel(meta_ref, x_ref, cot_ref, gains_ref, *refs, layer, weights):
    weights, refs = bound(weights, refs)
    out_ref, gin_ref, sums_ref, send_ref, keep_ref, *refs = refs
    keep, refs = refs[:13], refs[13:]
    (xh1, r1, qkv, krow, vrow, lse, att_ref, xh2_ref, r2_ref, ks_ref, vs_ref, gh, gatt) = keep
    act_ref, gp_ref, attf_ref, rows_ref, *refs = refs
    mlp_accs, attn_accs, refs = refs[:4], refs[4:8], refs[8:]
    held_mlp, *refs = refs
    targets, sems, copied = refs[:4], refs[4], refs[5]
    wqkv_ref, wout_ref, wup_ref, wdown_ref = targets
    step = pl.program_id(0)
    wait = weight_waits(meta_ref, layer, weights, targets, sems)
    copy = pltpu.make_async_copy(held_mlp, sums_ref, copied)

    @pl.when(step == 0)
    def _():
        zero_all(mlp_accs)
        zero_all(attn_accs)

    @pl.when(step < N_TILE)
    def _():
        tile = step
        outs = (
            xh1.at[tile], r1.at[tile], qkv.at[tile], krow.at[tile], vrow.at[tile], lse.at[tile],
            att_ref, xh2_ref, r2_ref, ks_ref, vs_ref,
        )
        hidden, second = forward_attn_part(
            meta_ref, tile, x_ref, gains_ref, outs, (attf_ref,), wqkv_ref, wout_ref, wait
        )
        wait(2)
        wait(3)
        forward_mlp_part(hidden, second, (out_ref, act_ref, gp_ref), wup_ref, wdown_ref)
        mlp_back_part(
            masked_low(meta_ref, tile, cot_ref[...].T), (act_ref, gp_ref, xh2_ref, r2_ref, att_ref),
            gains_ref, (wdown_ref, wup_ref, wout_ref), mlp_accs, lambda i: None, gh.at[tile],
            gatt.at[tile],
        )

    @pl.when(step == N_TILE)
    def _():
        part_a, part_b = mlp_parts(*mlp_accs[:3])
        write_shards(part_a + part_b, held_mlp)
        copy.start()

    @pl.when(step >= N_TILE)
    def _():
        tile = 2 * N_TILE - 1 - step
        data = (
            xh1.at[tile], r1.at[tile], qkv.at[tile], krow.at[tile], vrow.at[tile], lse.at[tile],
            ks_ref, vs_ref,
        )
        gin_ref[...] = attn_back_part(
            meta_ref, tile, gh.at[tile], gatt.at[tile], data, gains_ref, wqkv_ref, attn_accs,
            rows_ref, lambda i: None,
        )

    @pl.when(step == 2 * N_TILE - 1)
    def _():
        gln2 = jnp.sum(mlp_accs[3][...].T, axis=0, keepdims=True)
        parts = (
            (attn_accs[0], 0, QKV_ROWS), (gain_rows(attn_accs[1], gln2), 0, GAIN_ROWS)
        )
        write_halves(meta_ref, parts, send_ref, keep_ref)
        copy.wait()


ANY = pl.BlockSpec(memory_space=pl.ANY)
sds = jax.ShapeDtypeStruct


def whole(shape):
    return pl.BlockSpec(shape, lambda t, *_: (0,) * len(shape), pipeline_mode=pl.Buffered(1))


def rows_spec(width):
    return pl.BlockSpec((TILE, width), lambda t, *_: (t, 0))


def cols_spec(height):
    return pl.BlockSpec((height, TILE), lambda t, *_: (0, t))


def rev_rows(width):
    return pl.BlockSpec((TILE, width), lambda t, *_: (N_TILE - 1 - t, 0))


def rev_cols(height):
    return pl.BlockSpec((height, TILE), lambda t, *_: (0, N_TILE - 1 - t))


def call(kernel, grid, outs, in_specs, out_specs, scratch, args, limit=VMEM_LIMIT):
    return pl.pallas_call(
        kernel,
        out_shape=tuple(outs),
        grid_spec=pltpu.PrefetchScalarGridSpec(
            num_scalar_prefetch=1, grid=grid, in_specs=in_specs, out_specs=out_specs,
            scratch_shapes=scratch,
        ),
        cost_estimate=pl.CostEstimate(flops=0, bytes_accessed=0, transcendentals=0),
        compiler_params=pltpu.CompilerParams(vmem_limit_bytes=limit),
    )(*args)


def col(height, kind=BF):
    return sds((height, MB_TOK), kind)


def attn_outputs():
    shapes = [
        col(D), col(1, F32), col(3 * D), sds((MB_TOK, D), BF), sds((MB_TOK, D), BF),
        col(HEADS, F32), col(D), col(D), col(1, F32), sds((PAD_BLK, D), BF), sds((PAD_BLK, D), BF),
    ]
    specs = [
        cols_spec(D), cols_spec(1), cols_spec(3 * D), rows_spec(D), rows_spec(D), cols_spec(HEADS),
        cols_spec(D), cols_spec(D), cols_spec(1), whole((PAD_BLK, D)), whole((PAD_BLK, D)),
    ]
    return shapes, specs


MLP_OUTS = ([sds((MB_TOK, D), BF), col(FF), col(FF)], [(D, 0), (FF, 1), (FF, 1)])


def weight_scratch(*weights):
    return [pltpu.VMEM(w.own.shape, BF) for w in weights] + [
        pltpu.SemaphoreType.DMA((len(weights),))
    ]


def flat(weights):
    return [ref for weight in weights for ref in weight.flat()]


def attn_scratch():
    return [pltpu.VMEM((D, TILE), BF)]


def forward_attn(meta, x, gains, wqkv, wout, layer):
    shapes, specs = attn_outputs()
    weights = (wqkv, wout)
    out = call(
        functools.partial(forward_attn_kernel, layer=layer, weights=weights), (N_TILE,),
        shapes + [col(D, F32), col(D)],
        [
            pl.BlockSpec((TILE, D), lambda t, m: (m[6] * N_TILE + t, 0)), whole((2, D)),
        ] + [ANY] * len(flat(weights)),
        specs + [cols_spec(D), cols_spec(D)],
        attn_scratch() + weight_scratch(*weights),
        (meta, x, gains, *flat(weights)),
    )
    return out[:11], out[11], out[12]


def forward_mlp(meta, hidden, second, wup, wdown, layer):
    weights = (wup, wdown)
    return call(
        functools.partial(forward_mlp_kernel, layer=layer, weights=weights), (N_TILE,),
        MLP_OUTS[0],
        [cols_spec(D), cols_spec(D)] + [ANY] * len(flat(weights)),
        [rows_spec(D), cols_spec(FF), cols_spec(FF)],
        weight_scratch(*weights),
        (meta, hidden, second, *flat(weights)),
    )


def mlp_scratch():
    return [
        pltpu.VMEM((FF, D), F32), pltpu.VMEM((FF, D), F32), pltpu.VMEM((D, D), F32),
        pltpu.VMEM((D, SPAN), F32),
    ]


def attn_back_scratch():
    return [
        pltpu.VMEM((3 * D, D), F32), pltpu.VMEM((D, SPAN), F32), pltpu.VMEM((D, PAD_BLK), F32),
        pltpu.VMEM((D, PAD_BLK), F32),
    ]


def mlp_back(meta, seed, act, gp, xh2, r2, att, gains, wdown, wup, wout, layer):
    weights = (wdown, wup, wout)
    half = 8 * (PART_A + PART_B)
    return call(
        functools.partial(mlp_back_kernel, layer=layer, weights=weights), (N_TILE,),
        [sds((half, D), BF), sds((half, D), BF), sds((1, D), F32), col(D, F32), col(D)],
        [
            rev_rows(D), rev_cols(FF), rev_cols(FF), rev_cols(D), rev_cols(1), rev_cols(D),
            whole((2, D)),
        ] + [ANY] * len(flat(weights)),
        [whole((half, D)), whole((half, D)), whole((1, D)), rev_cols(D), rev_cols(D)],
        mlp_scratch() + weight_scratch(*weights),
        (meta, seed, act, gp, xh2, r2, att, gains, *flat(weights)),
    )


def attn_back(meta, gh, gatt, xh1, r1, qkv, krow, vrow, lse, ks, vs, gains, gln2, wqkv, layer):
    half = 8 * PART_C
    return call(
        functools.partial(attn_back_kernel, layer=layer, weights=(wqkv,)), (N_TILE,),
        [sds((MB_TOK, D), BF), sds((half, D), BF), sds((half, D), BF)],
        [
            rev_cols(D), rev_cols(D), rev_cols(D), rev_cols(1), rev_cols(3 * D), rev_rows(D),
            rev_rows(D), rev_cols(HEADS), whole((PAD_BLK, D)), whole((PAD_BLK, D)), whole((2, D)),
            whole((1, D)),
        ] + [ANY] * len(wqkv.flat()),
        [rev_rows(D), whole((half, D)), whole((half, D))],
        attn_back_scratch() + [pltpu.VMEM((3 * D, TILE), F32)] + weight_scratch(wqkv),
        (meta, gh, gatt, xh1, r1, qkv, krow, vrow, lse, ks, vs, gains, gln2, *wqkv.flat()),
        VMEM_LIMIT * 3 // 4,
    )


def whole_layer(meta, x, cotangent, gains, wqkv, wout, wup, wdown, layer):
    weights = (wqkv, wout, wup, wdown)
    tiled = lambda *shape: pltpu.VMEM((N_TILE,) + shape, BF)
    sums, half = sds((16, PART_A + PART_B, D), BF), 8 * PART_C
    forth = lambda t: jnp.minimum(t, N_TILE - 1)
    back = lambda t, *_: (jnp.where(t < N_TILE, N_TILE - 1, 2 * N_TILE - 1 - t), 0)
    return call(
        functools.partial(layer_kernel, layer=layer, weights=weights), (2 * N_TILE,),
        [
            sds((MB_TOK, D), BF), sds((MB_TOK, D), BF), sums, sds((half, D), BF),
            sds((half, D), BF),
        ],
        [
            pl.BlockSpec((TILE, D), lambda t, *_: (forth(t), 0)),
            pl.BlockSpec((TILE, D), lambda t, m: (m[6] * N_TILE + forth(t), 0)),
            whole((2, D)),
        ] + [ANY] * len(flat(weights)),
        [
            pl.BlockSpec((TILE, D), lambda t, *_: (forth(t), 0)),
            pl.BlockSpec((TILE, D), back), ANY, whole((half, D)), whole((half, D)),
        ],
        [
            tiled(D, TILE), pltpu.VMEM((N_TILE, 1, TILE), F32), tiled(3 * D, TILE), tiled(TILE, D),
            tiled(TILE, D), pltpu.VMEM((N_TILE, HEADS, TILE), F32), pltpu.VMEM((D, TILE), BF),
            pltpu.VMEM((D, TILE), BF), pltpu.VMEM((1, TILE), F32), pltpu.VMEM((PAD_BLK, D), BF),
            pltpu.VMEM((PAD_BLK, D), BF), pltpu.VMEM((N_TILE, D, TILE), F32), tiled(D, TILE),
            pltpu.VMEM((FF, TILE), BF), pltpu.VMEM((FF, TILE), BF), pltpu.VMEM((D, TILE), BF),
            pltpu.VMEM((3 * D, TILE), F32),
        ] + mlp_scratch() + attn_back_scratch() + [
            pltpu.VMEM((16, PART_A + PART_B, D), BF),
        ] + weight_scratch(*weights) + [pltpu.SemaphoreType.DMA],
        (meta, x, cotangent, gains, *flat(weights)),
    )


def combine_kernel(meta_ref, *refs, count, cuts):
    values, outs = refs[:count], refs[count:]
    x, z = (meta_ref[7] >> 1) & 1, meta_ref[8]
    for out, (start, kind, k) in zip(outs, cuts):
        rows = out.shape[0]
        spot = {"x": x ^ k, "z": z ^ k, "all": 0}[kind]
        part = pl.ds(pl.multiple_of(start + spot * rows, 16), rows)
        total = values[0][part].astype(F32)
        for value in values[1:]:
            total = total + value[part].astype(F32)
        out[...] = total.astype(BF)


def combine(meta, values, cuts, work=0):
    return pl.pallas_call(
        functools.partial(
            combine_kernel, count=len(values), cuts=tuple((c[0],) + c[2:] for c in cuts)
        ),
        out_shape=tuple(sds((c[1], D), BF) for c in cuts),
        grid_spec=pltpu.PrefetchScalarGridSpec(
            num_scalar_prefetch=1, grid=(1,),
            in_specs=[part_spec(v.shape, (0, 0)) for v in values],
            out_specs=[part_spec((c[1], D), (0, 0)) for c in cuts],
        ),
        cost_estimate=pl.CostEstimate(flops=work, bytes_accessed=0, transcendentals=0),
        compiler_params=pltpu.CompilerParams(vmem_limit_bytes=VMEM_LIMIT // 4),
    )(meta, *values)


def by_x(start, rows):
    return [(start, rows, "x", 0), (start, rows, "x", 1)]


def by_z(start, rows):
    return [(start, rows, "z", k) for k in range(4)]


def finish_kernel(meta_ref, *refs, widths, targets, extra):
    pieces, refs = refs[:4], refs[4 + extra:]
    outs, held, sem = refs[:len(widths)], refs[-2], refs[-1]
    rows = held.shape[0] // 4
    for index, piece in enumerate(pieces):
        place = meta_ref[7] ^ index
        spot = (place & 1) * 2 + (place >> 1)
        pltpu.make_async_copy(
            piece, held.at[pl.ds(pl.multiple_of(spot * rows, rows), rows)], sem
        ).start()
    for index, piece in enumerate(pieces):
        pltpu.make_async_copy(piece, held.at[pl.ds(index * rows, rows)], sem).wait()
    total = sum(widths)
    for i, (width, flip) in enumerate(zip(widths, targets)):
        start = sum(widths[:i])
        value = jnp.concatenate(
            [held[pl.ds(s * total + start, width)] for s in range(16)], axis=0
        )
        outs[i][...] = (value.T if flip else value).astype(F32)


def finish(meta, pieces, widths, flips, shapes, specs, more=(), alias=None):
    rows = pieces[0].shape[0]
    return pl.pallas_call(
        functools.partial(finish_kernel, widths=widths, targets=flips, extra=len(more)),
        out_shape=tuple(sds(shape, F32) for shape in shapes),
        grid_spec=pltpu.PrefetchScalarGridSpec(
            num_scalar_prefetch=1, grid=(1,), in_specs=[ANY] * (4 + len(more)), out_specs=specs,
            scratch_shapes=[pltpu.VMEM((4 * rows, D), BF), pltpu.SemaphoreType.DMA],
        ),
        input_output_aliases=alias or {},
        compiler_params=pltpu.CompilerParams(vmem_limit_bytes=VMEM_LIMIT * 5 // 8),
    )(meta, *pieces, *more)


def part_spec(shape, index):
    return pl.BlockSpec(shape, lambda t, *_: index)


def swap_xor(value, mask):
    size = lax.axis_size("dp")
    return lax.ppermute(value, "dp", [(i, i ^ mask) for i in range(size)])


def swap_section(value):
    return lax.ppermute(value, "section", [(0, 1), (1, 0)])


def to_section(value, target):
    return lax.ppermute(value, "section", [(1 - target, target)])


def exchange(value0, value1):
    return swap_section(jnp.where(lax.axis_index("section") == 0, value1, value0))


def low_groups():
    size = lax.axis_size("dp")
    return None if size == 16 else [list(range(i, i + 16)) for i in range(0, size, 16)]


def added(*values):
    total = values[0].astype(F32)
    for value in values[1:]:
        total = total + value.astype(F32)
    return total.astype(BF)


def halves(value, bit):
    half = value.shape[0] // 2
    mine = (lax.axis_index("dp") >> bit) & 1
    return (
        lax.dynamic_slice_in_dim(value, mine * half, half, 0),
        lax.dynamic_slice_in_dim(value, (1 - mine) * half, half, 0),
    )


def half_sum(pair, bit):
    return added(pair[0], swap_xor(pair[1], 1 << bit))


def quarters(value, bit):
    rows = value.shape[0] // 4
    mine = (lax.axis_index("dp") >> bit) & 3
    return tuple(lax.dynamic_slice_in_dim(value, (mine ^ k) * rows, rows, 0) for k in range(4))


def swap_quarters(parts, bit):
    return [swap_xor(parts[k], k << bit) for k in (1, 2, 3)]


def quarter_sum(parts, bit):
    return added(parts[0], *swap_quarters(parts, bit))


def tie(*values):
    return lax.optimization_barrier(values)


def rest_bits():
    return range(4, lax.axis_size("dp").bit_length() - 1)


def reduce_core(halves):
    return added(halves[1], swap_xor(halves[0], 1))


def reduce_rest(value):
    for bit in rest_bits():
        value = half_sum(halves(value, bit), bit)
    return value


def gather_bit(value, bit):
    mine = (lax.axis_index("dp") >> bit) & 1
    other = swap_xor(value, 1 << bit)
    return jnp.where(
        mine == 0,
        jnp.concatenate([value, other], axis=0),
        jnp.concatenate([other, value], axis=0),
    )


def gather_quad(value, bit):
    mine = (lax.axis_index("dp") >> bit) & 3
    got = [value] + [swap_xor(value, k << bit) for k in (1, 2, 3)]
    parts = []
    for p in range(4):
        which = mine ^ p
        part = got[3]
        for k in (2, 1, 0):
            part = jnp.where(which == k, got[k], part)
        parts.append(part)
    return jnp.concatenate(parts, axis=0)


def gather_rest(value):
    for bit in reversed(rest_bits()):
        value = gather_bit(value, bit)
    return value


def spread_pieces(value):
    across = swap_xor(value, 2)
    return value, swap_xor(value, 1), across, swap_xor(across, 1)


def sum_rest(value):
    for bit in rest_bits():
        value = added(value, swap_xor(value, 1 << bit))
    return value


def per_device(
    tokens, cotangent, span_counts, tail_lens, ln1_gain, w_qkv, w_out, ln2_gain, w_up, w_down
):
    section = lax.axis_index("section")
    first = section == 0
    place = lax.axis_index("dp") & 3
    meta = jnp.concatenate([
        lax.dynamic_index_in_dim(span_counts, section, 0, keepdims=False),
        lax.dynamic_index_in_dim(tail_lens, section, 0, keepdims=False),
        section.astype(jnp.int32)[None], place.astype(jnp.int32)[None],
        ((lax.axis_index("dp") >> 2) & 3).astype(jnp.int32)[None],
    ])
    own = (w_qkv[0], w_out[0], w_up[0], w_down[0])

    def part(weight, spot, count):
        rows = weight.shape[0] // count
        return lax.dynamic_slice_in_dim(weight, spot * rows, rows, 0)

    own_gains = jnp.concatenate([ln1_gain, ln2_gain], axis=0)
    attn = swap_section(
        jnp.concatenate([part(own[0], place, 4), part(own[1], place, 4)], axis=1)
    )
    other_gains = swap_section(own_gains)
    attn, other_gains = tie(attn, other_gains)
    gains = [jnp.where(first, own_gains, other_gains), jnp.where(first, other_gains, own_gains)]
    attn_x = swap_xor(attn, 2)
    attn = (attn, swap_xor(attn, 1), attn_x, swap_xor(attn_x, 1))
    wqkv, wout = Weight(own[0], (attn, 0, 0, None)), Weight(own[1], (attn, 3 * D, 0, None))
    up = swap_section(part(own[2], place, 4))
    down = swap_section(part(own[3], place & 1, 2))
    up_x, up_c = swap_xor(up, 2), swap_xor(up, 1)

    keep0, hidden, second = forward_attn(meta, tokens, gains[0], wqkv, wout, 0)
    keep0, hidden, second, up_x, up_c, down = tie(keep0, hidden, second, up_x, up_c, down)
    wup = Weight(own[2], ((up, up_c, up_x, swap_xor(up_x, 1)), 0, 0, None))
    wdown = Weight(own[3], ((down, swap_xor(down, 1)), 0, 0, None))
    act_out0, act0, gp0 = forward_mlp(meta, hidden, second, wup, wdown, 0)
    act_out1, ig1, sums1, send1, kept1 = whole_layer(
        meta, act_out0, cotangent, gains[1], wqkv, wout, wup, wdown, 1
    )
    cut = 2 * MB_TOK // 3
    acts_a = exchange(act_out0[:cut], act_out1[:cut])
    sums1 = lax.psum_scatter(
        sums1.reshape(-1, D), "dp", scatter_dimension=0, axis_index_groups=low_groups(), tiled=True
    )
    xh1, r1, qkv, krow, vrow, lse, att, xh2, r2, ks, vs = keep0
    back = mlp_back(meta, ig1, act0, gp0, xh2, r2, att, gains[0], wdown, wup, wout, 0)
    c1 = swap_xor(send1, 1)
    (send, kept, gln2, gh, gatt), acts_a, act_out0, act_out1, c1 = tie(
        back, acts_a, act_out0, act_out1, c1
    )
    mlp0 = combine(
        meta, (kept, swap_xor(send, 1)), by_x(0, 4 * PART_A) + by_z(8 * PART_A, 2 * PART_B)
    )
    a0, b0 = mlp0[:2], mlp0[2:]
    gh, a0, b0 = tie(gh, a0, b0)
    acts_b = exchange(act_out0[cut:], act_out1[cut:])
    a0_x, b0_z = swap_xor(a0[1], 2), swap_quarters(b0, 2)
    back = attn_back(
        meta, gh, gatt, xh1, r1, qkv, krow, vrow, lse, ks, vs, gains[0], gln2, wqkv, 0
    )
    (ig0, send, kept), a0_x, b0_z, acts_b = tie(back, a0_x, b0_z, acts_b)
    acts_in = jnp.concatenate([acts_a, acts_b], axis=0)
    c0 = swap_xor(send, 1)
    a0 = [added(*pair) for pair in zip(quarters(a0[0], 2), quarters(a0_x, 2))]
    a0, c0 = tie(a0, c0)
    a0_z = swap_quarters(a0, 2)
    c0 = combine(meta, (kept, c0), by_x(0, 4 * PART_C), OVERLAPPED)
    c1 = combine(meta, (kept1, c1), by_x(0, 4 * PART_C))
    b0 = halves(added(b0[0], *b0_z), 1)
    bc_x = swap_xor(jnp.concatenate([b0[1], c0[1], c1[1]], axis=0), 2)

    def own_sum(grad0, grad1):
        return added(jnp.where(first, grad0, grad1), swap_section(jnp.where(first, grad1, grad0)))

    bc_x, sums1 = tie(bc_x, sums1)
    cut = PART_B + 4 * PART_C
    b0 = added(b0[0], bc_x[:PART_B])
    c0 = quarters(added(c0[0], bc_x[PART_B:cut]), 2)
    c1 = quarters(added(c1[0], bc_x[cut:]), 2)
    c = [jnp.concatenate(pair, axis=0) for pair in zip(c0, c1)]
    c_z = swap_quarters(c, 2)
    a0_z, b0, c_1 = tie(a0_z, b0, c[1])
    (a0,) = combine(meta, (a0[0], *a0_z), [(0, PART_A, "all", 0)], OVERLAPPED)
    a1, b1 = sums1[:PART_A], sums1[PART_A:]
    ab0 = jnp.concatenate([reduce_rest(a0), reduce_rest(b0)], axis=0)
    ab1 = jnp.concatenate([reduce_rest(a1), reduce_rest(b1)], axis=0)
    ab = jnp.where(first, ab0, ab1), swap_section(jnp.where(first, ab1, ab0))
    if rest_bits():
        ab = added(*ab)
        a_rows = ab.shape[0] * PART_A // (PART_A + PART_B)
        a_own, b_own = ab[:a_rows], ab[a_rows:]
    else:
        a_own, b_own = combine(
            meta, ab, [(0, PART_A, "all", 0), (PART_A, PART_B, "all", 0)], OVERLAPPED
        )
    a_own, b_own, near = tie(a_own, b_own, c_z[0])
    c_z = [near] + c_z[1:]
    a_full = gather_quad(gather_rest(a_own), 2)
    c = added(c[0], *c_z)
    c_own = own_sum(*[
        jnp.concatenate([reduce_rest(v[:QKV_ROWS]), sum_rest(v[QKV_ROWS:])], axis=0)
        for v in (c[:PART_C], c[PART_C:])
    ])
    c_own, ig0 = tie(c_own, ig0)
    grads_in = exchange(ig0, ig1)
    lns = c_own[-GAIN_ROWS:][:2].astype(F32)
    bc_own = jnp.concatenate([gather_rest(b_own), gather_rest(c_own[:-GAIN_ROWS])], axis=0)
    def assemble(value0, value1, got):
        return jnp.concatenate(
            [jnp.where(first, value0, got), jnp.where(first, got, value1)], axis=0
        )

    activations = assemble(act_out0, act_out1, acts_in)
    input_grads = assemble(ig0, ig1, grads_in)
    a_full, bc_own = tie(a_full, bc_own)
    a_pieces = spread_pieces(a_full)
    bc_full = gather_quad(bc_own, 2)
    grads_a = finish(
        meta, a_pieces, (DOWN_ROWS, UP_A // 16, OUT_ROWS), (False, True, False),
        [(FF, D), (D, FF), (D, D)],
        [
            part_spec((FF, D), (0, 0)), part_spec((D, UP_A), (0, UP_B // UP_A)),
            part_spec((D, D), (0, 0)),
        ],
    )
    across, activations, input_grads, grads_a = tie(
        swap_xor(bc_full, 2), activations, input_grads, grads_a
    )
    grad_down, grad_up, grad_out = grads_a
    bc_pieces = (bc_full, swap_xor(bc_full, 1), across, swap_xor(across, 1))
    grad_up, grad_qkv = finish(
        meta, bc_pieces, (UP_B // 16, QKV_ROWS), (True, True), [(D, FF), (D, 3 * D)],
        [part_spec((D, UP_B), (0, 0)), part_spec((D, 3 * D), (0, 0))],
        (grad_up,), {5: 0},
    )

    return (
        activations[None],
        input_grads[None],
        lns[:1],
        grad_qkv[None],
        grad_out[None],
        lns[1:],
        grad_up[None],
        grad_down[None],
    )


def solution(mesh):
    return jax.shard_map(
        per_device,
        mesh=mesh,
        in_specs=(
            P("dp", None),
            P("dp", None),
            P("dp", None),
            P("dp", None),
            P("section", None),
            P("section", None, None),
            P("section", None, None),
            P("section", None),
            P("section", None, None),
            P("section", None, None),
        ),
        out_specs=(
            P("section", "dp", None),
            P("section", "dp", None),
            P("section", None),
            P("section", None, None),
            P("section", None, None),
            P("section", None),
            P("section", None, None),
            P("section", None, None),
        ),
        check_vma=False,
    )
```
